128 devices in a mesh: pts: 32 (over z, y, core), grp: 4 (over x).
Axes of the slice: x: 4, y: 4, z: 4, core: 2. Of those that a mesh axis runs over, the one named last changes fastest.
Arguments:
- nodes: bfloat16 [2, 131072, 256], P(None, ('pts', 'grp')), may hold values from -6 to 6
- cotangent: bfloat16 [2, 131072, 256], P(None, ('pts', 'grp')), may hold values from -6 to 6
- first_inward: bfloat16 [256, 768], replicated, may hold values from -0.375 to 0.375
- first_outward: bfloat16 [256, 256], replicated, may hold values from -0.375 to 0.375
- second_inward: bfloat16 [256, 768], replicated, may hold values from -0.375 to 0.375
- second_outward: bfloat16 [256, 256], replicated, may hold values from -0.375 to 0.375
- rotated_source: int32 [2, 131072], P(None, ('pts', 'grp')), may hold values from 0 to 131071, as said below
- rotated_index: int32 [2, 131072], P(None, ('pts', 'grp')), may hold values from 0 to 131071, as said below
Outputs:
- input_grad: bfloat16 [2, 131072, 256], P(None, ('pts', 'grp'))
- first_inward_grad: float32 [256, 768], replicated
- first_outward_grad: float32 [256, 256], replicated
- second_inward_grad: float32 [256, 768], replicated
- second_outward_grad: float32 [256, 256], replicated
The draws below stay inside these ranges and needn't reach their ends.
Inputs may be any that keep to these rules, and one draw needn't show every extreme that they name: For each sample, rotated_source and rotated_index are inverse permutations of the 131072 node indices. Split the indices into 128 aligned runs of 1024, one a device in the order of pts+grp. A node of run s has its rotated position in run t only where t - s, taken modulo 128, lies within -8 to 8. For every pair of different runs, at most 32 nodes of the first have their rotated position in the second, and exactly 32 for some pair. `rotated_index`: the inverse of rotated_source, sample by sample.
All inputs are finite; a program needn't handle non-finite values.
Results may differ from the reference program's by a relative error of at most 0.014.
Values may be sent and summed in bfloat16 or wider, within the bound.
No kernel may reach another device: no remote copies, remote signals or barrier semaphores. Data moves between devices by JAX's collectives and lax.ppermute only.
A program may use at most 128 MiB of HBM per device.

```python
import math
import jax
import jax.numpy as jnp
from jax import lax

D = 256
HEADS = 8
BALL = 256
SPAN = 8
CAP = 32
SAMPLES = 2
NODE_DEV = 1024
SHARDS = 128
NODES = 131072


def pair_counts(count_key):
    drawn = jax.random.randint(count_key, (SHARDS, SPAN), 1, CAP + 1)
    drawn = drawn.at[0, 0].set(CAP)
    sender = jnp.arange(SHARDS)[:, None]
    target = jnp.arange(SHARDS)[None, :]
    offset = (target - sender) % SHARDS
    backward_offset = SHARDS - offset
    ahead = drawn[sender, jnp.clip(offset - 1, 0, SPAN - 1)]
    behind = drawn[target, jnp.clip(backward_offset - 1, 0, SPAN - 1)]
    is_ahead = (offset >= 1) & (offset <= SPAN)
    is_behind = (backward_offset >= 1) & (backward_offset <= SPAN) & (offset != 0)
    counts = jnp.where(is_ahead, ahead, jnp.where(is_behind, behind, 0))
    counts = counts + jnp.diag(NODE_DEV - jnp.sum(counts, axis=1))
    return counts.astype(jnp.int32)


def permute_rows(row_key):
    return jax.random.permutation(row_key, NODE_DEV).astype(jnp.int32)


def one_sample(sample_key):
    count_key, send_key, land_key = jax.random.split(sample_key, 3)
    counts = pair_counts(count_key)
    inclusive = jnp.cumsum(counts, axis=1)
    send_start = inclusive - counts
    land_start = jnp.cumsum(counts, axis=0) - counts
    positions = jnp.arange(NODE_DEV, dtype=jnp.int32)
    target = jnp.sum((inclusive[:, None, :] <= positions[None, :, None]).astype(jnp.int32), axis=2)
    sender = jnp.arange(SHARDS, dtype=jnp.int32)[:, None]
    offset_rank = positions[None, :] - send_start[sender, target]
    landing = land_start[sender, target] + offset_rank
    send_order = jax.vmap(permute_rows)(jax.random.split(send_key, SHARDS))
    land_order = jax.vmap(permute_rows)(jax.random.split(land_key, SHARDS))
    node_ids = sender * NODE_DEV + send_order
    places = target * NODE_DEV + land_order[target, landing]
    index_table = jnp.zeros((NODES,), jnp.int32).at[node_ids.reshape(-1)].set(places.reshape(-1))
    source_table = jnp.zeros((NODES,), jnp.int32).at[places.reshape(-1)].set(node_ids.reshape(-1))
    return (source_table, index_table)


def rotation_tables(key):
    return jax.vmap(one_sample)(jax.random.split(key, SAMPLES))


def draw_rotated_source(key, part):
    source_table, index_table = rotation_tables(key)
    return source_table


def draw_rotated_index(key, part):
    source_table, index_table = rotation_tables(key)
    return index_table


def levels(rng, extent, cuts, low, top_value):
    gain, own = 1.0, jax.random.fold_in(rng, 6)
    for dim, shards_of in cuts:
        heights = jnp.exp(jax.random.uniform(jax.random.fold_in(own, dim), (shards_of,), jnp.float32, low / len(cuts), top_value / len(cuts)))
        gain = gain * jnp.repeat(heights, extent[dim] // shards_of).reshape([-1 if axis == dim else 1 for axis in range(len(extent))])
    return gain


def gaussian(own_key, dims, width, bound, cuts=(), kind=jnp.bfloat16):
    array = width * jax.random.normal(own_key, dims, jnp.float32)
    if cuts:
        array = array * levels(own_key, dims, cuts, -0.22, 0.18)
    return jnp.clip(array, -bound, bound).astype(kind)


def setup_inputs(seed: int = 0) -> dict:
    seeds = jax.random.split(jax.random.key(seed), 9)
    nodes = gaussian(seeds[0], (SAMPLES, NODES, D), 1.0, 6.0, ((1, 128),))
    cotangent = gaussian(seeds[1], (SAMPLES, NODES, D), 1.0, 6.0, ((1, 128),))
    first_inward = gaussian(seeds[2], (D, 3 * D), D ** -0.5, 0.375)
    first_outward = gaussian(seeds[3], (D, D), D ** -0.5, 0.375)
    second_inward = gaussian(seeds[4], (D, 3 * D), D ** -0.5, 0.375)
    second_outward = gaussian(seeds[5], (D, D), D ** -0.5, 0.375)
    rotated_source = draw_rotated_source(jax.random.fold_in(seeds[8], 71), 0)
    rotated_index = draw_rotated_index(jax.random.fold_in(seeds[8], 71), 0)
    return {"nodes": nodes, "cotangent": cotangent, "first_inward": first_inward, "first_outward": first_outward, "second_inward": second_inward, "second_outward": second_outward, "rotated_source": rotated_source, "rotated_index": rotated_index}


EPSILON = 1e-06

def batched(pattern, left_side, right_side):
    return jnp.einsum(pattern, left_side.astype(jnp.float32), right_side.astype(jnp.float32), precision=lax.Precision.HIGHEST)

def split_heads(matrix):
    return matrix.reshape(matrix.shape[0] // (2 * BALL), 2, BALL, HEADS, matrix.shape[1] // HEADS)

def join_heads(grouped):
    return grouped.reshape(-1, grouped.shape[3] * grouped.shape[4])

def attend_forward(pieces):
    queries, key_rows, values = pieces
    scores = batched('bqhd,bkhd->bhqk', queries, key_rows)
    weights = jnp.exp(scores)
    totals = lax.optimization_barrier(jnp.sum(weights, axis=-1, keepdims=True))
    prob_low = (weights / totals).astype(jnp.bfloat16)
    result = batched('bhqk,bkhd->bqhd', prob_low, values)
    return (result.astype(jnp.bfloat16), totals)

def attend_backward(pieces):
    queries, key_rows, values, totals, grad_out = pieces
    scores = batched('bqhd,bkhd->bhqk', queries, key_rows)
    prob_full = jnp.exp(scores) / totals
    prob_low = prob_full.astype(jnp.bfloat16)
    grad_values = batched('bhqk,bqhd->bkhd', prob_low, grad_out)
    grad_probs = batched('bqhd,bkhd->bhqk', grad_out, values)
    column_sum = lax.optimization_barrier(jnp.sum(grad_probs * prob_full, axis=-1, keepdims=True))
    grad_scores = (prob_full * (grad_probs - column_sum)).astype(jnp.bfloat16)
    grad_queries = batched('bhqk,bkhd->bqhd', grad_scores, key_rows)
    grad_keys = batched('bhqk,bqhd->bkhd', grad_scores, queries)
    return (grad_queries, grad_keys, grad_values)

def block_forward(row_block, inward, outward):
    feature_width = row_block.shape[1]
    widened = row_block.astype(jnp.float32)
    row_scale = lax.rsqrt(lax.optimization_barrier(jnp.mean(widened * widened, axis=-1, keepdims=True)) + EPSILON)
    normed = (widened * row_scale).astype(jnp.bfloat16)
    mixture = jnp.dot(normed, inward, preferred_element_type=jnp.float32)
    query_raw = mixture[:, :feature_width]
    key_raw = mixture[:, feature_width:2 * feature_width]
    value_raw = mixture[:, 2 * feature_width:]
    query_scale = lax.rsqrt(lax.optimization_barrier(jnp.mean(query_raw * query_raw, axis=-1, keepdims=True)) + EPSILON)
    query_unit = query_raw * query_scale
    key_scale = lax.rsqrt(lax.optimization_barrier(jnp.mean(key_raw * key_raw, axis=-1, keepdims=True)) + EPSILON)
    key_unit = key_raw * key_scale
    head_factor = (feature_width // HEADS) ** (-0.5)
    queries = (query_unit * head_factor).astype(jnp.bfloat16)
    key_rows = key_unit.astype(jnp.bfloat16)
    values = value_raw.astype(jnp.bfloat16)
    attended, totals = lax.map(attend_forward, (split_heads(queries), split_heads(key_rows), split_heads(values)))
    attended = join_heads(attended)
    return (widened, row_scale, normed, query_unit, query_scale, key_unit, key_scale, queries, key_rows, values, totals, attended)

def block_output(stashed, outward):
    widened = stashed[0]
    attended = stashed[11]
    return (widened + jnp.dot(attended, outward, preferred_element_type=jnp.float32)).astype(jnp.bfloat16)

def block_backward(stashed, inward, outward, grad_rows):
    widened, row_scale, normed, query_unit, query_scale, key_unit, key_scale, queries, key_rows, values, totals, attended = stashed
    feature_width = widened.shape[1]
    grad_outward = jnp.dot(attended.T, grad_rows, preferred_element_type=jnp.float32)
    grad_attended = jnp.dot(grad_rows, outward.T, preferred_element_type=jnp.float32).astype(jnp.bfloat16)
    grad_queries, grad_keys, grad_values = lax.map(attend_backward, (split_heads(queries), split_heads(key_rows), split_heads(values), totals, split_heads(grad_attended)))
    grad_queries = join_heads(grad_queries) * (feature_width // HEADS) ** (-0.5)
    grad_keys = join_heads(grad_keys)
    grad_values = join_heads(grad_values)
    grad_qraw = query_scale * (grad_queries - query_unit * lax.optimization_barrier(jnp.mean(grad_queries * query_unit, axis=-1, keepdims=True)))
    grad_kraw = key_scale * (grad_keys - key_unit * lax.optimization_barrier(jnp.mean(grad_keys * key_unit, axis=-1, keepdims=True)))
    grad_mixture = jnp.concatenate([grad_qraw, grad_kraw, grad_values], axis=1).astype(jnp.bfloat16)
    grad_inward = jnp.dot(normed.T, grad_mixture, preferred_element_type=jnp.float32)
    grad_normed = jnp.dot(grad_mixture, inward.T, preferred_element_type=jnp.float32)
    unit_rows = widened * row_scale
    grad_input = grad_rows.astype(jnp.float32) + row_scale * (grad_normed - unit_rows * lax.optimization_barrier(jnp.mean(grad_normed * unit_rows, axis=-1, keepdims=True)))
    return (grad_input.astype(jnp.bfloat16), grad_inward, grad_outward)

def make_step(inward, outward):

    def scan_step(running, pieces):
        row_block, grad_block = pieces
        stashed = block_forward(row_block, inward, outward)
        grad_input, grad_inward, grad_outward = block_backward(stashed, inward, outward, grad_block)
        return ((running[0] + grad_inward, running[1] + grad_outward), grad_input)
    return scan_step

def reference(nodes, cotangent, first_inward, first_outward, second_inward, second_outward, rotated_source, rotated_index):
    samples_count, node_count, feature_width = nodes.shape
    span_rows = 4 * BALL
    node_blocks = nodes.reshape(-1, span_rows, feature_width)

    def forward_first(row_block):
        return block_output(block_forward(row_block, first_inward, first_outward), first_outward)
    after_first = lax.map(forward_first, node_blocks).reshape(samples_count, node_count, feature_width)
    rotated = jnp.take_along_axis(after_first, rotated_source[:, :, None], axis=1)
    rotated_cot = jnp.take_along_axis(cotangent, rotated_source[:, :, None], axis=1)
    starting = (jnp.zeros((feature_width, 3 * feature_width), jnp.float32), jnp.zeros((feature_width, feature_width), jnp.float32))
    second_sums, rotated_grad = lax.scan(make_step(second_inward, second_outward), starting, (rotated.reshape(-1, span_rows, feature_width), rotated_cot.reshape(-1, span_rows, feature_width)))
    rotated_grad = rotated_grad.reshape(samples_count, node_count, feature_width)
    grad_after = jnp.take_along_axis(rotated_grad, rotated_index[:, :, None], axis=1)
    first_sums, input_grad = lax.scan(make_step(first_inward, first_outward), starting, (node_blocks, grad_after.reshape(-1, span_rows, feature_width)))
    factor = 1.0 / math.sqrt(samples_count * node_count)
    return (input_grad.reshape(nodes.shape), first_sums[0] * factor, first_sums[1] * factor, second_sums[0] * factor, second_sums[1] * factor)
```

```python
import functools
import math

import jax
import jax.numpy as jnp
from jax import lax
from jax.experimental import pallas as pl
from jax.experimental.pallas import tpu as pltpu
from jax.sharding import PartitionSpec as P

HEADS = 8
BALL = 256
SPAN = 8
CAP = 32
EPSILON = 1e-06
AXES = ("pts", "grp")
OFFSETS = tuple(d for d in range(-SPAN, SPAN + 1) if d != 0)
CLASSES = len(OFFSETS)
SLOTS = CLASSES * CAP
VMEM_LIMIT = 56 * 1024 * 1024

f32 = jnp.float32
bf16 = jnp.bfloat16


def dot(left, right, left_dim=1, right_dim=0):
    return lax.dot_general(
        left, right, (((left_dim,), (right_dim,)), ((), ())), preferred_element_type=f32
    )


def spread_column(row):
    return jnp.transpose(jnp.broadcast_to(row.astype(f32), (128, row.shape[1])))


def one_hot_rows(slot_row, slots):
    ids = lax.broadcasted_iota(jnp.int32, (slots, slot_row.shape[1]), 0)
    return jnp.where(ids == slot_row, 1.0, 0.0).astype(bf16)


def one_hot_picks(pick_column, width):
    lanes = lax.broadcasted_iota(jnp.int32, pick_column.shape, 1).astype(f32)
    pieces = [
        jnp.where(pick_column == lanes + float(128 * piece), 1.0, 0.0).astype(bf16)
        for piece in range(width // 128)
    ]
    return jnp.concatenate(pieces, axis=1)


def place_kernel(own_ref, index_ref, source_ref, cot_ref, meta_ref, *packet_refs, shards):
    samples, rows = index_ref.shape
    own = own_ref[0]
    row_ids = lax.broadcasted_iota(jnp.int32, (rows, 128), 0).astype(f32)
    lane_ids = lax.broadcasted_iota(jnp.int32, (rows, 128), 1).astype(f32)
    shift = rows.bit_length() - 1

    def class_of(ids):
        place = ((ids >> shift) - own + (SPAN + shards)) & (shards - 1)
        return place, jnp.where(place > SPAN, place - 1, place)

    for sample in range(samples):
        index = index_ref[sample : sample + 1, :]
        source = source_ref[sample : sample + 1, :]
        send_place, send_class = class_of(index)
        from_place, from_class = class_of(source)
        place_col = spread_column(send_place)
        source_col = spread_column(source)
        source_f = source.astype(f32)
        floor_f = ((source >> shift) << shift).astype(f32)
        send_rank = []
        receive_rank = []
        for piece in range(rows // 128):
            lanes = slice(128 * piece, 128 * piece + 128)
            here = send_place[:, lanes].astype(f32)
            same = (place_col == here) & (row_ids < lane_ids + float(128 * piece))
            send_rank.append(jnp.sum(jnp.where(same, 1.0, 0.0), axis=0, keepdims=True))
            same = (source_col >= floor_f[:, lanes]) & (source_col < source_f[:, lanes])
            receive_rank.append(jnp.sum(jnp.where(same, 1.0, 0.0), axis=0, keepdims=True))
        send_rank = jnp.concatenate(send_rank, axis=1).astype(jnp.int32)
        receive_rank = jnp.concatenate(receive_rank, axis=1).astype(jnp.int32)
        stays = send_place == SPAN
        home = from_place == SPAN
        send_slot = jnp.where(stays, -1, send_class * CAP + send_rank)
        receive_slot = jnp.where(home, -1, from_class * CAP + receive_rank)
        own_start = own * rows
        meta_ref[sample : sample + 1, :] = send_slot
        meta_ref[2 + sample : 3 + sample, :] = receive_slot
        meta_ref[4 + sample : 5 + sample, :] = jnp.where(
            home, source - own_start, rows + receive_slot
        )
        meta_ref[6 + sample : 7 + sample, :] = jnp.where(
            stays, index - own_start, rows + send_slot
        )
        packed = dot(one_hot_rows(send_slot, SLOTS), cot_ref[sample]).astype(bf16)
        for place in range(CLASSES):
            packet_refs[place][sample] = packed[CAP * place : CAP * place + CAP, :]


def head_masks(shape, axis=1):
    heads = lax.broadcasted_iota(jnp.int32, shape, axis) // (shape[axis] // HEADS)
    return [heads == head for head in range(HEADS)]


def project(rows, inward):
    width = rows.shape[1]
    widened = rows.astype(f32)
    row_scale = lax.rsqrt(jnp.mean(widened * widened, axis=-1, keepdims=True) + EPSILON)
    normed = (widened * row_scale).astype(bf16)
    mixture = dot(normed, inward)
    query_raw = mixture[:, :width]
    key_raw = mixture[:, width : 2 * width]
    value_raw = mixture[:, 2 * width :]
    query_scale = lax.rsqrt(jnp.mean(query_raw * query_raw, axis=-1, keepdims=True) + EPSILON)
    key_scale = lax.rsqrt(jnp.mean(key_raw * key_raw, axis=-1, keepdims=True) + EPSILON)
    return (
        widened,
        row_scale,
        normed,
        query_raw * query_scale,
        query_scale,
        key_raw * key_scale,
        key_scale,
        value_raw,
    )


def masked(array, mask):
    return jnp.where(mask, array, jnp.zeros_like(array))


def forward_kernel(
    nodes_ref, inward_ref, outward_ref, meta_ref, after_ref, attended_ref, *packet_refs
):
    sample, ball = pl.program_id(0), pl.program_id(1)
    width = nodes_ref.shape[2]
    depth = width // HEADS
    widened, _, _, query_unit, _, key_unit, _, value_raw = project(nodes_ref[0], inward_ref[...])
    queries = (query_unit * depth ** (-0.5)).astype(bf16)
    key_rows = key_unit.astype(bf16)
    values_t = jnp.transpose(value_raw).astype(bf16)
    masks = head_masks(key_rows.shape)
    parts = []
    for head in range(HEADS):
        scores = dot(masked(key_rows, masks[head]), queries, 1, 1)
        weights = jnp.exp(scores)
        inverse = 1.0 / jnp.sum(weights, axis=0, keepdims=True)
        prob_low = (weights * inverse).astype(bf16)
        parts.append(dot(values_t[head * depth : (head + 1) * depth, :], prob_low))
    attended_t = jnp.concatenate(parts, axis=0)
    attended_ref[0] = attended_t.astype(bf16)
    attended = jnp.transpose(attended_t).astype(bf16)
    result = (widened + dot(attended, outward_ref[...])).astype(bf16)
    after_ref[0, pl.ds(pl.multiple_of(ball * BALL, BALL), BALL), :] = result

    @pl.when(ball == pl.num_programs(1) - 1)
    def _():
        hits = one_hot_rows(meta_ref[pl.ds(sample, 1), :], SLOTS)
        packed = dot(hits, after_ref[0]).astype(bf16)
        for place in range(CLASSES):
            packet_refs[place][0] = packed[CAP * place : CAP * place + CAP, :]


def attention_backward(
    parts, grad_rows, inward, outward, attended_t, prob_cat, score_cat, grad_stack, query_stack
):
    widened, row_scale, normed, query_unit, query_scale, key_unit, key_scale, value_raw = parts
    width = widened.shape[1]
    depth = width // HEADS
    factor = depth ** (-0.5)
    queries = (query_unit * factor).astype(bf16)
    key_rows = key_unit.astype(bf16)
    values = value_raw.astype(bf16)
    keys_t = jnp.transpose(key_unit).astype(bf16)
    grad_attended = dot(grad_rows, outward, 1, 1).astype(bf16)
    masks = head_masks(key_rows.shape)
    with_forward = attended_t is None
    if with_forward:
        values_t = jnp.transpose(value_raw).astype(bf16)
    outputs = []
    query_parts = []
    for head in range(HEADS):
        block = slice(head * BALL, (head + 1) * BALL)
        band = slice(head * depth, (head + 1) * depth)
        grad_stack[block, :] = masked(grad_attended, masks[head])
        query_stack[block, :] = masked(queries, masks[head])
        scores = dot(masked(key_rows, masks[head]), queries, 1, 1)
        weights = jnp.exp(scores)
        inverse = 1.0 / jnp.sum(weights, axis=0, keepdims=True)
        prob_full = weights * inverse
        prob_low = prob_full.astype(bf16)
        prob_cat[:, block] = prob_low
        if with_forward:
            outputs.append(dot(values_t[band, :], prob_low))
        grad_probs = dot(masked(values, masks[head]), grad_attended, 1, 1)
        column_sum = jnp.sum(grad_probs * prob_full, axis=0, keepdims=True)
        grad_scores = (prob_full * (grad_probs - column_sum)).astype(bf16)
        score_cat[:, block] = grad_scores
        query_parts.append(dot(keys_t[band, :], grad_scores))
    if with_forward:
        attended_t = jnp.concatenate(outputs, axis=0).astype(bf16)
    grad_outward = dot(attended_t, grad_rows)
    grad_queries = jnp.transpose(jnp.concatenate(query_parts, axis=0)) * factor
    grad_values = dot(prob_cat[...], grad_stack[...])
    grad_keys = dot(score_cat[...], query_stack[...])
    grad_qraw = query_scale * (
        grad_queries - query_unit * jnp.mean(grad_queries * query_unit, axis=-1, keepdims=True)
    )
    grad_kraw = key_scale * (
        grad_keys - key_unit * jnp.mean(grad_keys * key_unit, axis=-1, keepdims=True)
    )
    grad_mixture = jnp.concatenate([grad_qraw, grad_kraw, grad_values], axis=1).astype(bf16)
    grad_inward = dot(normed, grad_mixture, 0, 0)
    grad_normed = dot(grad_mixture, inward, 1, 1)
    unit_rows = widened * row_scale
    grad_input = grad_rows.astype(f32) + row_scale * (
        grad_normed - unit_rows * jnp.mean(grad_normed * unit_rows, axis=-1, keepdims=True)
    )
    return grad_input.astype(bf16), grad_inward, grad_outward


def add_up(first, total_ref, term):
    @pl.when(first)
    def _():
        total_ref[...] = term

    @pl.when(jnp.logical_not(first))
    def _():
        total_ref[...] += term


def second_kernel(*refs):
    meta_ref, after_ref, cot_ref, inward_ref, outward_ref = refs[:5]
    arrived_refs = refs[5 : 5 + CLASSES]
    cot_refs = refs[5 + CLASSES : 5 + 2 * CLASSES]
    outs = refs[5 + 2 * CLASSES :]
    grad_ref, inward_grad_ref, outward_grad_ref = outs[:3]
    packet_refs = outs[3 : 3 + CLASSES]
    (picks, landed, landed_cot, prob_cat, score_cat, grad_stack, query_stack) = outs[3 + CLASSES :]
    sample, ball = pl.program_id(0), pl.program_id(1)
    rows = after_ref.shape[1]

    @pl.when(ball == 0)
    def _():
        picks[...] = spread_column(meta_ref[pl.ds(4 + sample, 1), :])
        for place in range(CLASSES):
            landed[CAP * place : CAP * place + CAP, :] = arrived_refs[place][0]
            landed_cot[CAP * place : CAP * place + CAP, :] = cot_refs[place][0]

    here = pl.ds(pl.multiple_of(ball * BALL, BALL), BALL)
    hits = one_hot_picks(picks[here, :], rows + SLOTS)
    rotated = (dot(hits[:, :rows], after_ref[0]) + dot(hits[:, rows:], landed[...])).astype(bf16)
    rotated_cot = (
        dot(hits[:, :rows], cot_ref[0]) + dot(hits[:, rows:], landed_cot[...])
    ).astype(bf16)
    grad_input, grad_inward, grad_outward = attention_backward(
        project(rotated, inward_ref[...]),
        rotated_cot,
        inward_ref[...],
        outward_ref[...],
        None,
        prob_cat,
        score_cat,
        grad_stack,
        query_stack,
    )
    grad_ref[0, here, :] = grad_input
    first = (sample == 0) & (ball == 0)
    add_up(first, inward_grad_ref, grad_inward)
    add_up(first, outward_grad_ref, grad_outward)

    @pl.when(ball == pl.num_programs(1) - 1)
    def _():
        hits = one_hot_rows(meta_ref[pl.ds(2 + sample, 1), :], SLOTS)
        packed = dot(hits, grad_ref[0]).astype(bf16)
        for place in range(CLASSES):
            packet_refs[place][0] = packed[CAP * place : CAP * place + CAP, :]


def first_kernel(*refs):
    meta_ref, nodes_ref, rotated_ref, attended_ref, inward_ref, outward_ref = refs[:6]
    returned_refs = refs[6 : 6 + CLASSES]
    outs = refs[6 + CLASSES :]
    grad_ref, inward_grad_ref, outward_grad_ref = outs[:3]
    (picks, landed, prob_cat, score_cat, grad_stack, query_stack) = outs[3:]
    sample, ball = pl.program_id(0), pl.program_id(1)
    rows = rotated_ref.shape[1]

    @pl.when(ball == 0)
    def _():
        picks[...] = spread_column(meta_ref[pl.ds(6 + sample, 1), :])
        for place in range(CLASSES):
            landed[CAP * place : CAP * place + CAP, :] = returned_refs[place][0]

    here = pl.ds(pl.multiple_of(ball * BALL, BALL), BALL)
    hits = one_hot_picks(picks[here, :], rows + SLOTS)
    grad_after = (
        dot(hits[:, :rows], rotated_ref[0]) + dot(hits[:, rows:], landed[...])
    ).astype(bf16)
    grad_input, grad_inward, grad_outward = attention_backward(
        project(nodes_ref[0], inward_ref[...]),
        grad_after,
        inward_ref[...],
        outward_ref[...],
        attended_ref[0],
        prob_cat,
        score_cat,
        grad_stack,
        query_stack,
    )
    grad_ref[0] = grad_input
    first = (sample == 0) & (ball == 0)
    add_up(first, inward_grad_ref, grad_inward)
    add_up(first, outward_grad_ref, grad_outward)


def shifted(value, steps):
    count = lax.axis_size(AXES)
    pairs = [(source, (source + steps) % count) for source in range(count)]
    return lax.ppermute(value, AXES, pairs)


def exchange(packets):
    return [shifted(packets[CLASSES - 1 - place], -OFFSETS[place]) for place in range(CLASSES)]


def reduce_all(parts):
    count = lax.axis_size(AXES)
    flat = jnp.concatenate([part.reshape(-1, 256) for part in parts], axis=0)
    pieces = flat.astype(bf16).reshape(count, -1, 256)
    mine = lax.all_to_all(pieces, AXES, 0, 0, tiled=True)
    total = jnp.sum(mine.astype(f32), axis=0).astype(bf16)
    spread = jnp.broadcast_to(total[None], pieces.shape)
    whole = lax.all_to_all(spread, AXES, 0, 0, tiled=True)
    return whole.reshape(flat.shape)


def per_device(
    nodes,
    cotangent,
    first_inward,
    first_outward,
    second_inward,
    second_outward,
    rotated_source,
    rotated_index,
):
    samples, rows, width = nodes.shape
    shards = lax.axis_size(AXES)
    own = lax.axis_index(AXES).astype(jnp.int32).reshape(1)
    balls = rows // BALL
    params = pltpu.CompilerParams(vmem_limit_bytes=VMEM_LIMIT)
    packet_shape = jax.ShapeDtypeStruct((samples, CAP, width), bf16)
    whole = lambda *shape: pl.BlockSpec(shape, lambda s, b: (0,) * len(shape))
    per_sample = lambda n: pl.BlockSpec((1, n, width), lambda s, b: (s, 0, 0))
    per_ball = pl.BlockSpec((1, BALL, width), lambda s, b: (s, b, 0))
    row_shape = jax.ShapeDtypeStruct((samples, rows, width), bf16)
    grad_shapes = [
        jax.ShapeDtypeStruct((width, 3 * width), f32),
        jax.ShapeDtypeStruct((width, width), f32),
    ]
    grad_specs = [whole(width, 3 * width), whole(width, width)]
    weight_specs = [whole(width, 3 * width), whole(width, width)]
    meta_spec = whole(8, rows)
    attention_scratch = [
        pltpu.VMEM((BALL, HEADS * BALL), bf16),
        pltpu.VMEM((BALL, HEADS * BALL), bf16),
        pltpu.VMEM((HEADS * BALL, width), bf16),
        pltpu.VMEM((HEADS * BALL, width), bf16),
    ]
    vmem = pl.BlockSpec(memory_space=pltpu.VMEM)
    meta, *cot_packets = pl.pallas_call(
        functools.partial(place_kernel, shards=shards),
        name="place",
        in_specs=[pl.BlockSpec(memory_space=pltpu.SMEM), vmem, vmem, vmem],
        out_specs=[vmem] * (1 + CLASSES),
        out_shape=[jax.ShapeDtypeStruct((8, rows), jnp.int32)] + [packet_shape] * CLASSES,
        compiler_params=params,
    )(own, rotated_index, rotated_source, cotangent)
    cot_arrived = exchange(cot_packets)
    after_first, attended_t, *packets = pl.pallas_call(
        forward_kernel,
        name="forward",
        grid=(samples, balls),
        in_specs=[per_ball] + weight_specs + [meta_spec],
        out_specs=[per_sample(rows), per_ball] + [per_sample(CAP)] * CLASSES,
        out_shape=[row_shape, row_shape] + [packet_shape] * CLASSES,
        compiler_params=params,
    )(nodes, first_inward, first_outward, meta)
    arrived = exchange(packets)
    rotated_grad, second_in_grad, second_out_grad, *back_packets = pl.pallas_call(
        second_kernel,
        name="second",
        grid=(samples, balls),
        in_specs=[meta_spec, per_sample(rows), per_sample(rows)]
        + weight_specs
        + [per_sample(CAP)] * (2 * CLASSES),
        out_specs=[per_sample(rows)] + grad_specs + [per_sample(CAP)] * CLASSES,
        out_shape=[row_shape] + grad_shapes + [packet_shape] * CLASSES,
        scratch_shapes=[
            pltpu.VMEM((rows, 128), f32),
            pltpu.VMEM((SLOTS, width), bf16),
            pltpu.VMEM((SLOTS, width), bf16),
        ]
        + attention_scratch,
        compiler_params=params,
    )(meta, after_first, cotangent, second_inward, second_outward, *arrived, *cot_arrived)
    returned = exchange(back_packets)
    input_grad, first_in_grad, first_out_grad = pl.pallas_call(
        first_kernel,
        name="first",
        grid=(samples, balls),
        in_specs=[meta_spec, per_ball, per_sample(rows), per_ball]
        + weight_specs
        + [per_sample(CAP)] * CLASSES,
        out_specs=[per_ball] + grad_specs,
        out_shape=[row_shape] + grad_shapes,
        scratch_shapes=[pltpu.VMEM((rows, 128), f32), pltpu.VMEM((SLOTS, width), bf16)]
        + attention_scratch,
        compiler_params=params,
    )(meta, nodes, rotated_grad, attended_t, first_inward, first_outward, *returned)
    factor = 1.0 / math.sqrt(samples * rows * shards)
    terms = [first_in_grad, first_out_grad, second_in_grad, second_out_grad]
    summed = reduce_all(terms)
    results = []
    start = 0
    for term in terms:
        length = term.size // 256
        results.append(summed[start : start + length].reshape(term.shape).astype(f32) * factor)
        start += length
    return (input_grad, *results)


def solution(mesh):
    in_specs = (
        P(None, AXES, None),
        P(None, AXES, None),
        P(),
        P(),
        P(),
        P(),
        P(None, AXES),
        P(None, AXES),
    )
    out_specs = (P(None, AXES, None), P(), P(), P(), P())
    return jax.shard_map(
        per_device, mesh=mesh, in_specs=in_specs, out_specs=out_specs, check_vma=False
    )
```

```python
import functools
import math

import jax
import jax.numpy as jnp
from jax import lax
from jax.experimental import pallas as pl
from jax.experimental.pallas import tpu as pltpu
from jax.sharding import PartitionSpec as P

HEADS = 8
BALL = 256
SPAN = 8
CAP = 32
EPSILON = 1e-06
AXES = ("pts", "grp")
GROUP = 4
HOPS = tuple(range(-(SPAN // GROUP), SPAN // GROUP + 1))
REACH = len(HOPS)
SLOTS = REACH * GROUP * CAP
VMEM_LIMIT = 56 * 1024 * 1024

f32 = jnp.float32
bf16 = jnp.bfloat16


def dot(left, right, left_dim=1, right_dim=0):
    return lax.dot_general(
        left, right, (((left_dim,), (right_dim,)), ((), ())), preferred_element_type=f32
    )


def spread_column(row):
    return jnp.transpose(jnp.broadcast_to(row.astype(f32), (128, row.shape[1])))


def one_hot_rows(slot_row, slots):
    ids = lax.broadcasted_iota(jnp.int32, (slots, slot_row.shape[1]), 0)
    return jnp.where(ids == slot_row, 1.0, 0.0).astype(bf16)


def one_hot_picks(pick_column, width):
    lanes = lax.broadcasted_iota(jnp.int32, pick_column.shape, 1).astype(f32)
    pieces = [
        jnp.where(pick_column == lanes + float(128 * piece), 1.0, 0.0).astype(bf16)
        for piece in range(width // 128)
    ]
    return jnp.concatenate(pieces, axis=1)


def place_kernel(own_ref, index_ref, source_ref, cot_ref, meta_ref, *packet_refs, shards):
    samples, rows = index_ref.shape
    own = own_ref[0]
    own_start = own * rows
    row_ids = lax.broadcasted_iota(jnp.int32, (rows, 128), 0).astype(f32)
    lane_ids = lax.broadcasted_iota(jnp.int32, (rows, 128), 1).astype(f32)
    shift = rows.bit_length() - 1
    hop_mask = shards // GROUP - 1

    def slots_of(shard, rank):
        member = shard & (GROUP - 1)
        ahead = ((shard >> 2) - (own >> 2) + REACH // 2) & hop_mask
        behind = (REACH - 1) - ahead
        leave = (ahead * GROUP + member) * CAP + rank
        land = (member * REACH + behind) * CAP + rank
        return leave, land

    for sample in range(samples):
        index = index_ref[sample : sample + 1, :]
        source = source_ref[sample : sample + 1, :]
        to_shard = index >> shift
        from_shard = source >> shift
        to_col = spread_column(to_shard)
        source_col = spread_column(source)
        to_row = to_shard.astype(f32)
        source_row = source.astype(f32)
        floor_row = (from_shard << shift).astype(f32)
        send_rank = []
        receive_rank = []
        for piece in range(rows // 128):
            lanes = slice(128 * piece, 128 * piece + 128)
            same = (to_col == to_row[:, lanes]) & (row_ids < lane_ids + float(128 * piece))
            send_rank.append(jnp.sum(jnp.where(same, 1.0, 0.0), axis=0, keepdims=True))
            same = (source_col >= floor_row[:, lanes]) & (source_col < source_row[:, lanes])
            receive_rank.append(jnp.sum(jnp.where(same, 1.0, 0.0), axis=0, keepdims=True))
        send_rank = jnp.concatenate(send_rank, axis=1).astype(jnp.int32)
        receive_rank = jnp.concatenate(receive_rank, axis=1).astype(jnp.int32)
        stays = to_shard == own
        home = from_shard == own
        leave, back_land = slots_of(to_shard, send_rank)
        back_leave, land = slots_of(from_shard, receive_rank)
        leave = jnp.where(stays, -1, leave)
        meta_ref[sample : sample + 1, :] = leave
        meta_ref[2 + sample : 3 + sample, :] = jnp.where(home, -1, back_leave)
        meta_ref[4 + sample : 5 + sample, :] = jnp.where(home, source - own_start, rows + land)
        meta_ref[6 + sample : 7 + sample, :] = jnp.where(stays, index - own_start, rows + back_land)
        packed = dot(one_hot_rows(leave, SLOTS), cot_ref[sample]).astype(bf16)
        for hop in range(REACH):
            for member in range(GROUP):
                start = (hop * GROUP + member) * CAP
                packet_refs[hop][member, sample] = packed[start : start + CAP, :]


LOG2E = 1.4426950408889634


def masked(array, mask):
    return jnp.where(mask, array, jnp.zeros_like(array))


def head_masks(width):
    heads = lax.broadcasted_iota(jnp.int32, (BALL, width), 1) // (width // HEADS)
    own = [heads == head for head in range(HEADS)]
    return own, own[1:] + own[:1]


def project(rows, inward):
    width = rows.shape[1]
    widened = rows.astype(f32)
    row_scale = lax.rsqrt(jnp.mean(widened * widened, axis=-1, keepdims=True) + EPSILON)
    normed = (widened * row_scale).astype(bf16)
    mixture = dot(normed, inward)
    query_raw = mixture[:, :width]
    key_raw = mixture[:, width : 2 * width]
    value_raw = mixture[:, 2 * width :]
    query_scale = lax.rsqrt(jnp.mean(query_raw * query_raw, axis=-1, keepdims=True) + EPSILON)
    key_scale = lax.rsqrt(jnp.mean(key_raw * key_raw, axis=-1, keepdims=True) + EPSILON)
    query_unit = query_raw * query_scale
    key_unit = key_raw * key_scale
    factor = LOG2E * (width // HEADS) ** (-0.5)
    rounded = ((query_unit * factor).astype(bf16), key_unit.astype(bf16), value_raw.astype(bf16))
    return (widened, row_scale, normed, query_unit, query_scale, key_unit, key_scale), rounded


def attend(queries, key_rows, values):
    width = queries.shape[1]
    own, after = head_masks(width)
    sums = jnp.zeros((BALL, width), f32)
    totals = jnp.zeros((BALL, width), f32)
    for head in range(HEADS):
        scores = dot(masked(queries, own[head]), key_rows, 1, 1)
        weights = jnp.exp2(scores).astype(bf16)
        result = dot(weights, jnp.where(own[head], values, jnp.ones_like(values)))
        sums = jnp.where(own[head], result, sums)
        totals = jnp.where(after[head], result, totals)
    inverse = 1.0 / pltpu.roll(totals, width - width // HEADS, 1)
    return sums * inverse, inverse


def attend_backward(queries, key_rows, values, attended, inverse, grad_attended):
    width = queries.shape[1]
    depth = width // HEADS
    own, after = head_masks(width)
    scaled = (grad_attended * inverse).astype(bf16)
    product = scaled.astype(f32) * attended
    high = product.astype(bf16)
    low = (product - high.astype(f32)).astype(bf16)
    groups = lax.broadcasted_iota(jnp.int32, (width, width), 0) // depth
    same_head = groups == lax.broadcasted_iota(jnp.int32, (width, width), 1) // depth
    group_ones = jnp.where(same_head, 1.0, 0.0).astype(bf16)
    column_sum = pltpu.roll(dot(high, group_ones) + dot(low, group_ones), depth, 1)
    column_high = column_sum.astype(bf16)
    column_low = (column_sum - column_high.astype(f32)).astype(bf16)
    lane = lax.broadcasted_iota(jnp.int32, (BALL, width), 1) % depth
    carried = jnp.where(lane == 0, column_high, masked(column_low, lane == 1))
    grad_queries = jnp.zeros((BALL, width), f32)
    grad_keys = jnp.zeros((BALL, width), f32)
    grad_values = jnp.zeros((BALL, width), f32)
    for head in range(HEADS):
        own_keys = masked(key_rows, own[head])
        left = jnp.where(own[head], scaled, masked(carried, after[head]))
        right = jnp.where(after[head], -jnp.ones_like(values), values)
        weights = jnp.exp2(dot(own_keys, queries, 1, 1))
        grad_scores = (weights * dot(right, left, 1, 1)).astype(bf16)
        grad_values += dot(weights.astype(bf16), masked(scaled, own[head]))
        grad_keys += dot(grad_scores, masked(queries, own[head]))
        grad_queries += dot(grad_scores, own_keys, 0, 0)
    return grad_queries, grad_keys * (1.0 / LOG2E), grad_values


def ball_slices(rows):
    return [slice(start, start + BALL) for start in range(0, rows, BALL)]


def block_backward(kept, rounded, attended, inverse, grad_rows, inward, outward):
    widened, row_scale, normed, query_unit, query_scale, key_unit, key_scale = kept
    width = widened.shape[1]
    grad_attended = dot(grad_rows, outward, 1, 1)
    parts = [
        attend_backward(
            *(array[ball] for array in rounded),
            attended[ball].astype(f32),
            inverse[ball],
            grad_attended[ball],
        )
        for ball in ball_slices(widened.shape[0])
    ]
    grad_queries, grad_keys, grad_values = (jnp.concatenate(p, axis=0) for p in zip(*parts))
    grad_queries = grad_queries * (width // HEADS) ** (-0.5)
    grad_qraw = query_scale * (
        grad_queries - query_unit * jnp.mean(grad_queries * query_unit, axis=-1, keepdims=True)
    )
    grad_kraw = key_scale * (
        grad_keys - key_unit * jnp.mean(grad_keys * key_unit, axis=-1, keepdims=True)
    )
    grad_mixture = jnp.concatenate([grad_qraw, grad_kraw, grad_values], axis=1).astype(bf16)
    grad_outward = dot(attended.astype(bf16), grad_rows, 0, 0)
    grad_inward = dot(normed, grad_mixture, 0, 0)
    grad_normed = dot(grad_mixture, inward, 1, 1)
    unit_rows = widened * row_scale
    grad_input = grad_rows.astype(f32) + row_scale * (
        grad_normed - unit_rows * jnp.mean(grad_normed * unit_rows, axis=-1, keepdims=True)
    )
    return grad_input.astype(bf16), grad_inward, grad_outward


def pack(slot_row, rows, packet_refs):
    packed = dot(one_hot_rows(slot_row, SLOTS), rows).astype(bf16)
    for hop in range(REACH):
        for member in range(GROUP):
            start = (hop * GROUP + member) * CAP
            packet_refs[hop][member] = packed[start : start + CAP, :]


def pick(pick_row, home, landed):
    rows = home.shape[0]
    hits = one_hot_picks(spread_column(pick_row), rows + SLOTS)
    return (dot(hits[:, :rows], home) + dot(hits[:, rows:], landed)).astype(bf16)


def put_grads(previous, refs, inward_grad, outward_grad):
    if previous is None:
        refs[0][...] = inward_grad
        refs[1][...] = outward_grad
        return
    width = outward_grad.shape[0]
    inward_grad = inward_grad + previous[0][...]
    for third in range(3):
        part = inward_grad[:, third * width : (third + 1) * width]
        refs[0][third * width : (third + 1) * width, :] = part.astype(bf16)
    refs[0][3 * width :, :] = (outward_grad + previous[1][...]).astype(bf16)


def forward_kernel(
    nodes_ref, inward_ref, outward_ref, meta_ref, after_ref, attended_ref, inverse_ref,
    *packet_refs, sample
):
    kept, rounded = project(nodes_ref[0], inward_ref[...])
    parts = [attend(*(a[ball] for a in rounded)) for ball in ball_slices(nodes_ref.shape[1])]
    attended, inverse = (jnp.concatenate(p, axis=0) for p in zip(*parts))
    attended = attended.astype(bf16)
    attended_ref[...] = attended
    inverse_ref[...] = inverse
    result = (kept[0] + dot(attended, outward_ref[...])).astype(bf16)
    after_ref[...] = result
    pack(meta_ref[sample : sample + 1, :], result, packet_refs)


def second_kernel(*refs, sample):
    meta_ref, after_ref, cot_ref, arrived_ref, cot_arrived_ref, inward_ref, outward_ref = refs[:7]
    refs = refs[7:]
    previous = None
    if sample > 0:
        previous, refs = refs[:2], refs[2:]
    grad_ref, packet_refs, grad_refs = refs[0], refs[1 : 1 + REACH], refs[1 + REACH :]
    width = after_ref.shape[1]
    home = jnp.concatenate([after_ref[...], cot_ref[0]], axis=1)
    cot_landed = cot_arrived_ref[:, sample].reshape(SLOTS, width)
    landed = jnp.concatenate([arrived_ref[...], cot_landed], axis=1)
    both = pick(meta_ref[4 + sample : 5 + sample, :], home, landed)
    rotated, rotated_cot = both[:, :width], both[:, width:]
    kept, rounded = project(rotated, inward_ref[...])
    parts = [attend(*(a[ball] for a in rounded)) for ball in ball_slices(rotated.shape[0])]
    attended, inverse = (jnp.concatenate(p, axis=0) for p in zip(*parts))
    grad_input, inward_grad, outward_grad = block_backward(
        kept, rounded, attended, inverse, rotated_cot, inward_ref[...], outward_ref[...]
    )
    grad_ref[...] = grad_input
    pack(meta_ref[2 + sample : 3 + sample, :], grad_input, packet_refs)
    put_grads(previous, grad_refs, inward_grad, outward_grad)


def first_kernel(*refs, sample):
    meta_ref, nodes_ref, rotated_ref, returned_ref, attended_ref, inverse_ref = refs[:6]
    inward_ref, outward_ref = refs[6:8]
    refs = refs[8:]
    previous = None
    if sample > 0:
        previous, refs = refs[:2], refs[3:]
    grad_ref, grad_refs = refs[0], refs[1:]
    grad_after = pick(meta_ref[6 + sample : 7 + sample, :], rotated_ref[...], returned_ref[...])
    kept, rounded = project(nodes_ref[0], inward_ref[...])
    grad_input, inward_grad, outward_grad = block_backward(
        kept,
        rounded,
        attended_ref[...],
        inverse_ref[...],
        grad_after,
        inward_ref[...],
        outward_ref[...],
    )
    grad_ref[0] = grad_input
    put_grads(previous, grad_refs, inward_grad, outward_grad)


def unpack_kernel(whole_ref, inward_ref, outward_ref):
    width = outward_ref.shape[0]
    for third in range(3):
        columns = slice(third * width, (third + 1) * width)
        inward_ref[:, columns] = whole_ref[columns, :].astype(f32)
    outward_ref[...] = whole_ref[3 * width :, :].astype(f32)


def hop_exchange(packets):
    count = lax.axis_size("pts")
    moved = []
    for hop, packet in zip(HOPS, packets):
        pairs = [(source, (source + hop) % count) for source in range(count)]
        moved.append(packet if hop == 0 else lax.ppermute(packet, "pts", pairs))
    return lax.all_to_all(jnp.stack(moved, axis=1), "grp", 0, 0, tiled=True)


def reduce_all(terms, factor):
    count = lax.axis_size(AXES)
    pieces = terms.reshape(count, -1, terms.shape[1])
    mine = lax.all_to_all(pieces, AXES, 0, 0, tiled=True)
    total = (jnp.sum(mine.astype(f32), axis=0) * factor).astype(bf16)
    spread = jnp.broadcast_to(total[None], pieces.shape)
    return lax.all_to_all(spread, AXES, 0, 0, tiled=True).reshape(terms.shape)


def per_device(
    nodes,
    cotangent,
    first_inward,
    first_outward,
    second_inward,
    second_outward,
    rotated_source,
    rotated_index,
):
    samples, rows, width = nodes.shape
    shards = lax.axis_size(AXES)
    own = lax.axis_index(AXES).astype(jnp.int32).reshape(1)
    shape = jax.ShapeDtypeStruct
    vmem = pl.BlockSpec(memory_space=pltpu.VMEM)
    rows_spec = pl.BlockSpec((rows, width), lambda i: (0, 0))
    row_shape = shape((rows, width), bf16)
    slot_spec = pl.BlockSpec((SLOTS, width), lambda i: (0, 0))
    packet_spec = pl.BlockSpec((GROUP, CAP, width), lambda i: (0, 0, 0))
    packet_shape = shape((GROUP, CAP, width), bf16)
    weight_specs = [
        pl.BlockSpec((width, 3 * width), lambda i: (0, 0)),
        pl.BlockSpec((width, width), lambda i: (0, 0)),
    ]
    grad_shapes = [shape((width, 3 * width), f32), shape((width, width), f32)]
    joined_spec = pl.BlockSpec((4 * width, width), lambda i: (0, 0))
    joined_shape = shape((4 * width, width), bf16)
    meta_spec = pl.BlockSpec((8, rows), lambda i: (0, 0))
    cot_spec = pl.BlockSpec((GROUP * REACH, samples, CAP, width), lambda i: (0, 0, 0, 0))

    def of_sample(sample):
        return pl.BlockSpec((1, rows, width), lambda i: (sample, 0, 0))

    def call(kernel, name, in_specs, out_specs, out_shape, **options):
        return pl.pallas_call(
            kernel,
            name=name,
            grid=(1,),
            in_specs=in_specs,
            out_specs=out_specs,
            out_shape=out_shape,
            compiler_params=pltpu.CompilerParams(vmem_limit_bytes=VMEM_LIMIT),
            **options,
        )

    meta, *cot_packets = pl.pallas_call(
        functools.partial(place_kernel, shards=shards),
        name="place",
        in_specs=[pl.BlockSpec(memory_space=pltpu.SMEM), vmem, vmem, vmem],
        out_specs=[vmem] * (1 + REACH),
        out_shape=[shape((8, rows), jnp.int32)]
        + [shape((GROUP, samples, CAP, width), bf16)] * REACH,
        compiler_params=pltpu.CompilerParams(vmem_limit_bytes=VMEM_LIMIT),
    )(own, rotated_index, rotated_source, cotangent)
    cot_arrived = hop_exchange(cot_packets).reshape(GROUP * REACH, samples, CAP, width)
    forward = []
    arrived = []
    for sample in range(samples):
        after, attended, inverse, *packets = call(
            functools.partial(forward_kernel, sample=sample),
            f"forward{sample}",
            [of_sample(sample)] + weight_specs + [meta_spec],
            [rows_spec] * 3 + [packet_spec] * REACH,
            [row_shape, row_shape, shape((rows, width), f32)] + [packet_shape] * REACH,
        )(nodes, first_inward, first_outward, meta)
        forward.append((after, attended, inverse))
        arrived.append(hop_exchange(packets).reshape(SLOTS, width))
    rotated = []
    returned = []
    second_grads = []
    for sample in range(samples):
        last = sample > 0
        rotated_grad, *rest = call(
            functools.partial(second_kernel, sample=sample),
            f"second{sample}",
            [meta_spec, rows_spec, of_sample(sample), slot_spec, cot_spec]
            + weight_specs * (2 if last else 1),
            [rows_spec] + [packet_spec] * REACH + ([joined_spec] if last else weight_specs),
            [row_shape] + [packet_shape] * REACH + ([joined_shape] if last else grad_shapes),
        )(
            meta,
            forward[sample][0],
            cotangent,
            arrived[sample],
            cot_arrived,
            second_inward,
            second_outward,
            *second_grads,
        )
        second_grads = rest[REACH:]
        rotated.append(rotated_grad)
        returned.append(hop_exchange(rest[:REACH]).reshape(SLOTS, width))
    factor = 1.0 / math.sqrt(samples * rows * shards)
    second_sum = reduce_all(second_grads[0], factor)
    input_grad = []
    first_grads = []
    for sample in range(samples):
        last = sample > 0
        _, attended, inverse = forward[sample]
        grad, *first_grads = call(
            functools.partial(first_kernel, sample=sample),
            f"first{sample}",
            [meta_spec, of_sample(sample), rows_spec, slot_spec, rows_spec, rows_spec]
            + weight_specs * (2 if last else 1)
            + ([pl.BlockSpec(memory_space=pl.ANY)] if last else []),
            [of_sample(sample)] + ([joined_spec] if last else weight_specs),
            [shape(nodes.shape, bf16)] + ([joined_shape] if last else grad_shapes),
            input_output_aliases={10: 0} if last else {},
        )(
            meta,
            nodes,
            rotated[sample],
            returned[sample],
            attended,
            inverse,
            first_inward,
            first_outward,
            *first_grads,
            *input_grad,
        )
        input_grad = [grad]
    first_sum = reduce_all(first_grads[0], factor)
    outs = [input_grad[0]]
    for whole in (first_sum, second_sum):
        outs += call(unpack_kernel, "unpack", [joined_spec], weight_specs, grad_shapes)(whole)
    return tuple(outs)


def solution(mesh):
    in_specs = (
        P(None, AXES, None),
        P(None, AXES, None),
        P(),
        P(),
        P(),
        P(),
        P(None, AXES),
        P(None, AXES),
    )
    out_specs = (P(None, AXES, None), P(), P(), P(), P())
    return jax.shard_map(
        per_device, mesh=mesh, in_specs=in_specs, out_specs=out_specs, check_vma=False
    )
```

```python
import functools
import math

import jax
import jax.numpy as jnp
from jax import lax
from jax.experimental import pallas as pl
from jax.experimental.pallas import tpu as pltpu
from jax.sharding import PartitionSpec as P

HEADS = 8
BALL = 256
SPAN = 8
CAP = 32
EPSILON = 1e-06
AXES = ("pts", "grp")
GROUP = 4
HOPS = tuple(range(-(SPAN // GROUP), SPAN // GROUP + 1))
REACH = len(HOPS)
SLOTS = REACH * GROUP * CAP
VMEM_LIMIT = 56 * 1024 * 1024

f32 = jnp.float32
bf16 = jnp.bfloat16


def dot(left, right, left_dim=1, right_dim=0):
    return lax.dot_general(
        left, right, (((left_dim,), (right_dim,)), ((), ())), preferred_element_type=f32
    )


def spread_column(row):
    return jnp.transpose(jnp.broadcast_to(row.astype(f32), (128, row.shape[1])))


def one_hot_rows(slot_row, slots):
    ids = lax.broadcasted_iota(jnp.int32, (slots, slot_row.shape[1]), 0)
    return jnp.where(ids == slot_row, 1.0, 0.0).astype(bf16)


def one_hot_picks(pick_column, width):
    lanes = lax.broadcasted_iota(jnp.int32, pick_column.shape, 1).astype(f32)
    pieces = [
        jnp.where(pick_column == lanes + float(128 * piece), 1.0, 0.0).astype(bf16)
        for piece in range(width // 128)
    ]
    return jnp.concatenate(pieces, axis=1)


def same_before(column, row, row_ids, lane_ids):
    counts = []
    for piece in range(row.shape[1] // 128):
        lanes = slice(128 * piece, 128 * piece + 128)
        same = (column == row[:, lanes]) & (row_ids < lane_ids + float(128 * piece))
        counts.append(jnp.sum(jnp.where(same, 1.0, 0.0), axis=0, keepdims=True))
    return jnp.concatenate(counts, axis=1).astype(jnp.int32)


def count_between(column, floor_row, row):
    counts = []
    for piece in range(row.shape[1] // 128):
        lanes = slice(128 * piece, 128 * piece + 128)
        inside = (column >= floor_row[:, lanes]) & (column < row[:, lanes])
        counts.append(jnp.sum(jnp.where(inside, 1.0, 0.0), axis=0, keepdims=True))
    return jnp.concatenate(counts, axis=1).astype(jnp.int32)


def slots_of(shard, own, rank, shards):
    member = (shard - own) & (GROUP - 1)
    hop = ((shard // GROUP) - (own // GROUP) + REACH // 2) & (shards // GROUP - 1)
    leave = (hop * GROUP + member) * CAP + rank
    land = (((-member) & (GROUP - 1)) * REACH + (REACH - 1 - hop)) * CAP + rank
    return leave, land


def send_kernel(own_ref, index_ref, cot_ref, meta_ref, *packet_refs, shards):
    samples, rows = index_ref.shape
    own = own_ref[0]
    row_ids = lax.broadcasted_iota(jnp.int32, (rows, 128), 0).astype(f32)
    lane_ids = lax.broadcasted_iota(jnp.int32, (rows, 128), 1).astype(f32)
    for sample in range(samples):
        index = index_ref[sample : sample + 1, :]
        shard = index // rows
        rank = same_before(spread_column(shard), shard.astype(f32), row_ids, lane_ids)
        leave, land = slots_of(shard, own, rank, shards)
        leave = jnp.where(shard == own, -1, leave)
        meta_ref[sample : sample + 1, :] = leave
        meta_ref[samples + sample : samples + sample + 1, :] = jnp.where(
            shard == own, index - own * rows, rows + land
        )
        put_packets(pack(leave, cot_ref[sample]), packet_refs, sample)


def receive_kernel(own_ref, source_ref, meta_ref, *, shards):
    samples, rows = source_ref.shape
    own = own_ref[0]
    for sample in range(samples):
        source = source_ref[sample : sample + 1, :]
        shard = source // rows
        floor_row = (shard * rows).astype(f32)
        rank = count_between(spread_column(source), floor_row, source.astype(f32))
        leave, land = slots_of(shard, own, rank, shards)
        meta_ref[sample : sample + 1, :] = jnp.where(shard == own, -1, leave)
        meta_ref[samples + sample : samples + sample + 1, :] = jnp.where(
            shard == own, source - own * rows, rows + land
        )


def restack_kernel(*refs):
    for hop in range(REACH):
        for member in range(GROUP):
            refs[REACH + member][hop] = refs[hop][member]


LOG2E = 1.4426950408889634


def masked(array, mask):
    return jnp.where(mask, array, jnp.zeros_like(array))


def head_masks(width):
    heads = lax.broadcasted_iota(jnp.int32, (BALL, width), 1) // (width // HEADS)
    own = [heads == head for head in range(HEADS)]
    return own, own[1:] + own[:1]


def project(rows, inward):
    width = rows.shape[1]
    widened = rows.astype(f32)
    row_scale = lax.rsqrt(jnp.mean(widened * widened, axis=-1, keepdims=True) + EPSILON)
    normed = (widened * row_scale).astype(bf16)
    mixture = dot(normed, inward)
    query_raw = mixture[:, :width]
    key_raw = mixture[:, width : 2 * width]
    value_raw = mixture[:, 2 * width :]
    query_scale = lax.rsqrt(jnp.mean(query_raw * query_raw, axis=-1, keepdims=True) + EPSILON)
    key_scale = lax.rsqrt(jnp.mean(key_raw * key_raw, axis=-1, keepdims=True) + EPSILON)
    query_unit = query_raw * query_scale
    key_unit = key_raw * key_scale
    factor = LOG2E * (width // HEADS) ** (-0.5)
    rounded = ((query_unit * factor).astype(bf16), key_unit.astype(bf16), value_raw.astype(bf16))
    return (widened, row_scale, normed, query_unit, query_scale, key_unit, key_scale), rounded


def attend(queries, key_rows, values):
    width = queries.shape[1]
    own, after = head_masks(width)
    sums = jnp.zeros((BALL, width), f32)
    totals = jnp.zeros((BALL, width), f32)
    for head in range(HEADS):
        scores = dot(masked(queries, own[head]), key_rows, 1, 1)
        weights = jnp.exp2(scores).astype(bf16)
        result = dot(weights, jnp.where(own[head], values, jnp.ones_like(values)))
        sums = jnp.where(own[head], result, sums)
        totals = jnp.where(after[head], result, totals)
    inverse = 1.0 / pltpu.roll(totals, width - width // HEADS, 1)
    return sums * inverse, inverse


def attend_backward(queries, key_rows, values, attended, inverse, grad_attended):
    width = queries.shape[1]
    depth = width // HEADS
    own, after = head_masks(width)
    scaled = (grad_attended * inverse).astype(bf16)
    product = scaled.astype(f32) * attended
    high = product.astype(bf16)
    low = (product - high.astype(f32)).astype(bf16)
    groups = lax.broadcasted_iota(jnp.int32, (width, width), 0) // depth
    same_head = groups == lax.broadcasted_iota(jnp.int32, (width, width), 1) // depth
    group_ones = jnp.where(same_head, 1.0, 0.0).astype(bf16)
    column_sum = pltpu.roll(dot(high, group_ones) + dot(low, group_ones), depth, 1)
    column_high = column_sum.astype(bf16)
    column_low = (column_sum - column_high.astype(f32)).astype(bf16)
    lane = lax.broadcasted_iota(jnp.int32, (BALL, width), 1) % depth
    carried = jnp.where(lane == 0, column_high, masked(column_low, lane == 1))
    grad_queries = jnp.zeros((BALL, width), f32)
    grad_keys = jnp.zeros((BALL, width), f32)
    grad_values = jnp.zeros((BALL, width), f32)
    for head in range(HEADS):
        own_keys = masked(key_rows, own[head])
        left = jnp.where(own[head], scaled, masked(carried, after[head]))
        right = jnp.where(after[head], -jnp.ones_like(values), values)
        weights = jnp.exp2(dot(own_keys, queries, 1, 1))
        grad_scores = (weights * dot(right, left, 1, 1)).astype(bf16)
        grad_values += dot(weights.astype(bf16), masked(scaled, own[head]))
        grad_keys += dot(grad_scores, masked(queries, own[head]))
        grad_queries += dot(grad_scores, own_keys, 0, 0)
    return grad_queries, grad_keys * (1.0 / LOG2E), grad_values


def ball_slices(rows):
    return [slice(start, start + BALL) for start in range(0, rows, BALL)]


def block_backward(kept, rounded, attended, inverse, grad_rows, inward, outward):
    widened, row_scale, normed, query_unit, query_scale, key_unit, key_scale = kept
    width = widened.shape[1]
    grad_attended = dot(grad_rows, outward, 1, 1)
    parts = [
        attend_backward(
            *(array[ball] for array in rounded),
            attended[ball].astype(f32),
            inverse[ball],
            grad_attended[ball],
        )
        for ball in ball_slices(widened.shape[0])
    ]
    grad_queries, grad_keys, grad_values = (jnp.concatenate(p, axis=0) for p in zip(*parts))
    grad_queries = grad_queries * (width // HEADS) ** (-0.5)
    grad_qraw = query_scale * (
        grad_queries - query_unit * jnp.mean(grad_queries * query_unit, axis=-1, keepdims=True)
    )
    grad_kraw = key_scale * (
        grad_keys - key_unit * jnp.mean(grad_keys * key_unit, axis=-1, keepdims=True)
    )
    grad_mixture = jnp.concatenate([grad_qraw, grad_kraw, grad_values], axis=1).astype(bf16)
    grad_outward = dot(attended.astype(bf16), grad_rows, 0, 0)
    grad_inward = dot(normed, grad_mixture, 0, 0)
    grad_normed = dot(grad_mixture, inward, 1, 1)
    unit_rows = widened * row_scale
    grad_input = grad_rows.astype(f32) + row_scale * (
        grad_normed - unit_rows * jnp.mean(grad_normed * unit_rows, axis=-1, keepdims=True)
    )
    return grad_input.astype(bf16), grad_inward, grad_outward


def pack(slot_row, rows):
    return dot(one_hot_rows(slot_row, SLOTS), rows).astype(bf16)


def put_packets(packed, packet_refs, sample):
    for hop in range(REACH):
        for member in range(GROUP):
            start = (hop * GROUP + member) * CAP
            packet_refs[hop][member, sample] = packed[start : start + CAP, :]


def pick(pick_row, home, landed):
    rows = home.shape[0]
    hits = one_hot_picks(spread_column(pick_row), rows + SLOTS)
    return (dot(hits[:, :rows], home) + dot(hits[:, rows:], landed)).astype(bf16)


def flat(refs):
    return jnp.concatenate([ref[hop, 0] for ref in refs for hop in range(REACH)], axis=0)


def add_up(total_ref, term):
    first = pl.program_id(0) == 0

    @pl.when(first)
    def _():
        total_ref[...] = term

    @pl.when(jnp.logical_not(first))
    def _():
        total_ref[...] += term


def join_grads(total_ref, start, inward_grad, outward_grad):
    width = outward_grad.shape[0]
    for third in range(3):
        part = inward_grad[:, third * width : (third + 1) * width]
        total_ref[start + third * width : start + (third + 1) * width, :] = part.astype(bf16)
    total_ref[start + 3 * width : start + 4 * width, :] = outward_grad.astype(bf16)


def forward_kernel(nodes_ref, inward_ref, outward_ref, meta_ref, *refs, sample):
    earlier_refs, refs = refs[: sample * REACH], refs[sample * REACH :]
    after_ref, attended_ref, inverse_ref, *packet_refs = refs
    kept, rounded = project(nodes_ref[0], inward_ref[...])
    parts = [attend(*(a[ball] for a in rounded)) for ball in ball_slices(nodes_ref.shape[1])]
    attended, inverse = (jnp.concatenate(p, axis=0) for p in zip(*parts))
    attended = attended.astype(bf16)
    attended_ref[...] = attended
    inverse_ref[...] = inverse
    result = (kept[0] + dot(attended, outward_ref[...])).astype(bf16)
    after_ref[...] = result
    put_packets(pack(meta_ref[sample : sample + 1, :], result), packet_refs, sample)
    for earlier_ref, packet_ref in zip(earlier_refs, packet_refs):
        packet_ref[:, :sample] = earlier_ref[:, :sample]


def sample_row(meta_ref, kind):
    samples = meta_ref.shape[0] // 2
    return meta_ref[pl.ds(kind * samples + pl.program_id(0), 1), :]


def pick_kernel(meta_ref, cot_ref, *refs):
    refs[GROUP][0] = pick(sample_row(meta_ref, 1), cot_ref[0], flat(refs[:GROUP]))


def second_kernel(meta_ref, first_ref, other_ref, cot_ref, inward_ref, outward_ref, *refs):
    arrived_refs, refs = refs[:GROUP], refs[GROUP:]
    grad_ref, inward_grad_ref, outward_grad_ref, *packet_refs = refs
    home = jnp.where(pl.program_id(0) == 0, first_ref[...], other_ref[...])
    rotated = pick(sample_row(meta_ref, 1), home, flat(arrived_refs))
    kept, rounded = project(rotated, inward_ref[...])
    parts = [attend(*(a[ball] for a in rounded)) for ball in ball_slices(rotated.shape[0])]
    attended, inverse = (jnp.concatenate(p, axis=0) for p in zip(*parts))
    grad_input, inward_grad, outward_grad = block_backward(
        kept, rounded, attended, inverse, cot_ref[0], inward_ref[...], outward_ref[...]
    )
    grad_ref[0] = grad_input
    add_up(inward_grad_ref, inward_grad)
    add_up(outward_grad_ref, outward_grad)
    put_packets(pack(sample_row(meta_ref, 0), grad_input), packet_refs, 0)


def first_kernel(meta_ref, nodes_ref, rotated_ref, inward_ref, outward_ref, *refs):
    samples = meta_ref.shape[0] // 2
    kept_refs, refs = refs[: 2 * samples], refs[2 * samples :]
    returned_refs, refs = refs[:GROUP], refs[GROUP:]
    second_grads, refs = refs[:2], refs[2:]
    grad_ref, total_ref, inward_sum, outward_sum = refs
    grad_after = pick(sample_row(meta_ref, 1), rotated_ref[0], flat(returned_refs))
    kept, rounded = project(nodes_ref[0], inward_ref[...])
    first = pl.program_id(0) == 0
    attended = jnp.where(first, kept_refs[0][...], kept_refs[2][...])
    inverse = jnp.where(first, kept_refs[1][...], kept_refs[3][...])
    grad_input, inward_grad, outward_grad = block_backward(
        kept, rounded, attended, inverse, grad_after, inward_ref[...], outward_ref[...]
    )
    grad_ref[0] = grad_input
    add_up(inward_sum, inward_grad)
    add_up(outward_sum, outward_grad)

    @pl.when(pl.program_id(0) == samples - 1)
    def _():
        join_grads(total_ref, 0, inward_sum[...], outward_sum[...])
        join_grads(total_ref, total_ref.shape[0] // 2, *(ref[...] for ref in second_grads))


def split_kernel(whole_ref, *refs):
    width = refs[1].shape[0]
    for place, (inward_ref, outward_ref) in enumerate((refs[:2], refs[2:])):
        start = place * 4 * width
        for third in range(3):
            part = whole_ref[start + third * width : start + (third + 1) * width, :]
            inward_ref[:, third * width : (third + 1) * width] = part.astype(f32)
        outward_ref[...] = whole_ref[start + 3 * width : start + 4 * width, :].astype(f32)


def full_spec(shape):
    return pl.BlockSpec(shape, lambda i: (0,) * len(shape))


def call(kernel, name, micros, in_specs, operands, outs, out_specs=None, steps=1, **options):
    specs = [
        full_spec(operand.shape) if spec is None else spec
        for spec, operand in zip(in_specs or [None] * len(operands), operands)
    ]
    return pl.pallas_call(
        kernel,
        name=name,
        grid=(steps,),
        in_specs=specs,
        out_specs=out_specs or [full_spec(out.shape) for out in outs],
        out_shape=outs,
        compiler_params=pltpu.CompilerParams(vmem_limit_bytes=VMEM_LIMIT),
        cost_estimate=pl.CostEstimate(
            flops=int(micros * 1.15e9), bytes_accessed=2**20, transcendentals=0
        ),
        **options,
    )(*operands)


def rotate(value, axis, steps):
    count = lax.axis_size(axis)
    pairs = [(source, (source + steps) % count) for source in range(count)]
    return lax.ppermute(value, axis, pairs)


def exchange(packets, name):
    moved = [p if hop == 0 else rotate(p, "pts", hop) for hop, p in zip(HOPS, packets)]
    outs = [jax.ShapeDtypeStruct((REACH, *moved[0].shape[1:]), bf16)] * GROUP
    stacked = call(restack_kernel, name, 1, None, moved, outs)
    return [s if member == 0 else rotate(s, "grp", member) for member, s in enumerate(stacked)]


def reduce_all(terms, factor):
    count = lax.axis_size(AXES)
    pieces = terms.reshape(count, -1, terms.shape[1])
    mine = lax.all_to_all(pieces, AXES, 0, 0, tiled=True)
    total = (jnp.sum(mine.astype(f32), axis=0) * factor).astype(bf16)
    spread = jnp.broadcast_to(total[None], pieces.shape)
    return lax.all_to_all(spread, AXES, 0, 0, tiled=True).reshape(terms.shape)


def per_device(
    nodes,
    cotangent,
    first_inward,
    first_outward,
    second_inward,
    second_outward,
    rotated_source,
    rotated_index,
):
    samples, rows, width = nodes.shape
    shards = lax.axis_size(AXES)
    own = lax.axis_index(AXES).astype(jnp.int32).reshape(1)
    shape = jax.ShapeDtypeStruct
    smem = pl.BlockSpec(memory_space=pltpu.SMEM)
    row_shape = shape((rows, width), bf16)
    packet_shapes = [shape((GROUP, samples, CAP, width), bf16)] * REACH
    grad_shapes = [shape((width, 3 * width), f32), shape((width, width), f32)]
    meta_shape = shape((2 * samples, rows), jnp.int32)
    first_weights = (first_inward, first_outward)
    second_weights = (second_inward, second_outward)
    by_sample = pl.BlockSpec((1, rows, width), lambda s: (s, 0, 0))
    packets_by_sample = pl.BlockSpec((GROUP, 1, CAP, width), lambda s: (0, s, 0, 0))
    landed_by_sample = pl.BlockSpec((REACH, 1, CAP, width), lambda s: (0, s, 0, 0))
    send_meta, *cot_packets = call(
        functools.partial(send_kernel, shards=shards),
        "send_places",
        4,
        [smem, None, None],
        (own, rotated_index, cotangent),
        [meta_shape] + packet_shapes,
    )
    cot_arrived = exchange(cot_packets, "restack_cot")
    after_first = []
    kept = []
    packets = []
    for sample in range(samples):
        after, attended, inverse, *packets = call(
            functools.partial(forward_kernel, sample=sample),
            f"forward_s{sample}",
            6,
            [pl.BlockSpec((1, rows, width), lambda i, sample=sample: (sample, 0, 0))]
            + [None] * (3 + len(packets)),
            (nodes, *first_weights, send_meta, *packets),
            [row_shape, row_shape, shape((rows, width), f32)] + packet_shapes,
        )
        after_first.append(after)
        kept += [attended, inverse]
    arrived = exchange(packets, "restack_out")
    (receive_meta,) = call(
        functools.partial(receive_kernel, shards=shards),
        "receive_places",
        2,
        [smem, None],
        (own, rotated_source),
        [meta_shape],
    )
    (rotated_cot,) = call(
        pick_kernel,
        "pick_cot",
        5,
        [None, by_sample] + [landed_by_sample] * GROUP,
        (receive_meta, cotangent, *cot_arrived),
        [shape(nodes.shape, bf16)],
        [by_sample],
        samples,
    )
    rotated_grad, *rest = call(
        second_kernel,
        "second",
        36,
        [None, None, None, by_sample, None, None] + [landed_by_sample] * GROUP,
        (receive_meta, *after_first, rotated_cot, *second_weights, *arrived),
        [shape(nodes.shape, bf16)] + grad_shapes + packet_shapes,
        [by_sample] + [full_spec(g.shape) for g in grad_shapes] + [packets_by_sample] * REACH,
        samples,
    )
    second_grads, back_packets = rest[:2], rest[2:]
    returned = exchange(back_packets, "restack_back")
    joined_shape = shape((8 * width, width), bf16)
    input_grad, joined = call(
        first_kernel,
        "first",
        30,
        [None, by_sample, by_sample]
        + [None] * (2 + len(kept))
        + [landed_by_sample] * GROUP
        + [None, None],
        (send_meta, nodes, rotated_grad, *first_weights, *kept, *returned, *second_grads),
        [shape(nodes.shape, bf16), joined_shape],
        [by_sample, full_spec(joined_shape.shape)],
        samples,
        scratch_shapes=[pltpu.VMEM(g.shape, f32) for g in grad_shapes],
    )
    factor = 1.0 / math.sqrt(samples * rows * shards)
    summed = reduce_all(joined, factor)
    grads = call(split_kernel, "split", 2, None, (summed,), grad_shapes * 2)
    return (input_grad, *grads)


def solution(mesh):
    in_specs = (
        P(None, AXES, None),
        P(None, AXES, None),
        P(),
        P(),
        P(),
        P(),
        P(None, AXES),
        P(None, AXES),
    )
    out_specs = (P(None, AXES, None), P(), P(), P(), P())
    return jax.shard_map(
        per_device, mesh=mesh, in_specs=in_specs, out_specs=out_specs, check_vma=False
    )
```

```python
import functools
import math

import jax
import jax.numpy as jnp
from jax import lax
from jax.experimental import pallas as pl
from jax.experimental.pallas import tpu as pltpu
from jax.sharding import PartitionSpec as P

HEADS = 8
BALL = 256
SPAN = 8
CAP = 32
EPSILON = 1e-06
AXES = ("pts", "grp")
GROUP = 4
HOPS = tuple(range(-(SPAN // GROUP), SPAN // GROUP + 1))
REACH = len(HOPS)
SLOTS = REACH * GROUP * CAP
LANDED = REACH + GROUP - 1
VMEM_LIMIT = 56 * 1024 * 1024

f32 = jnp.float32
bf16 = jnp.bfloat16


def dot(left, right, left_dim=1, right_dim=0):
    return lax.dot_general(
        left, right, (((left_dim,), (right_dim,)), ((), ())), preferred_element_type=f32
    )


def spread_column(row):
    return jnp.transpose(jnp.broadcast_to(row.astype(f32), (128, row.shape[1])))


def one_hot_rows(slot_row, slots):
    ids = lax.broadcasted_iota(jnp.int32, (slots, slot_row.shape[1]), 0)
    return jnp.where(ids == slot_row, 1.0, 0.0).astype(bf16)


def one_hot_picks(pick_column, start, width):
    lanes = lax.broadcasted_iota(jnp.int32, pick_column.shape, 1).astype(f32)
    pieces = [
        jnp.where(pick_column == lanes + float(start + 128 * piece), 1.0, 0.0).astype(bf16)
        for piece in range(width // 128)
    ]
    return jnp.concatenate(pieces, axis=1)


def same_before(column, row, row_ids, lane_ids):
    counts = []
    for piece in range(row.shape[1] // 128):
        lanes = slice(128 * piece, 128 * piece + 128)
        same = (column == row[:, lanes]) & (row_ids < lane_ids + float(128 * piece))
        counts.append(jnp.sum(jnp.where(same, 1.0, 0.0), axis=0, keepdims=True))
    return jnp.concatenate(counts, axis=1).astype(jnp.int32)


def count_between(column, floor_row, row):
    counts = []
    for piece in range(row.shape[1] // 128):
        lanes = slice(128 * piece, 128 * piece + 128)
        inside = (column >= floor_row[:, lanes]) & (column < row[:, lanes])
        counts.append(jnp.sum(jnp.where(inside, 1.0, 0.0), axis=0, keepdims=True))
    return jnp.concatenate(counts, axis=1).astype(jnp.int32)


def slots_of(shard, own, rank, shards):
    member = (shard - own) & (GROUP - 1)
    hop = ((shard // GROUP) - (own // GROUP) + REACH // 2) & (shards // GROUP - 1)
    leave = (hop * GROUP + member) * CAP + rank
    land = (((-member) & (GROUP - 1)) * REACH + (REACH - 1 - hop)) * CAP + rank
    return leave, land


def send_kernel(own_ref, index_ref, cot_ref, meta_ref, *packet_refs, shards):
    samples, rows = index_ref.shape
    own = own_ref[0]
    row_ids = lax.broadcasted_iota(jnp.int32, (rows, 128), 0).astype(f32)
    lane_ids = lax.broadcasted_iota(jnp.int32, (rows, 128), 1).astype(f32)
    for sample in range(samples):
        index = index_ref[sample : sample + 1, :]
        shard = index // rows
        rank = same_before(spread_column(shard), shard.astype(f32), row_ids, lane_ids)
        leave, land = slots_of(shard, own, rank, shards)
        leave = jnp.where(shard == own, -1, leave)
        meta_ref[sample : sample + 1, :] = leave
        meta_ref[samples + sample : samples + sample + 1, :] = jnp.where(
            shard == own, index - own * rows, rows + land
        )
        put_packets(pack(leave, cot_ref[sample]), packet_refs, sample)


def receive_kernel(own_ref, source_ref, meta_ref, *, shards):
    samples, rows = source_ref.shape
    own = own_ref[0]
    for sample in range(samples):
        source = source_ref[sample : sample + 1, :]
        shard = source // rows
        floor_row = (shard * rows).astype(f32)
        rank = count_between(spread_column(source), floor_row, source.astype(f32))
        leave, land = slots_of(shard, own, rank, shards)
        meta_ref[sample : sample + 1, :] = jnp.where(shard == own, -1, leave)
        meta_ref[samples + sample : samples + sample + 1, :] = jnp.where(
            shard == own, source - own * rows, rows + land
        )


def restack_kernel(*refs):
    for hop in range(REACH):
        for member in range(1, GROUP):
            refs[REACH + member - 1][hop] = refs[hop][member]


LOG2E = 1.4426950408889634
JOINED = 4


def masked(array, mask):
    return jnp.where(mask, array, jnp.zeros_like(array))


def head_masks(width):
    heads = lax.broadcasted_iota(jnp.int32, (BALL, width), 1) // (width // HEADS)
    own = [heads == head for head in range(HEADS)]
    return own, own[1:] + own[:1]


def project(rows, inward):
    width = rows.shape[1]
    widened = rows.astype(f32)
    row_scale = lax.rsqrt(jnp.mean(widened * widened, axis=-1, keepdims=True) + EPSILON)
    normed = (widened * row_scale).astype(bf16)
    mixture = dot(normed, inward)
    query_raw = mixture[:, :width]
    key_raw = mixture[:, width : 2 * width]
    value_raw = mixture[:, 2 * width :]
    query_scale = lax.rsqrt(jnp.mean(query_raw * query_raw, axis=-1, keepdims=True) + EPSILON)
    key_scale = lax.rsqrt(jnp.mean(key_raw * key_raw, axis=-1, keepdims=True) + EPSILON)
    query_unit = query_raw * query_scale
    key_unit = key_raw * key_scale
    factor = LOG2E * (width // HEADS) ** (-0.5)
    rounded = ((query_unit * factor).astype(bf16), key_unit.astype(bf16), value_raw.astype(bf16))
    return (widened, row_scale, normed, query_unit, query_scale, key_unit, key_scale), rounded


def attend(queries, key_rows, values):
    width = queries.shape[1]
    half = width // 2
    own, _ = head_masks(width)
    results = []
    for start in range(0, HEADS, HEADS // 2):
        weights = []
        rights = []
        for head in range(start, start + HEADS // 2):
            scores = dot(masked(queries, own[head]), key_rows, 1, 1)
            weights.append(jnp.exp2(scores).astype(bf16))
            opposite = own[(head + HEADS // 2) % HEADS]
            ones = jnp.where(opposite, jnp.ones_like(values), jnp.zeros_like(values))
            rights.append(jnp.where(own[head], values, ones))
        results.append(dot(jnp.concatenate(weights, axis=1), jnp.concatenate(rights, axis=0)))
    low, high = results
    sums = jnp.concatenate([low[:, :half], high[:, half:]], axis=1)
    inverse = 1.0 / jnp.concatenate([low[:, half:], high[:, :half]], axis=1)
    return sums * inverse, inverse


def attend_backward(queries, key_rows, values, attended, inverse, grad_attended):
    width = queries.shape[1]
    depth = width // HEADS
    own, after = head_masks(width)
    scaled = (grad_attended * inverse).astype(bf16)
    product = scaled.astype(f32) * attended
    high = product.astype(bf16)
    low = (product - high.astype(f32)).astype(bf16)
    groups = lax.broadcasted_iota(jnp.int32, (width, width), 0) // depth
    same_head = groups == lax.broadcasted_iota(jnp.int32, (width, width), 1) // depth
    group_ones = jnp.where(same_head, 1.0, 0.0).astype(bf16)
    column_sum = pltpu.roll(dot(high, group_ones) + dot(low, group_ones), depth, 1)
    column_high = column_sum.astype(bf16)
    column_low = (column_sum - column_high.astype(f32)).astype(bf16)
    lane = lax.broadcasted_iota(jnp.int32, (BALL, width), 1) % depth
    carried = jnp.where(lane == 0, column_high, masked(column_low, lane == 1))
    grad_queries = jnp.zeros((BALL, width), f32)
    grad_keys = jnp.zeros((BALL, width), f32)
    grad_values = jnp.zeros((BALL, width), f32)
    for start in range(0, HEADS, JOINED):
        weight_parts, score_parts, scaled_parts, query_parts, key_parts = [], [], [], [], []
        for head in range(start, start + JOINED):
            own_keys = masked(key_rows, own[head])
            left = jnp.where(own[head], scaled, masked(carried, after[head]))
            right = jnp.where(after[head], -jnp.ones_like(values), values)
            weights = jnp.exp2(dot(own_keys, queries, 1, 1))
            score_parts.append((weights * dot(right, left, 1, 1)).astype(bf16))
            weight_parts.append(weights.astype(bf16))
            scaled_parts.append(masked(scaled, own[head]))
            query_parts.append(masked(queries, own[head]))
            key_parts.append(own_keys)
        grad_values += dot(
            jnp.concatenate(weight_parts, axis=1), jnp.concatenate(scaled_parts, axis=0)
        )
        grad_keys += dot(
            jnp.concatenate(score_parts, axis=1), jnp.concatenate(query_parts, axis=0)
        )
        grad_queries += dot(
            jnp.concatenate(score_parts, axis=0), jnp.concatenate(key_parts, axis=0), 0, 0
        )
    return grad_queries, grad_keys * (1.0 / LOG2E), grad_values


def ball_slices(rows):
    return [slice(start, start + BALL) for start in range(0, rows, BALL)]


def block_backward(kept, rounded, attended, inverse, grad_rows, inward, outward):
    widened, row_scale, normed, query_unit, query_scale, key_unit, key_scale = kept
    width = widened.shape[1]
    grad_attended = dot(grad_rows, outward, 1, 1)
    parts = [
        attend_backward(
            *(array[ball] for array in rounded),
            attended[ball].astype(f32),
            inverse[ball],
            grad_attended[ball],
        )
        for ball in ball_slices(widened.shape[0])
    ]
    grad_queries, grad_keys, grad_values = (jnp.concatenate(p, axis=0) for p in zip(*parts))
    grad_queries = grad_queries * (width // HEADS) ** (-0.5)
    grad_qraw = query_scale * (
        grad_queries - query_unit * jnp.mean(grad_queries * query_unit, axis=-1, keepdims=True)
    )
    grad_kraw = key_scale * (
        grad_keys - key_unit * jnp.mean(grad_keys * key_unit, axis=-1, keepdims=True)
    )
    grad_mixture = jnp.concatenate([grad_qraw, grad_kraw, grad_values], axis=1).astype(bf16)
    grad_outward = dot(attended.astype(bf16), grad_rows, 0, 0)
    grad_inward = dot(normed, grad_mixture, 0, 0)
    grad_normed = dot(grad_mixture, inward, 1, 1)
    unit_rows = widened * row_scale
    grad_input = grad_rows.astype(f32) + row_scale * (
        grad_normed - unit_rows * jnp.mean(grad_normed * unit_rows, axis=-1, keepdims=True)
    )
    return grad_input.astype(bf16), grad_inward, grad_outward


def pack(slot_row, rows):
    return dot(one_hot_rows(slot_row, SLOTS), rows).astype(bf16)


def put_packets(packed, packet_refs, sample):
    for hop in range(REACH):
        for member in range(GROUP):
            start = (hop * GROUP + member) * CAP
            packet_refs[hop][member, sample] = packed[start : start + CAP, :]


def pick_near(pick_row, home):
    return dot(one_hot_picks(spread_column(pick_row), 0, home.shape[0]), home)


def pick_far(pick_row, home_rows, landed):
    return dot(one_hot_picks(spread_column(pick_row), home_rows, SLOTS), landed)


def flat(refs):
    parts = [ref[0, 0] for ref in refs[:REACH]]
    parts += [ref[hop, 0] for ref in refs[REACH:] for hop in range(REACH)]
    return jnp.concatenate(parts, axis=0)


def add_up(total_ref, term):
    first = pl.program_id(0) == 0

    @pl.when(first)
    def _():
        total_ref[...] = term

    @pl.when(jnp.logical_not(first))
    def _():
        total_ref[...] += term


def join_grads(total_ref, inward_grad, outward_grad):
    width = outward_grad.shape[0]
    for third in range(3):
        part = inward_grad[:, third * width : (third + 1) * width]
        total_ref[third * width : (third + 1) * width, :] = part.astype(bf16)
    total_ref[3 * width : 4 * width, :] = outward_grad.astype(bf16)


def add_grads(total_ref, sum_refs, grads, other_ref=None):
    for sum_ref, grad in zip(sum_refs, grads):
        add_up(sum_ref, grad)

    @pl.when(pl.program_id(0) == pl.num_programs(0) - 1)
    def _():
        join_grads(total_ref, *(ref[...] for ref in sum_refs))
        if other_ref is not None:
            total_ref[other_ref.shape[0] :, :] = other_ref[...]


def forward_kernel(nodes_ref, inward_ref, outward_ref, meta_ref, *refs, sample):
    earlier = (REACH + 3) * min(sample, 1)
    earlier_refs = refs[:earlier][3:]
    after_ref, attended_ref, inverse_ref, *packet_refs = refs[earlier:]
    kept, rounded = project(nodes_ref[0], inward_ref[...])
    parts = [attend(*(a[ball] for a in rounded)) for ball in ball_slices(nodes_ref.shape[1])]
    attended, inverse = (jnp.concatenate(p, axis=0) for p in zip(*parts))
    attended = attended.astype(bf16)
    attended_ref[0] = attended
    inverse_ref[0] = inverse
    result = (kept[0] + dot(attended, outward_ref[...])).astype(bf16)
    after_ref[0] = result
    put_packets(pack(meta_ref[sample : sample + 1, :], result), packet_refs, sample)
    for earlier_ref, packet_ref in zip(earlier_refs, packet_refs):
        packet_ref[:, :sample] = earlier_ref[:, :sample]


def sample_row(meta_ref, kind):
    samples = meta_ref.shape[0] // 2
    return meta_ref[pl.ds(kind * samples + pl.program_id(0), 1), :]


def near_cot_kernel(meta_ref, after_ref, cot_ref, *refs):
    near_ref, rotated_cot_ref = refs[LANDED:]
    width = after_ref.shape[2]
    row = sample_row(meta_ref, 1)
    home = jnp.concatenate([after_ref[0], cot_ref[0]], axis=1)
    near = pick_near(row, home)
    near_ref[0] = near[:, :width].astype(bf16)
    far = pick_far(row, home.shape[0], flat(refs[:LANDED]))
    rotated_cot_ref[0] = (near[:, width:] + far).astype(bf16)


def near_kernel(meta_ref, home_ref, near_ref):
    near_ref[0] = pick_near(sample_row(meta_ref, 1), home_ref[0]).astype(bf16)


def second_kernel(meta_ref, near_ref, cot_ref, inward_ref, outward_ref, *refs):
    arrived_refs, refs = refs[:LANDED], refs[LANDED:]
    grad_ref, total_ref, *packet_refs = refs[: 2 + REACH]
    far = pick_far(sample_row(meta_ref, 1), near_ref.shape[1], flat(arrived_refs))
    rotated = (near_ref[0].astype(f32) + far).astype(bf16)
    kept, rounded = project(rotated, inward_ref[...])
    parts = [attend(*(a[ball] for a in rounded)) for ball in ball_slices(rotated.shape[0])]
    attended, inverse = (jnp.concatenate(p, axis=0) for p in zip(*parts))
    grad_input, *grads = block_backward(
        kept, rounded, attended, inverse, cot_ref[0], inward_ref[...], outward_ref[...]
    )
    grad_ref[0] = grad_input
    add_grads(total_ref, refs[2 + REACH :], grads)
    put_packets(pack(sample_row(meta_ref, 0), grad_input), packet_refs, 0)


def first_kernel(
    meta_ref, nodes_ref, near_ref, attended_ref, inverse_ref, inward_ref, outward_ref, *refs
):
    returned_refs, refs = refs[:LANDED], refs[LANDED:]
    other_ref, grad_ref, total_ref, *sum_refs = refs
    far = pick_far(sample_row(meta_ref, 1), near_ref.shape[1], flat(returned_refs))
    grad_after = (near_ref[0].astype(f32) + far).astype(bf16)
    kept, rounded = project(nodes_ref[0], inward_ref[...])
    grad_input, *grads = block_backward(
        kept,
        rounded,
        attended_ref[0],
        inverse_ref[0],
        grad_after,
        inward_ref[...],
        outward_ref[...],
    )
    grad_ref[0] = grad_input
    add_grads(total_ref, sum_refs, grads, other_ref)


def split_kernel(whole_ref, *refs):
    width = refs[1].shape[0]
    for place, (inward_ref, outward_ref) in enumerate((refs[:2], refs[2:])):
        start = place * 4 * width
        for third in range(3):
            part = whole_ref[start + third * width : start + (third + 1) * width, :]
            inward_ref[:, third * width : (third + 1) * width] = part.astype(f32)
        outward_ref[...] = whole_ref[start + 3 * width : start + 4 * width, :].astype(f32)


def full_spec(shape):
    return pl.BlockSpec(shape, lambda i: (0,) * len(shape))


def call(kernel, name, micros, in_specs, operands, outs, out_specs=None, steps=1, **options):
    specs = [
        full_spec(operand.shape) if spec is None else spec
        for spec, operand in zip(in_specs or [None] * len(operands), operands)
    ]
    return pl.pallas_call(
        kernel,
        name=name,
        grid=(steps,),
        in_specs=specs,
        out_specs=out_specs or [full_spec(out.shape) for out in outs],
        out_shape=outs,
        compiler_params=pltpu.CompilerParams(vmem_limit_bytes=VMEM_LIMIT),
        cost_estimate=pl.CostEstimate(
            flops=int(micros * 1.15e9), bytes_accessed=2**20, transcendentals=0
        ),
        **options,
    )(*operands)


def rotate(value, axis, steps):
    count = lax.axis_size(axis)
    pairs = [(source, (source + steps) % count) for source in range(count)]
    return lax.ppermute(value, axis, pairs)


def hop_stage(packets):
    return [p if hop == 0 else rotate(p, "pts", hop) for hop, p in zip(HOPS, packets)]


def restack(moved, name):
    outs = [jax.ShapeDtypeStruct((REACH, *moved[0].shape[1:]), bf16)] * (GROUP - 1)
    return call(restack_kernel, name, 2, None, moved, outs)


def member_stage(moved, stacked):
    return moved + [rotate(s, "grp", 1 + place) for place, s in enumerate(stacked)]


def exchange(packets, name):
    moved = hop_stage(packets)
    return member_stage(moved, restack(moved, name))


def reduce_all(terms, factor):
    count = lax.axis_size(AXES)
    pieces = terms.reshape(count, -1, terms.shape[1])
    mine = lax.all_to_all(pieces, AXES, 0, 0, tiled=True)
    total = (jnp.sum(mine.astype(f32), axis=0) * factor).astype(bf16)
    spread = jnp.broadcast_to(total[None], pieces.shape)
    return lax.all_to_all(spread, AXES, 0, 0, tiled=True).reshape(terms.shape)


def per_device(
    nodes,
    cotangent,
    first_inward,
    first_outward,
    second_inward,
    second_outward,
    rotated_source,
    rotated_index,
):
    samples, rows, width = nodes.shape
    shards = lax.axis_size(AXES)
    own = lax.axis_index(AXES).astype(jnp.int32).reshape(1)
    shape = jax.ShapeDtypeStruct
    smem = pl.BlockSpec(memory_space=pltpu.SMEM)
    rows_shape = shape(nodes.shape, bf16)
    packet_shapes = [shape((GROUP, samples, CAP, width), bf16)] * REACH
    meta_shape = shape((2 * samples, rows), jnp.int32)
    joined_shape = shape((4 * width, width), bf16)
    sums = [pltpu.VMEM((width, 3 * width), f32), pltpu.VMEM((width, width), f32)]
    first_weights = (first_inward, first_outward)
    second_weights = (second_inward, second_outward)
    by_sample = pl.BlockSpec((1, rows, width), lambda s: (s, 0, 0))
    packets_by_sample = pl.BlockSpec((GROUP, 1, CAP, width), lambda s: (0, s, 0, 0))
    landed_by_sample = [pl.BlockSpec((1, 1, CAP, width), lambda s: (0, s, 0, 0))] * REACH
    landed_by_sample += [pl.BlockSpec((REACH, 1, CAP, width), lambda s: (0, s, 0, 0))] * (GROUP - 1)
    send_meta, *cot_packets = call(
        functools.partial(send_kernel, shards=shards),
        "send_places",
        4,
        [smem, None, None],
        (own, rotated_index, cotangent),
        [meta_shape] + packet_shapes,
    )
    cot_moved = hop_stage(cot_packets)
    forward = []
    for sample in range(samples):
        one = pl.BlockSpec((1, rows, width), lambda i, sample=sample: (sample, 0, 0))
        meta = send_meta
        if sample > 0:
            cot_stacked, meta = lax.optimization_barrier((restack(cot_moved, "restack_cot"), meta))
            cot_arrived = member_stage(cot_moved, cot_stacked)
        forward = call(
            functools.partial(forward_kernel, sample=sample),
            f"forward_s{sample}",
            6,
            [one, None, None, None]
            + ([pl.BlockSpec(memory_space=pl.ANY)] * 3 + [None] * REACH if forward else []),
            (nodes, *first_weights, meta, *forward),
            [rows_shape, rows_shape, shape(nodes.shape, f32)] + packet_shapes,
            [one] * 3 + [full_spec(p.shape) for p in packet_shapes],
            input_output_aliases={4: 0, 5: 1, 6: 2} if forward else {},
        )
    after_first, attended, inverse, *packets = forward
    packets, cot_arrived = lax.optimization_barrier((packets, cot_arrived))
    arrived = exchange(packets, "restack_out")
    (receive_meta,) = call(
        functools.partial(receive_kernel, shards=shards),
        "receive_places",
        2,
        [smem, None],
        (own, rotated_source),
        [meta_shape],
    )
    near, rotated_cot = call(
        near_cot_kernel,
        "near_cot",
        6,
        [None, by_sample, by_sample] + landed_by_sample,
        (receive_meta, after_first, cotangent, *cot_arrived),
        [rows_shape] * 2,
        [by_sample] * 2,
        samples,
    )
    rotated_grad, second_joined, *back_packets = call(
        second_kernel,
        "second",
        36,
        [None, by_sample, by_sample, None, None] + landed_by_sample,
        (receive_meta, near, rotated_cot, *second_weights, *arrived),
        [rows_shape, joined_shape] + packet_shapes,
        [by_sample, full_spec(joined_shape.shape)] + [packets_by_sample] * REACH,
        samples,
        scratch_shapes=sums,
    )
    returned = exchange(back_packets, "restack_back")
    (grad_near,) = call(
        near_kernel,
        "near_grad",
        3,
        [None, by_sample],
        (send_meta, rotated_grad),
        [rows_shape],
        [by_sample],
        samples,
    )
    both_shape = shape((8 * width, width), bf16)
    input_grad, joined = call(
        first_kernel,
        "first",
        30,
        [None] + [by_sample] * 4 + [None, None] + landed_by_sample + [None],
        (
            send_meta,
            nodes,
            grad_near,
            attended,
            inverse,
            *first_weights,
            *returned,
            second_joined,
        ),
        [rows_shape, both_shape],
        [by_sample, full_spec(both_shape.shape)],
        samples,
        scratch_shapes=sums,
    )
    factor = 1.0 / math.sqrt(samples * rows * shards)
    grad_shapes = [shape((width, 3 * width), f32), shape((width, width), f32)]
    grads = call(split_kernel, "split", 2, None, (reduce_all(joined, factor),), grad_shapes * 2)
    return (input_grad, *grads)


def solution(mesh):
    in_specs = (
        P(None, AXES, None),
        P(None, AXES, None),
        P(),
        P(),
        P(),
        P(),
        P(None, AXES),
        P(None, AXES),
    )
    out_specs = (P(None, AXES, None), P(), P(), P(), P())
    return jax.shard_map(
        per_device, mesh=mesh, in_specs=in_specs, out_specs=out_specs, check_vma=False
    )
```

```python
import functools
import math

import jax
import jax.numpy as jnp
from jax import lax
from jax.experimental import pallas as pl
from jax.experimental.pallas import tpu as pltpu
from jax.sharding import PartitionSpec as P

HEADS = 8
BALL = 256
SPAN = 8
CAP = 32
EPSILON = 1e-06
AXES = ("pts", "grp")
GROUP = 4
HOPS = tuple(range(-(SPAN // GROUP), SPAN // GROUP + 1))
REACH = len(HOPS)
SLOTS = REACH * GROUP * CAP
LANDED = REACH + GROUP - 1
VMEM_LIMIT = 28 * 1024 * 1024

f32 = jnp.float32
bf16 = jnp.bfloat16


def dot(left, right, left_dim=1, right_dim=0):
    return lax.dot_general(
        left, right, (((left_dim,), (right_dim,)), ((), ())), preferred_element_type=f32
    )


def spread_column(row):
    return jnp.transpose(jnp.broadcast_to(row.astype(f32), (128, row.shape[1])))


def one_hot_rows(slot_row, slots):
    ids = lax.broadcasted_iota(jnp.int32, (slots, slot_row.shape[1]), 0)
    return jnp.where(ids == slot_row, 1.0, 0.0).astype(bf16)


def one_hot_picks(pick_column, start, width):
    lanes = lax.broadcasted_iota(jnp.int32, pick_column.shape, 1).astype(f32)
    pieces = [
        jnp.where(pick_column == lanes + float(start + 128 * piece), 1.0, 0.0).astype(bf16)
        for piece in range(width // 128)
    ]
    return jnp.concatenate(pieces, axis=1)


def same_before(column, row, row_ids, lane_ids):
    counts = []
    for piece in range(row.shape[1] // 128):
        lanes = slice(128 * piece, 128 * piece + 128)
        same = (column == row[:, lanes]) & (row_ids < lane_ids + float(128 * piece))
        counts.append(jnp.sum(jnp.where(same, 1.0, 0.0), axis=0, keepdims=True))
    return jnp.concatenate(counts, axis=1).astype(jnp.int32)


def count_between(column, floor_row, row):
    counts = []
    for piece in range(row.shape[1] // 128):
        lanes = slice(128 * piece, 128 * piece + 128)
        inside = (column >= floor_row[:, lanes]) & (column < row[:, lanes])
        counts.append(jnp.sum(jnp.where(inside, 1.0, 0.0), axis=0, keepdims=True))
    return jnp.concatenate(counts, axis=1).astype(jnp.int32)


def slots_of(shard, own, rank, shards):
    member = (shard - own) & (GROUP - 1)
    hop = ((shard // GROUP) - (own // GROUP) + REACH // 2) & (shards // GROUP - 1)
    leave = (hop * GROUP + member) * CAP + rank
    land = (((-member) & (GROUP - 1)) * REACH + (REACH - 1 - hop)) * CAP + rank
    return leave, land


def send_kernel(own_ref, index_ref, cot_ref, meta_ref, *packet_refs, shards):
    samples, rows = index_ref.shape
    own = own_ref[0]
    row_ids = lax.broadcasted_iota(jnp.int32, (rows, 128), 0).astype(f32)
    lane_ids = lax.broadcasted_iota(jnp.int32, (rows, 128), 1).astype(f32)
    for sample in range(samples):
        index = index_ref[sample : sample + 1, :]
        shard = index // rows
        rank = same_before(spread_column(shard), shard.astype(f32), row_ids, lane_ids)
        leave, land = slots_of(shard, own, rank, shards)
        leave = jnp.where(shard == own, -1, leave)
        meta_ref[sample : sample + 1, :] = leave
        meta_ref[samples + sample : samples + sample + 1, :] = jnp.where(
            shard == own, index - own * rows, rows + land
        )
        put_packets(pack(leave, cot_ref[sample]), packet_refs, sample)


def receive_kernel(own_ref, source_ref, meta_ref, *, shards):
    samples, rows = source_ref.shape
    own = own_ref[0]
    for sample in range(samples):
        source = source_ref[sample : sample + 1, :]
        shard = source // rows
        floor_row = (shard * rows).astype(f32)
        rank = count_between(spread_column(source), floor_row, source.astype(f32))
        leave, land = slots_of(shard, own, rank, shards)
        meta_ref[sample : sample + 1, :] = jnp.where(shard == own, -1, leave)
        meta_ref[samples + sample : samples + sample + 1, :] = jnp.where(
            shard == own, source - own * rows, rows + land
        )


LOG2E = 1.4426950408889634
JOINED = 4


def masked(array, mask):
    return jnp.where(mask, array, jnp.zeros_like(array))


def head_masks(width):
    heads = lax.broadcasted_iota(jnp.int32, (BALL, width), 1) // (width // HEADS)
    own = [heads == head for head in range(HEADS)]
    return own, own[1:] + own[:1]


def project(rows, inward):
    width = rows.shape[1]
    widened = rows.astype(f32)
    row_scale = lax.rsqrt(jnp.mean(widened * widened, axis=-1, keepdims=True) + EPSILON)
    normed = (widened * row_scale).astype(bf16)
    mixture = dot(normed, inward)
    query_raw = mixture[:, :width]
    key_raw = mixture[:, width : 2 * width]
    value_raw = mixture[:, 2 * width :]
    query_scale = lax.rsqrt(jnp.mean(query_raw * query_raw, axis=-1, keepdims=True) + EPSILON)
    key_scale = lax.rsqrt(jnp.mean(key_raw * key_raw, axis=-1, keepdims=True) + EPSILON)
    query_unit = query_raw * query_scale
    key_unit = key_raw * key_scale
    factor = LOG2E * (width // HEADS) ** (-0.5)
    rounded = ((query_unit * factor).astype(bf16), key_unit.astype(bf16), value_raw.astype(bf16))
    return (widened, row_scale, normed, query_unit, query_scale, key_unit, key_scale), rounded


def attend(queries, key_rows, values):
    width = queries.shape[1]
    half = width // 2
    own, _ = head_masks(width)
    results = []
    for start in range(0, HEADS, HEADS // 2):
        weights = []
        rights = []
        for head in range(start, start + HEADS // 2):
            scores = dot(masked(queries, own[head]), key_rows, 1, 1)
            weights.append(jnp.exp2(scores).astype(bf16))
            opposite = own[(head + HEADS // 2) % HEADS]
            ones = jnp.where(opposite, jnp.ones_like(values), jnp.zeros_like(values))
            rights.append(jnp.where(own[head], values, ones))
        results.append(dot(jnp.concatenate(weights, axis=1), jnp.concatenate(rights, axis=0)))
    low, high = results
    sums = jnp.concatenate([low[:, :half], high[:, half:]], axis=1)
    inverse = 1.0 / jnp.concatenate([low[:, half:], high[:, :half]], axis=1)
    return sums * inverse, inverse


def attend_backward(queries, key_rows, values, attended, inverse, grad_attended):
    width = queries.shape[1]
    depth = width // HEADS
    own, after = head_masks(width)
    scaled = (grad_attended * inverse).astype(bf16)
    product = scaled.astype(f32) * attended
    high = product.astype(bf16)
    low = (product - high.astype(f32)).astype(bf16)
    groups = lax.broadcasted_iota(jnp.int32, (width, width), 0) // depth
    same_head = groups == lax.broadcasted_iota(jnp.int32, (width, width), 1) // depth
    group_ones = jnp.where(same_head, 1.0, 0.0).astype(bf16)
    column_sum = pltpu.roll(dot(high, group_ones) + dot(low, group_ones), depth, 1)
    column_high = column_sum.astype(bf16)
    column_low = (column_sum - column_high.astype(f32)).astype(bf16)
    lane = lax.broadcasted_iota(jnp.int32, (BALL, width), 1) % depth
    carried = jnp.where(lane == 0, column_high, masked(column_low, lane == 1))
    grad_queries = jnp.zeros((BALL, width), f32)
    grad_keys = jnp.zeros((BALL, width), f32)
    grad_values = jnp.zeros((BALL, width), f32)
    for start in range(0, HEADS, JOINED):
        weight_parts, score_parts, scaled_parts, query_parts, key_parts = [], [], [], [], []
        for head in range(start, start + JOINED):
            own_keys = masked(key_rows, own[head])
            left = jnp.where(own[head], scaled, masked(carried, after[head]))
            right = jnp.where(after[head], -jnp.ones_like(values), values)
            weights = jnp.exp2(dot(own_keys, queries, 1, 1))
            score_parts.append((weights * dot(right, left, 1, 1)).astype(bf16))
            weight_parts.append(weights.astype(bf16))
            scaled_parts.append(masked(scaled, own[head]))
            query_parts.append(masked(queries, own[head]))
            key_parts.append(own_keys)
        grad_values += dot(
            jnp.concatenate(weight_parts, axis=1), jnp.concatenate(scaled_parts, axis=0)
        )
        grad_keys += dot(
            jnp.concatenate(score_parts, axis=1), jnp.concatenate(query_parts, axis=0)
        )
        grad_queries += dot(
            jnp.concatenate(score_parts, axis=0), jnp.concatenate(key_parts, axis=0), 0, 0
        )
    return grad_queries, grad_keys * (1.0 / LOG2E), grad_values


def ball_slices(rows):
    return [slice(start, start + BALL) for start in range(0, rows, BALL)]


def block_backward(kept, rounded, attended, inverse, grad_rows, inward, outward):
    widened, row_scale, normed, query_unit, query_scale, key_unit, key_scale = kept
    width = widened.shape[1]
    grad_attended = dot(grad_rows, outward, 1, 1)
    parts = [
        attend_backward(
            *(array[ball] for array in rounded),
            attended[ball].astype(f32),
            inverse[ball],
            grad_attended[ball],
        )
        for ball in ball_slices(widened.shape[0])
    ]
    grad_queries, grad_keys, grad_values = (jnp.concatenate(p, axis=0) for p in zip(*parts))
    grad_queries = grad_queries * (width // HEADS) ** (-0.5)
    grad_qraw = query_scale * (
        grad_queries - query_unit * jnp.mean(grad_queries * query_unit, axis=-1, keepdims=True)
    )
    grad_kraw = key_scale * (
        grad_keys - key_unit * jnp.mean(grad_keys * key_unit, axis=-1, keepdims=True)
    )
    grad_mixture = jnp.concatenate([grad_qraw, grad_kraw, grad_values], axis=1).astype(bf16)
    grad_outward = dot(attended.astype(bf16), grad_rows, 0, 0)
    grad_inward = dot(normed, grad_mixture, 0, 0)
    grad_normed = dot(grad_mixture, inward, 1, 1)
    unit_rows = widened * row_scale
    grad_input = grad_rows.astype(f32) + row_scale * (
        grad_normed - unit_rows * jnp.mean(grad_normed * unit_rows, axis=-1, keepdims=True)
    )
    return grad_input.astype(bf16), grad_inward, grad_outward


def pack(slot_row, rows):
    return dot(one_hot_rows(slot_row, SLOTS), rows).astype(bf16)


def put_packets(packed, packet_refs, sample):
    for hop in range(REACH):
        for member in range(GROUP):
            start = (hop * GROUP + member) * CAP
            packet_refs[hop][member, sample] = packed[start : start + CAP, :]


def pick_near(pick_row, home):
    return dot(one_hot_picks(spread_column(pick_row), 0, home.shape[0]), home)


def pick_far(pick_row, home_rows, landed):
    return dot(one_hot_picks(spread_column(pick_row), home_rows, SLOTS), landed)


def flat(refs):
    parts = [ref[0, 0] for ref in refs[:REACH]]
    parts += [ref[hop, 0] for ref in refs[REACH:] for hop in range(REACH)]
    return jnp.concatenate(parts, axis=0)


def add_up(total_ref, term):
    first = pl.program_id(0) == 0

    @pl.when(first)
    def _():
        total_ref[...] = term

    @pl.when(jnp.logical_not(first))
    def _():
        total_ref[...] += term


def join_grads(total_ref, inward_grad, outward_grad):
    width = outward_grad.shape[0]
    for third in range(3):
        part = inward_grad[:, third * width : (third + 1) * width]
        total_ref[third * width : (third + 1) * width, :] = part.astype(bf16)
    total_ref[3 * width : 4 * width, :] = outward_grad.astype(bf16)


def add_grads(total_ref, sum_refs, grads, other_ref=None):
    for sum_ref, grad in zip(sum_refs, grads):
        add_up(sum_ref, grad)

    @pl.when(pl.program_id(0) == pl.num_programs(0) - 1)
    def _():
        join_grads(total_ref, *(ref[...] for ref in sum_refs))
        if other_ref is not None:
            total_ref[other_ref.shape[0] :, :] = other_ref[...]


def forward_kernel(nodes_ref, inward_ref, outward_ref, meta_ref, *refs, sample):
    earlier = (REACH + 3) * min(sample, 1)
    earlier_refs = refs[:earlier][3:]
    after_ref, attended_ref, inverse_ref, *packet_refs = refs[earlier:]
    kept, rounded = project(nodes_ref[0], inward_ref[...])
    parts = [attend(*(a[ball] for a in rounded)) for ball in ball_slices(nodes_ref.shape[1])]
    attended, inverse = (jnp.concatenate(p, axis=0) for p in zip(*parts))
    attended = attended.astype(bf16)
    attended_ref[0] = attended
    inverse_ref[0] = inverse
    result = (kept[0] + dot(attended, outward_ref[...])).astype(bf16)
    after_ref[0] = result
    put_packets(pack(meta_ref[sample : sample + 1, :], result), packet_refs, sample)
    for earlier_ref, packet_ref in zip(earlier_refs, packet_refs):
        packet_ref[:, :sample] = earlier_ref[:, :sample]


def sample_row(meta_ref, kind):
    samples = meta_ref.shape[0] // 2
    return meta_ref[pl.ds(kind * samples + pl.program_id(0), 1), :]


def near_cot_kernel(meta_ref, after_ref, cot_ref, *refs):
    near_ref, rotated_cot_ref = refs[LANDED:]
    width = after_ref.shape[2]
    row = sample_row(meta_ref, 1)
    home = jnp.concatenate([after_ref[0], cot_ref[0]], axis=1)
    near = pick_near(row, home)
    near_ref[0] = near[:, :width].astype(bf16)
    far = pick_far(row, home.shape[0], flat(refs[:LANDED]))
    rotated_cot_ref[0] = (near[:, width:] + far).astype(bf16)


def near_kernel(meta_ref, home_ref, near_ref):
    near_ref[0] = pick_near(sample_row(meta_ref, 1), home_ref[0]).astype(bf16)


def second_kernel(meta_ref, near_ref, cot_ref, inward_ref, outward_ref, *refs):
    arrived_refs, refs = refs[:LANDED], refs[LANDED:]
    grad_ref, total_ref, *packet_refs = refs[: 2 + REACH]
    far = pick_far(sample_row(meta_ref, 1), near_ref.shape[1], flat(arrived_refs))
    rotated = (near_ref[0].astype(f32) + far).astype(bf16)
    kept, rounded = project(rotated, inward_ref[...])
    parts = [attend(*(a[ball] for a in rounded)) for ball in ball_slices(rotated.shape[0])]
    attended, inverse = (jnp.concatenate(p, axis=0) for p in zip(*parts))
    grad_input, *grads = block_backward(
        kept, rounded, attended, inverse, cot_ref[0], inward_ref[...], outward_ref[...]
    )
    grad_ref[0] = grad_input
    add_grads(total_ref, refs[2 + REACH :], grads)
    put_packets(pack(sample_row(meta_ref, 0), grad_input), packet_refs, 0)


def first_kernel(
    meta_ref, nodes_ref, near_ref, attended_ref, inverse_ref, inward_ref, outward_ref, *refs
):
    returned_refs, refs = refs[:LANDED], refs[LANDED:]
    other_ref, grad_ref, total_ref, *sum_refs = refs
    far = pick_far(sample_row(meta_ref, 1), near_ref.shape[1], flat(returned_refs))
    grad_after = (near_ref[0].astype(f32) + far).astype(bf16)
    kept, rounded = project(nodes_ref[0], inward_ref[...])
    grad_input, *grads = block_backward(
        kept,
        rounded,
        attended_ref[0],
        inverse_ref[0],
        grad_after,
        inward_ref[...],
        outward_ref[...],
    )
    grad_ref[0] = grad_input
    add_grads(total_ref, sum_refs, grads, other_ref)


def split_kernel(whole_ref, *refs):
    width = refs[1].shape[0]
    for place, (inward_ref, outward_ref) in enumerate((refs[:2], refs[2:])):
        start = place * 4 * width
        for third in range(3):
            part = whole_ref[start + third * width : start + (third + 1) * width, :]
            inward_ref[:, third * width : (third + 1) * width] = part.astype(f32)
        outward_ref[...] = whole_ref[start + 3 * width : start + 4 * width, :].astype(f32)


def full_spec(shape):
    return pl.BlockSpec(shape, lambda i: (0,) * len(shape))


def call(kernel, name, micros, in_specs, operands, outs, out_specs=None, steps=1, **options):
    specs = [
        full_spec(operand.shape) if spec is None else spec
        for spec, operand in zip(in_specs or [None] * len(operands), operands)
    ]
    return pl.pallas_call(
        kernel,
        name=name,
        grid=(steps,),
        in_specs=specs,
        out_specs=out_specs or [full_spec(out.shape) for out in outs],
        out_shape=outs,
        compiler_params=pltpu.CompilerParams(vmem_limit_bytes=VMEM_LIMIT),
        cost_estimate=pl.CostEstimate(
            flops=int(micros * 1.15e9), bytes_accessed=2**20, transcendentals=0
        ),
        **options,
    )(*operands)


def rotate(value, axis, steps):
    count = lax.axis_size(axis)
    pairs = [(source, (source + steps) % count) for source in range(count)]
    return lax.ppermute(value, axis, pairs)


def hop_stage(packets):
    return [p if hop == 0 else rotate(p, "pts", hop) for hop, p in zip(HOPS, packets)]


def restack(moved):
    return [
        jnp.concatenate([packet[member : member + 1] for packet in moved], axis=0)
        for member in range(1, GROUP)
    ]


def member_stage(moved, stacked):
    return moved + [rotate(s, "grp", 1 + place) for place, s in enumerate(stacked)]


def exchange(packets):
    moved = hop_stage(packets)
    return member_stage(moved, restack(moved))


def reduce_all(terms, factor):
    count = lax.axis_size(AXES)
    pieces = terms.reshape(count, -1, terms.shape[1])
    mine = lax.all_to_all(pieces, AXES, 0, 0, tiled=True)
    total = (jnp.sum(mine.astype(f32), axis=0) * factor).astype(bf16)
    spread = jnp.broadcast_to(total[None], pieces.shape)
    return lax.all_to_all(spread, AXES, 0, 0, tiled=True).reshape(terms.shape)


def per_device(
    nodes,
    cotangent,
    first_inward,
    first_outward,
    second_inward,
    second_outward,
    rotated_source,
    rotated_index,
):
    samples, rows, width = nodes.shape
    shards = lax.axis_size(AXES)
    own = lax.axis_index(AXES).astype(jnp.int32).reshape(1)
    shape = jax.ShapeDtypeStruct
    smem = pl.BlockSpec(memory_space=pltpu.SMEM)
    rows_shape = shape(nodes.shape, bf16)
    packet_shapes = [shape((GROUP, samples, CAP, width), bf16)] * REACH
    meta_shape = shape((2 * samples, rows), jnp.int32)
    joined_shape = shape((4 * width, width), bf16)
    sums = [pltpu.VMEM((width, 3 * width), f32), pltpu.VMEM((width, width), f32)]
    first_weights = (first_inward, first_outward)
    second_weights = (second_inward, second_outward)
    by_sample = pl.BlockSpec((1, rows, width), lambda s: (s, 0, 0))
    packets_by_sample = pl.BlockSpec((GROUP, 1, CAP, width), lambda s: (0, s, 0, 0))
    landed_by_sample = [pl.BlockSpec((1, 1, CAP, width), lambda s: (0, s, 0, 0))] * REACH
    landed_by_sample += [pl.BlockSpec((REACH, 1, CAP, width), lambda s: (0, s, 0, 0))] * (GROUP - 1)
    send_meta, *cot_packets = call(
        functools.partial(send_kernel, shards=shards),
        "send_places",
        4,
        [smem, None, None],
        (own, rotated_index, cotangent),
        [meta_shape] + packet_shapes,
    )
    cot_moved = hop_stage(cot_packets)
    forward = []
    for sample in range(samples):
        one = pl.BlockSpec((1, rows, width), lambda i, sample=sample: (sample, 0, 0))
        meta = send_meta
        if sample > 0:
            cot_stacked, meta = lax.optimization_barrier((restack(cot_moved), meta))
            cot_arrived = member_stage(cot_moved, cot_stacked)
        forward = call(
            functools.partial(forward_kernel, sample=sample),
            f"forward_s{sample}",
            6,
            [one, None, None, None]
            + ([pl.BlockSpec(memory_space=pl.ANY)] * 3 + [None] * REACH if forward else []),
            (nodes, *first_weights, meta, *forward),
            [rows_shape, rows_shape, shape(nodes.shape, f32)] + packet_shapes,
            [one] * 3 + [full_spec(p.shape) for p in packet_shapes],
            input_output_aliases={4: 0, 5: 1, 6: 2} if forward else {},
        )
    after_first, attended, inverse, *packets = forward
    packets, cot_arrived = lax.optimization_barrier((packets, cot_arrived))
    arrived = exchange(packets)
    (receive_meta,) = call(
        functools.partial(receive_kernel, shards=shards),
        "receive_places",
        2,
        [smem, None],
        (own, rotated_source),
        [meta_shape],
    )
    near, rotated_cot = call(
        near_cot_kernel,
        "near_cot",
        6,
        [None, by_sample, by_sample] + landed_by_sample,
        (receive_meta, after_first, cotangent, *cot_arrived),
        [rows_shape] * 2,
        [by_sample] * 2,
        samples,
    )
    rotated_grad, second_joined, *back_packets = call(
        second_kernel,
        "second",
        36,
        [None, by_sample, by_sample, None, None] + landed_by_sample,
        (receive_meta, near, rotated_cot, *second_weights, *arrived),
        [rows_shape, joined_shape] + packet_shapes,
        [by_sample, full_spec(joined_shape.shape)] + [packets_by_sample] * REACH,
        samples,
        scratch_shapes=sums,
    )
    returned = exchange(back_packets)
    (grad_near,) = call(
        near_kernel,
        "near_grad",
        3,
        [None, by_sample],
        (send_meta, rotated_grad),
        [rows_shape],
        [by_sample],
        samples,
    )
    both_shape = shape((8 * width, width), bf16)
    input_grad, joined = call(
        first_kernel,
        "first",
        30,
        [None] + [by_sample] * 4 + [None, None] + landed_by_sample + [None],
        (
            send_meta,
            nodes,
            grad_near,
            attended,
            inverse,
            *first_weights,
            *returned,
            second_joined,
        ),
        [rows_shape, both_shape],
        [by_sample, full_spec(both_shape.shape)],
        samples,
        scratch_shapes=sums,
    )
    factor = 1.0 / math.sqrt(samples * rows * shards)
    grad_shapes = [shape((width, 3 * width), f32), shape((width, width), f32)]
    grads = call(split_kernel, "split", 2, None, (reduce_all(joined, factor),), grad_shapes * 2)
    return (input_grad, *grads)


def solution(mesh):
    in_specs = (
        P(None, AXES, None),
        P(None, AXES, None),
        P(),
        P(),
        P(),
        P(),
        P(None, AXES),
        P(None, AXES),
    )
    out_specs = (P(None, AXES, None), P(), P(), P(), P())
    return jax.shard_map(
        per_device, mesh=mesh, in_specs=in_specs, out_specs=out_specs, check_vma=False
    )
```

```python
import functools
import math

import jax
import jax.numpy as jnp
from jax import lax
from jax.experimental import pallas as pl
from jax.experimental.pallas import tpu as pltpu
from jax.sharding import PartitionSpec as P

HEADS = 8
BALL = 256
SPAN = 8
CAP = 32
EPSILON = 1e-06
AXES = ("pts", "grp")
GROUP = 4
HOPS = tuple(range(-(SPAN // GROUP), SPAN // GROUP + 1))
REACH = len(HOPS)
SLOTS = REACH * GROUP * CAP
LANDED = REACH + GROUP - 1
VMEM_LIMIT = 28 * 1024 * 1024

f32 = jnp.float32
bf16 = jnp.bfloat16


def dot(left, right, left_dim=1, right_dim=0):
    return lax.dot_general(
        left, right, (((left_dim,), (right_dim,)), ((), ())), preferred_element_type=f32
    )


def spread_column(row):
    return jnp.transpose(jnp.broadcast_to(row.astype(f32), (128, row.shape[1])))


def one_hot_rows(slot_row, slots):
    ids = lax.broadcasted_iota(jnp.int32, (slots, slot_row.shape[1]), 0)
    return jnp.where(ids == slot_row, 1.0, 0.0).astype(bf16)


def one_hot_picks(pick_column, start, width):
    lanes = lax.broadcasted_iota(jnp.int32, pick_column.shape, 1).astype(f32)
    pieces = [
        jnp.where(pick_column == lanes + float(start + 128 * piece), 1.0, 0.0).astype(bf16)
        for piece in range(width // 128)
    ]
    return jnp.concatenate(pieces, axis=1)


def same_before(column, row, row_ids, lane_ids):
    counts = []
    for piece in range(row.shape[1] // 128):
        lanes = slice(128 * piece, 128 * piece + 128)
        same = (column == row[:, lanes]) & (row_ids < lane_ids + float(128 * piece))
        counts.append(jnp.sum(jnp.where(same, 1.0, 0.0), axis=0, keepdims=True))
    return jnp.concatenate(counts, axis=1).astype(jnp.int32)


def count_between(column, floor_row, row):
    counts = []
    for piece in range(row.shape[1] // 128):
        lanes = slice(128 * piece, 128 * piece + 128)
        inside = (column >= floor_row[:, lanes]) & (column < row[:, lanes])
        counts.append(jnp.sum(jnp.where(inside, 1.0, 0.0), axis=0, keepdims=True))
    return jnp.concatenate(counts, axis=1).astype(jnp.int32)


def slots_of(shard, own, rank, shards):
    member = (shard - own) & (GROUP - 1)
    hop = ((shard // GROUP) - (own // GROUP) + REACH // 2) & (shards // GROUP - 1)
    leave = (hop * GROUP + member) * CAP + rank
    land = (((-member) & (GROUP - 1)) * REACH + (REACH - 1 - hop)) * CAP + rank
    return leave, land


def send_kernel(own_ref, index_ref, meta_ref, *, shards):
    samples, rows = index_ref.shape
    own = own_ref[0]
    row_ids = lax.broadcasted_iota(jnp.int32, (rows, 128), 0).astype(f32)
    lane_ids = lax.broadcasted_iota(jnp.int32, (rows, 128), 1).astype(f32)
    for sample in range(samples):
        index = index_ref[sample : sample + 1, :]
        shard = index // rows
        rank = same_before(spread_column(shard), shard.astype(f32), row_ids, lane_ids)
        leave, land = slots_of(shard, own, rank, shards)
        meta_ref[sample : sample + 1, :] = jnp.where(shard == own, -1, leave)
        meta_ref[samples + sample : samples + sample + 1, :] = jnp.where(
            shard == own, index - own * rows, rows + land
        )


def receive_kernel(own_ref, source_ref, meta_ref, *, shards):
    samples, rows = source_ref.shape
    own = own_ref[0]
    for sample in range(samples):
        source = source_ref[sample : sample + 1, :]
        shard = source // rows
        floor_row = (shard * rows).astype(f32)
        rank = count_between(spread_column(source), floor_row, source.astype(f32))
        leave, land = slots_of(shard, own, rank, shards)
        meta_ref[sample : sample + 1, :] = jnp.where(shard == own, -1, leave)
        meta_ref[samples + sample : samples + sample + 1, :] = jnp.where(
            shard == own, source - own * rows, rows + land
        )


LOG2E = 1.4426950408889634
JOINED = 4


def masked(array, mask):
    return jnp.where(mask, array, jnp.zeros_like(array))


def head_masks(width):
    heads = lax.broadcasted_iota(jnp.int32, (BALL, width), 1) // (width // HEADS)
    own = [heads == head for head in range(HEADS)]
    return own, own[1:] + own[:1]


def norm(rows):
    widened = rows.astype(f32)
    row_scale = lax.rsqrt(jnp.mean(widened * widened, axis=-1, keepdims=True) + EPSILON)
    return widened, row_scale, (widened * row_scale).astype(bf16)


def score_factor(width):
    return LOG2E * (width // HEADS) ** (-0.5)


def project(normed, inward):
    width = normed.shape[1]
    mixture = dot(normed, inward)
    query_raw = mixture[:, :width]
    key_raw = mixture[:, width : 2 * width]
    query_scale = lax.rsqrt(jnp.mean(query_raw * query_raw, axis=-1, keepdims=True) + EPSILON)
    key_scale = lax.rsqrt(jnp.mean(key_raw * key_raw, axis=-1, keepdims=True) + EPSILON)
    query_unit = query_raw * query_scale
    key_unit = key_raw * key_scale
    rounded = (
        (query_unit * score_factor(width)).astype(bf16),
        key_unit.astype(bf16),
        mixture[:, 2 * width :].astype(bf16),
    )
    return (query_unit, query_scale, key_unit, key_scale), rounded


def key_weights(own_keys, queries):
    return jnp.exp2(dot(own_keys, queries, 1, 1))


def attend(queries, key_rows, values):
    width = queries.shape[1]
    half = width // 2
    own, _ = head_masks(width)
    results = []
    for start in range(0, HEADS, HEADS // 2):
        weights = []
        rights = []
        for head in range(start, start + HEADS // 2):
            scores = dot(masked(queries, own[head]), key_rows, 1, 1)
            weights.append(jnp.exp2(scores).astype(bf16))
            opposite = own[(head + HEADS // 2) % HEADS]
            ones = jnp.where(opposite, jnp.ones_like(values), jnp.zeros_like(values))
            rights.append(jnp.where(own[head], values, ones))
        results.append(dot(jnp.concatenate(weights, axis=1), jnp.concatenate(rights, axis=0)))
    low, high = results
    sums = jnp.concatenate([low[:, :half], high[:, half:]], axis=1)
    inverse = 1.0 / jnp.concatenate([low[:, half:], high[:, :half]], axis=1)
    return sums * inverse, inverse


def attend_backward(
    queries, key_rows, values, attended, inverse, grad_attended, kept_weights=None
):
    width = queries.shape[1]
    depth = width // HEADS
    own, after = head_masks(width)
    scaled = (grad_attended * inverse).astype(bf16)
    product = scaled.astype(f32) * attended
    high = product.astype(bf16)
    low = (product - high.astype(f32)).astype(bf16)
    groups = lax.broadcasted_iota(jnp.int32, (width, width), 0) // depth
    same_head = groups == lax.broadcasted_iota(jnp.int32, (width, width), 1) // depth
    group_ones = jnp.where(same_head, 1.0, 0.0).astype(bf16)
    column_sum = pltpu.roll(dot(high, group_ones) + dot(low, group_ones), depth, 1)
    column_high = column_sum.astype(bf16)
    column_low = (column_sum - column_high.astype(f32)).astype(bf16)
    lane = lax.broadcasted_iota(jnp.int32, (BALL, width), 1) % depth
    carried = jnp.where(lane == 0, column_high, masked(column_low, lane == 1))
    grad_queries = jnp.zeros((BALL, width), f32)
    grad_keys = jnp.zeros((BALL, width), f32)
    grad_values = jnp.zeros((BALL, width), f32)
    for start in range(0, HEADS, JOINED):
        weight_parts, score_parts, scaled_parts, query_parts, key_parts = [], [], [], [], []
        for head in range(start, start + JOINED):
            own_keys = masked(key_rows, own[head])
            left = jnp.where(own[head], scaled, masked(carried, after[head]))
            right = jnp.where(after[head], -jnp.ones_like(values), values)
            if kept_weights is None:
                weights = key_weights(own_keys, queries)
            else:
                weights = kept_weights[head * BALL : (head + 1) * BALL, :].astype(f32)
            score_parts.append((weights * dot(right, left, 1, 1)).astype(bf16))
            weight_parts.append(weights.astype(bf16))
            scaled_parts.append(masked(scaled, own[head]))
            query_parts.append(masked(queries, own[head]))
            key_parts.append(own_keys)
        grad_values += dot(
            jnp.concatenate(weight_parts, axis=1), jnp.concatenate(scaled_parts, axis=0)
        )
        grad_keys += dot(
            jnp.concatenate(score_parts, axis=1), jnp.concatenate(query_parts, axis=0)
        )
        grad_queries += dot(
            jnp.concatenate(score_parts, axis=0), jnp.concatenate(key_parts, axis=0), 0, 0
        )
    return grad_queries, grad_keys * (1.0 / LOG2E), grad_values


def ball_slices(rows):
    return [slice(start, start + BALL) for start in range(0, rows, BALL)]


def block_backward(
    kept, rounded, attended, inverse, grad_rows, inward, outward, weights_ref=None
):
    widened, row_scale, normed, query_unit, query_scale, key_unit, key_scale = kept
    width = widened.shape[1]
    grad_attended = dot(grad_rows, outward, 1, 1)
    parts = []
    for place, ball in enumerate(ball_slices(widened.shape[0])):
        kept_weights = None
        if weights_ref is not None:
            kept_weights = weights_ref[0, place * HEADS * BALL : (place + 1) * HEADS * BALL, :]
        parts.append(
            attend_backward(
                *(array[ball] for array in rounded),
                attended[ball].astype(f32),
                inverse[ball],
                grad_attended[ball],
                kept_weights,
            )
        )
    grad_queries, grad_keys, grad_values = (jnp.concatenate(p, axis=0) for p in zip(*parts))
    grad_queries = grad_queries * (width // HEADS) ** (-0.5)
    grad_qraw = query_scale * (
        grad_queries - query_unit * jnp.mean(grad_queries * query_unit, axis=-1, keepdims=True)
    )
    grad_kraw = key_scale * (
        grad_keys - key_unit * jnp.mean(grad_keys * key_unit, axis=-1, keepdims=True)
    )
    grad_mixture = jnp.concatenate([grad_qraw, grad_kraw, grad_values], axis=1).astype(bf16)
    grad_outward = dot(attended.astype(bf16), grad_rows, 0, 0)
    grad_inward = dot(normed, grad_mixture, 0, 0)
    grad_normed = dot(grad_mixture, inward, 1, 1)
    unit_rows = widened * row_scale
    grad_input = grad_rows.astype(f32) + row_scale * (
        grad_normed - unit_rows * jnp.mean(grad_normed * unit_rows, axis=-1, keepdims=True)
    )
    return grad_input.astype(bf16), grad_inward, grad_outward


def pack(slot_row, rows):
    return dot(one_hot_rows(slot_row, SLOTS), rows).astype(bf16)


def put_packets(packed, packet_refs):
    kinds, width = packet_refs[0].shape[2], packet_refs[0].shape[4]
    for hop in range(REACH):
        for member in range(GROUP):
            start = (hop * GROUP + member) * CAP
            for kind in range(kinds):
                part = packed[start : start + CAP, kind * width : (kind + 1) * width]
                packet_refs[hop][member, 0, kind] = part


def pick_near(pick_row, home):
    return dot(one_hot_picks(spread_column(pick_row), 0, home.shape[0]), home)


def flat(refs):
    parts = [(ref, 0) for ref in refs[:REACH]]
    parts += [(ref, hop) for ref in refs[REACH:] for hop in range(REACH)]
    kinds = refs[0].shape[2]
    return [jnp.concatenate([ref[hop, 0, k] for ref, hop in parts], axis=0) for k in range(kinds)]


def add_up(total_ref, term):
    first = pl.program_id(0) == 0

    @pl.when(first)
    def _():
        total_ref[...] = term

    @pl.when(jnp.logical_not(first))
    def _():
        total_ref[...] += term


def join_grads(total_ref, inward_grad, outward_grad):
    width = outward_grad.shape[0]
    for third in range(3):
        part = inward_grad[:, third * width : (third + 1) * width]
        total_ref[third * width : (third + 1) * width, :] = part.astype(bf16)
    total_ref[3 * width : 4 * width, :] = outward_grad.astype(bf16)


def add_grads(total_ref, sum_refs, grads, other_ref=None):
    for sum_ref, grad in zip(sum_refs, grads):
        add_up(sum_ref, grad)

    @pl.when(pl.program_id(0) == pl.num_programs(0) - 1)
    def _():
        join_grads(total_ref, *(ref[...] for ref in sum_refs))
        if other_ref is not None:
            total_ref[other_ref.shape[0] :, :] = other_ref[...]


def sample_row(meta_ref, kind):
    samples = meta_ref.shape[0] // 2
    return meta_ref[pl.ds(kind * samples + pl.program_id(0), 1), :]


def attend_balls(rounded):
    rows = rounded[0].shape[0]
    parts = [attend(*(array[ball] for array in rounded)) for ball in ball_slices(rows)]
    attended, inverse = (jnp.concatenate(part, axis=0) for part in zip(*parts))
    return attended, inverse


def forward_kernel(nodes_ref, cot_ref, inward_ref, outward_ref, meta_ref, *refs):
    after_ref, attended_ref, inverse_ref, rounded_ref, scales_ref, *packet_refs = refs
    width = nodes_ref.shape[2]
    widened, _, normed = norm(nodes_ref[0])
    (_, query_scale, _, key_scale), rounded = project(normed, inward_ref[...])
    attended, inverse = attend_balls(rounded)
    attended = attended.astype(bf16)
    attended_ref[0] = attended
    inverse_ref[0] = inverse
    for place, array in enumerate(rounded):
        rounded_ref[0, :, place * width : (place + 1) * width] = array
    lane = lax.broadcasted_iota(jnp.int32, scales_ref.shape[1:], 1)
    scales_ref[0] = jnp.where(lane == 0, query_scale, key_scale)
    result = (widened + dot(attended, outward_ref[...])).astype(bf16)
    after_ref[0] = result
    both = jnp.concatenate([result, cot_ref[0]], axis=1)
    put_packets(pack(sample_row(meta_ref, 0), both), packet_refs)


def weights_kernel(rounded_ref, weights_ref):
    width = rounded_ref.shape[2] // 3
    own, _ = head_masks(width)
    for place, ball in enumerate(ball_slices(rounded_ref.shape[1])):
        queries = rounded_ref[0, ball, :width]
        key_rows = rounded_ref[0, ball, width : 2 * width]
        for head in range(HEADS):
            start = (place * HEADS + head) * BALL
            weights = key_weights(masked(key_rows, own[head]), queries)
            weights_ref[0, start : start + BALL, :] = weights.astype(bf16)


def near_both_kernel(meta_ref, after_ref, cot_ref, near_ref):
    home = jnp.concatenate([after_ref[0], cot_ref[0]], axis=1)
    near_ref[0] = pick_near(sample_row(meta_ref, 1), home).astype(bf16)


def near_kernel(meta_ref, home_ref, near_ref):
    near_ref[0] = pick_near(sample_row(meta_ref, 1), home_ref[0]).astype(bf16)


def add_far(meta_ref, near_ref, landed_refs):
    hits = one_hot_picks(spread_column(sample_row(meta_ref, 1)), near_ref.shape[1], SLOTS)
    rows = []
    for kind, landed in enumerate(flat(landed_refs)):
        width = landed.shape[1]
        near = near_ref[0, :, kind * width : (kind + 1) * width]
        rows.append((near.astype(f32) + dot(hits, landed)).astype(bf16))
    return rows


def second_kernel(meta_ref, near_ref, inward_ref, outward_ref, *refs):
    arrived_refs, refs = refs[:LANDED], refs[LANDED:]
    grad_ref, total_ref, *packet_refs = refs[: 2 + REACH]
    *sum_refs, rotated_ref, rotated_cot_ref = refs[2 + REACH :]

    @pl.when(pl.program_id(0) >= 0)
    def _():
        rotated_ref[...], rotated_cot_ref[...] = add_far(meta_ref, near_ref, arrived_refs)

    kept = norm(rotated_ref[...])
    units, rounded = project(kept[2], inward_ref[...])
    attended, inverse = attend_balls(rounded)
    grad_input, *grads = block_backward(
        kept + units,
        rounded,
        attended,
        inverse,
        rotated_cot_ref[...],
        inward_ref[...],
        outward_ref[...],
    )
    grad_ref[0] = grad_input
    add_grads(total_ref, sum_refs, grads)
    put_packets(pack(sample_row(meta_ref, 0), grad_input), packet_refs)


def first_kernel(
    meta_ref,
    nodes_ref,
    near_ref,
    attended_ref,
    inverse_ref,
    rounded_ref,
    scales_ref,
    weights_ref,
    inward_ref,
    outward_ref,
    *refs,
):
    returned_refs, refs = refs[:LANDED], refs[LANDED:]
    other_ref, grad_ref, total_ref, *sum_refs = refs
    (grad_after,) = add_far(meta_ref, near_ref, returned_refs)
    width = nodes_ref.shape[2]
    rounded = [rounded_ref[0, :, place * width : (place + 1) * width] for place in range(3)]
    query_unit = rounded[0].astype(f32) * (1.0 / score_factor(width))
    key_unit = rounded[1].astype(f32)
    units = (query_unit, scales_ref[0, :, 0:1], key_unit, scales_ref[0, :, 1:2])
    grad_input, *grads = block_backward(
        norm(nodes_ref[0]) + units,
        rounded,
        attended_ref[0],
        inverse_ref[0],
        grad_after,
        inward_ref[...],
        outward_ref[...],
        weights_ref,
    )
    grad_ref[0] = grad_input
    add_grads(total_ref, sum_refs, grads, other_ref)


def split_kernel(whole_ref, *refs):
    width = refs[1].shape[0]
    for place, (inward_ref, outward_ref) in enumerate((refs[:2], refs[2:])):
        start = place * 4 * width
        for third in range(3):
            part = whole_ref[start + third * width : start + (third + 1) * width, :]
            inward_ref[:, third * width : (third + 1) * width] = part.astype(f32)
        outward_ref[...] = whole_ref[start + 3 * width : start + 4 * width, :].astype(f32)


def full_spec(shape):
    return pl.BlockSpec(shape, lambda i: (0,) * len(shape))


def call(kernel, name, micros, in_specs, operands, outs, out_specs=None, steps=1, **options):
    specs = [
        full_spec(operand.shape) if spec is None else spec
        for spec, operand in zip(in_specs or [None] * len(operands), operands)
    ]
    return pl.pallas_call(
        kernel,
        name=name,
        grid=(steps,),
        in_specs=specs,
        out_specs=out_specs or [full_spec(out.shape) for out in outs],
        out_shape=outs,
        compiler_params=pltpu.CompilerParams(vmem_limit_bytes=VMEM_LIMIT),
        cost_estimate=pl.CostEstimate(
            flops=int(micros * 1.15e9), bytes_accessed=2**20, transcendentals=0
        ),
        **options,
    )(*operands)


def rotate(value, axis, steps):
    count = lax.axis_size(axis)
    pairs = [(source, (source + steps) % count) for source in range(count)]
    return lax.ppermute(value, axis, pairs)


def hop_stage(packets):
    return [p if hop == 0 else rotate(p, "pts", hop) for hop, p in zip(HOPS, packets)]


def restack(moved):
    return [
        jnp.concatenate([packet[member : member + 1] for packet in moved], axis=0)
        for member in range(1, GROUP)
    ]


def member_stage(moved, stacked):
    return moved + [rotate(s, "grp", 1 + place) for place, s in enumerate(stacked)]


def exchange(packets):
    moved = hop_stage(packets)
    return member_stage(moved, restack(moved))


def reduce_all(terms, factor):
    count = lax.axis_size(AXES)
    pieces = terms.reshape(count, -1, terms.shape[1])
    mine = lax.all_to_all(pieces, AXES, 0, 0, tiled=True)
    total = (jnp.sum(mine.astype(f32), axis=0) * factor).astype(bf16)
    spread = jnp.broadcast_to(total[None], pieces.shape)
    return lax.all_to_all(spread, AXES, 0, 0, tiled=True).reshape(terms.shape)


def per_device(
    nodes,
    cotangent,
    first_inward,
    first_outward,
    second_inward,
    second_outward,
    rotated_source,
    rotated_index,
):
    samples, rows, width = nodes.shape
    shards = lax.axis_size(AXES)
    own = lax.axis_index(AXES).astype(jnp.int32).reshape(1)
    shape = jax.ShapeDtypeStruct
    smem = pl.BlockSpec(memory_space=pltpu.SMEM)
    rows_shape = shape(nodes.shape, bf16)
    meta_shape = shape((2 * samples, rows), jnp.int32)
    joined_shape = shape((4 * width, width), bf16)
    both_shape = shape((8 * width, width), bf16)
    sums = [pltpu.VMEM((width, 3 * width), f32), pltpu.VMEM((width, width), f32)]
    first_weights = (first_inward, first_outward)
    second_weights = (second_inward, second_outward)

    def by_sample(*dims):
        return pl.BlockSpec((1, *dims), lambda s: (s, *(0 for _ in dims)))

    def packets(kinds):
        return [shape((GROUP, samples, kinds, CAP, width), bf16)] * REACH

    def packets_by_sample(kinds):
        return [pl.BlockSpec((GROUP, 1, kinds, CAP, width), lambda s: (0, s, 0, 0, 0))] * REACH

    def landed_by_sample(kinds):
        one = pl.BlockSpec((1, 1, kinds, CAP, width), lambda s: (0, s, 0, 0, 0))
        hops = pl.BlockSpec((REACH, 1, kinds, CAP, width), lambda s: (0, s, 0, 0, 0))
        return [one] * REACH + [hops] * (GROUP - 1)

    rows_spec = by_sample(rows, width)
    (send_meta,) = call(
        functools.partial(send_kernel, shards=shards),
        "send_places",
        2,
        [smem, None],
        (own, rotated_index),
        [meta_shape],
    )
    after_first, attended, inverse, rounded, scales, *out_packets = call(
        forward_kernel,
        "forward",
        9,
        [rows_spec, rows_spec, None, None, None],
        (nodes, cotangent, *first_weights, send_meta),
        [
            rows_shape,
            rows_shape,
            shape(nodes.shape, f32),
            shape((samples, rows, 3 * width), bf16),
            shape((samples, rows, 128), f32),
        ]
        + packets(2),
        [rows_spec] * 3
        + [by_sample(rows, 3 * width), by_sample(rows, 128)]
        + packets_by_sample(2),
        samples,
    )
    arrived = exchange(out_packets)
    (receive_meta,) = call(
        functools.partial(receive_kernel, shards=shards),
        "receive_places",
        2,
        [smem, None],
        (own, rotated_source),
        [meta_shape],
    )
    (near,) = call(
        near_both_kernel,
        "near_out",
        3,
        [None, rows_spec, rows_spec],
        (receive_meta, after_first, cotangent),
        [shape((samples, rows, 2 * width), bf16)],
        [by_sample(rows, 2 * width)],
        samples,
    )
    weights_spec = by_sample(rows * HEADS, BALL)
    (weights,) = call(
        weights_kernel,
        "weights",
        6,
        [by_sample(rows, 3 * width)],
        (rounded,),
        [shape((samples, rows * HEADS, BALL), bf16)],
        [weights_spec],
        samples,
    )
    rotated_grad, second_joined, *back_packets = call(
        second_kernel,
        "second",
        26,
        [None, by_sample(rows, 2 * width), None, None] + landed_by_sample(2),
        (receive_meta, near, *second_weights, *arrived),
        [rows_shape, joined_shape] + packets(1),
        [rows_spec, full_spec(joined_shape.shape)] + packets_by_sample(1),
        samples,
        scratch_shapes=sums + [pltpu.VMEM((rows, width), bf16)] * 2,
    )
    returned = exchange(back_packets)
    (grad_near,) = call(
        near_kernel,
        "near_back",
        2,
        [None, rows_spec],
        (send_meta, rotated_grad),
        [rows_shape],
        [rows_spec],
        samples,
    )
    input_grad, joined = call(
        first_kernel,
        "first",
        16,
        [None]
        + [rows_spec] * 4
        + [by_sample(rows, 3 * width), by_sample(rows, 128), weights_spec, None, None]
        + landed_by_sample(1)
        + [None],
        (
            send_meta,
            nodes,
            grad_near,
            attended,
            inverse,
            rounded,
            scales,
            weights,
            *first_weights,
            *returned,
            second_joined,
        ),
        [rows_shape, both_shape],
        [rows_spec, full_spec(both_shape.shape)],
        samples,
        scratch_shapes=sums,
    )
    factor = 1.0 / math.sqrt(samples * rows * shards)
    grad_shapes = [shape((width, 3 * width), f32), shape((width, width), f32)]
    grads = call(split_kernel, "split", 2, None, (reduce_all(joined, factor),), grad_shapes * 2)
    return (input_grad, *grads)


def solution(mesh):
    in_specs = (
        P(None, AXES, None),
        P(None, AXES, None),
        P(),
        P(),
        P(),
        P(),
        P(None, AXES),
        P(None, AXES),
    )
    out_specs = (P(None, AXES, None), P(), P(), P(), P())
    return jax.shard_map(
        per_device, mesh=mesh, in_specs=in_specs, out_specs=out_specs, check_vma=False
    )
```

```python
import functools
import math

import jax
import jax.numpy as jnp
from jax import lax
from jax.experimental import pallas as pl
from jax.experimental.pallas import tpu as pltpu
from jax.sharding import PartitionSpec as P

HEADS = 8
BALL = 256
SPAN = 8
CAP = 32
EPSILON = 1e-06
AXES = ("pts", "grp")
GROUP = 4
HOPS = tuple(range(-(SPAN // GROUP), SPAN // GROUP + 1))
REACH = len(HOPS)
SLOTS = REACH * GROUP * CAP
LANDED = REACH + GROUP - 1
VMEM_LIMIT = 28 * 1024 * 1024

f32 = jnp.float32
bf16 = jnp.bfloat16


def dot(left, right, left_dim=1, right_dim=0):
    return lax.dot_general(
        left, right, (((left_dim,), (right_dim,)), ((), ())), preferred_element_type=f32
    )


def spread_column(row):
    return jnp.transpose(jnp.broadcast_to(row.astype(f32), (128, row.shape[1])))


def one_hot_rows(slot_row, slots):
    ids = lax.broadcasted_iota(jnp.int32, (slots, slot_row.shape[1]), 0)
    return jnp.where(ids == slot_row, 1.0, 0.0).astype(bf16)


def one_hot_picks(pick_column, start, width):
    lanes = lax.broadcasted_iota(jnp.int32, pick_column.shape, 1).astype(f32)
    pieces = [
        jnp.where(pick_column == lanes + float(start + 128 * piece), 1.0, 0.0).astype(bf16)
        for piece in range(width // 128)
    ]
    return jnp.concatenate(pieces, axis=1)


def same_before(column, row, row_ids, lane_ids):
    counts = []
    for piece in range(row.shape[1] // 128):
        lanes = slice(128 * piece, 128 * piece + 128)
        same = (column == row[:, lanes]) & (row_ids < lane_ids + float(128 * piece))
        counts.append(jnp.sum(jnp.where(same, 1.0, 0.0), axis=0, keepdims=True))
    return jnp.concatenate(counts, axis=1).astype(jnp.int32)


def count_between(column, floor_row, row):
    counts = []
    for piece in range(row.shape[1] // 128):
        lanes = slice(128 * piece, 128 * piece + 128)
        inside = (column >= floor_row[:, lanes]) & (column < row[:, lanes])
        counts.append(jnp.sum(jnp.where(inside, 1.0, 0.0), axis=0, keepdims=True))
    return jnp.concatenate(counts, axis=1).astype(jnp.int32)


def slots_of(shard, own, rank, shards):
    member = (shard - own) & (GROUP - 1)
    hop = ((shard // GROUP) - (own // GROUP) + REACH // 2) & (shards // GROUP - 1)
    leave = (hop * GROUP + member) * CAP + rank
    land = (((-member) & (GROUP - 1)) * REACH + (REACH - 1 - hop)) * CAP + rank
    return leave, land


def send_kernel(own_ref, index_ref, meta_ref, *, shards):
    samples, rows = index_ref.shape
    own = own_ref[0]
    row_ids = lax.broadcasted_iota(jnp.int32, (rows, 128), 0).astype(f32)
    lane_ids = lax.broadcasted_iota(jnp.int32, (rows, 128), 1).astype(f32)
    for sample in range(samples):
        index = index_ref[sample : sample + 1, :]
        shard = index // rows
        rank = same_before(spread_column(shard), shard.astype(f32), row_ids, lane_ids)
        leave, land = slots_of(shard, own, rank, shards)
        meta_ref[sample : sample + 1, :] = jnp.where(shard == own, -1, leave)
        meta_ref[samples + sample : samples + sample + 1, :] = jnp.where(
            shard == own, index - own * rows, rows + land
        )


def receive_kernel(own_ref, source_ref, meta_ref, *, shards):
    samples, rows = source_ref.shape
    own = own_ref[0]
    for sample in range(samples):
        source = source_ref[sample : sample + 1, :]
        shard = source // rows
        floor_row = (shard * rows).astype(f32)
        rank = count_between(spread_column(source), floor_row, source.astype(f32))
        leave, land = slots_of(shard, own, rank, shards)
        meta_ref[sample : sample + 1, :] = jnp.where(shard == own, -1, leave)
        meta_ref[samples + sample : samples + sample + 1, :] = jnp.where(
            shard == own, source - own * rows, rows + land
        )


LOG2E = 1.4426950408889634
JOINED = 4


def masked(array, mask):
    return jnp.where(mask, array, jnp.zeros_like(array))


def head_masks(width):
    heads = lax.broadcasted_iota(jnp.int32, (BALL, width), 1) // (width // HEADS)
    own = [heads == head for head in range(HEADS)]
    return own, own[1:] + own[:1]


def norm(rows):
    widened = rows.astype(f32)
    row_scale = lax.rsqrt(jnp.mean(widened * widened, axis=-1, keepdims=True) + EPSILON)
    return widened, row_scale, (widened * row_scale).astype(bf16)


def score_factor(width):
    return LOG2E * (width // HEADS) ** (-0.5)


def project(normed, inward):
    width = normed.shape[1]
    mixture = dot(normed, inward)
    query_raw = mixture[:, :width]
    key_raw = mixture[:, width : 2 * width]
    query_scale = lax.rsqrt(jnp.mean(query_raw * query_raw, axis=-1, keepdims=True) + EPSILON)
    key_scale = lax.rsqrt(jnp.mean(key_raw * key_raw, axis=-1, keepdims=True) + EPSILON)
    query_unit = query_raw * query_scale
    key_unit = key_raw * key_scale
    rounded = (
        (query_unit * score_factor(width)).astype(bf16),
        key_unit.astype(bf16),
        mixture[:, 2 * width :].astype(bf16),
    )
    return (query_unit, query_scale, key_unit, key_scale), rounded


def key_weights(own_keys, queries):
    return jnp.exp2(dot(own_keys, queries, 1, 1))


def attend(queries, key_rows, values):
    width = queries.shape[1]
    half = width // 2
    own, _ = head_masks(width)
    results = []
    for start in range(0, HEADS, HEADS // 2):
        weights = []
        rights = []
        for head in range(start, start + HEADS // 2):
            scores = dot(masked(queries, own[head]), key_rows, 1, 1)
            weights.append(jnp.exp2(scores).astype(bf16))
            opposite = own[(head + HEADS // 2) % HEADS]
            ones = jnp.where(opposite, jnp.ones_like(values), jnp.zeros_like(values))
            rights.append(jnp.where(own[head], values, ones))
        results.append(dot(jnp.concatenate(weights, axis=1), jnp.concatenate(rights, axis=0)))
    low, high = results
    sums = jnp.concatenate([low[:, :half], high[:, half:]], axis=1)
    inverse = 1.0 / jnp.concatenate([low[:, half:], high[:, :half]], axis=1)
    return sums * inverse, inverse


def attend_backward(
    queries, key_rows, values, attended, inverse, grad_attended, kept_weights=None
):
    width = queries.shape[1]
    depth = width // HEADS
    own, after = head_masks(width)
    scaled = (grad_attended * inverse).astype(bf16)
    product = scaled.astype(f32) * attended
    high = product.astype(bf16)
    low = (product - high.astype(f32)).astype(bf16)
    groups = lax.broadcasted_iota(jnp.int32, (width, width), 0) // depth
    same_head = groups == lax.broadcasted_iota(jnp.int32, (width, width), 1) // depth
    group_ones = jnp.where(same_head, 1.0, 0.0).astype(bf16)
    column_sum = pltpu.roll(dot(high, group_ones) + dot(low, group_ones), depth, 1)
    column_high = column_sum.astype(bf16)
    column_low = (column_sum - column_high.astype(f32)).astype(bf16)
    lane = lax.broadcasted_iota(jnp.int32, (BALL, width), 1) % depth
    carried = jnp.where(lane == 0, column_high, masked(column_low, lane == 1))
    grad_queries = jnp.zeros((BALL, width), f32)
    grad_keys = jnp.zeros((BALL, width), f32)
    grad_values = jnp.zeros((BALL, width), f32)
    for start in range(0, HEADS, JOINED):
        weight_parts, score_parts, scaled_parts, query_parts, key_parts = [], [], [], [], []
        for head in range(start, start + JOINED):
            own_keys = masked(key_rows, own[head])
            left = jnp.where(own[head], scaled, masked(carried, after[head]))
            right = jnp.where(after[head], -jnp.ones_like(values), values)
            if kept_weights is None:
                weights = key_weights(own_keys, queries)
            else:
                weights = kept_weights[head * BALL : (head + 1) * BALL, :].astype(f32)
            score_parts.append((weights * dot(right, left, 1, 1)).astype(bf16))
            weight_parts.append(weights.astype(bf16))
            scaled_parts.append(masked(scaled, own[head]))
            query_parts.append(masked(queries, own[head]))
            key_parts.append(own_keys)
        grad_values += dot(
            jnp.concatenate(weight_parts, axis=1), jnp.concatenate(scaled_parts, axis=0)
        )
        grad_keys += dot(
            jnp.concatenate(score_parts, axis=1), jnp.concatenate(query_parts, axis=0)
        )
        grad_queries += dot(
            jnp.concatenate(score_parts, axis=0), jnp.concatenate(key_parts, axis=0), 0, 0
        )
    return grad_queries, grad_keys * (1.0 / LOG2E), grad_values


def ball_slices(rows):
    return [slice(start, start + BALL) for start in range(0, rows, BALL)]


def block_backward(
    kept, rounded, attended, inverse, grad_rows, inward, outward, weights_ref=None
):
    widened, row_scale, normed, query_unit, query_scale, key_unit, key_scale = kept
    width = widened.shape[1]
    grad_attended = dot(grad_rows, outward, 1, 1)
    parts = []
    for place, ball in enumerate(ball_slices(widened.shape[0])):
        kept_weights = None
        if weights_ref is not None:
            kept_weights = weights_ref[0, place * HEADS * BALL : (place + 1) * HEADS * BALL, :]
        parts.append(
            attend_backward(
                *(array[ball] for array in rounded),
                attended[ball].astype(f32),
                inverse[ball],
                grad_attended[ball],
                kept_weights,
            )
        )
    grad_queries, grad_keys, grad_values = (jnp.concatenate(p, axis=0) for p in zip(*parts))
    grad_queries = grad_queries * (width // HEADS) ** (-0.5)
    grad_qraw = query_scale * (
        grad_queries - query_unit * jnp.mean(grad_queries * query_unit, axis=-1, keepdims=True)
    )
    grad_kraw = key_scale * (
        grad_keys - key_unit * jnp.mean(grad_keys * key_unit, axis=-1, keepdims=True)
    )
    grad_mixture = jnp.concatenate([grad_qraw, grad_kraw, grad_values], axis=1).astype(bf16)
    grad_outward = dot(attended.astype(bf16), grad_rows, 0, 0)
    grad_inward = dot(normed, grad_mixture, 0, 0)
    grad_normed = dot(grad_mixture, inward, 1, 1)
    unit_rows = widened * row_scale
    grad_input = grad_rows.astype(f32) + row_scale * (
        grad_normed - unit_rows * jnp.mean(grad_normed * unit_rows, axis=-1, keepdims=True)
    )
    return grad_input.astype(bf16), grad_inward, grad_outward


def pack(slot_row, rows):
    return dot(one_hot_rows(slot_row, SLOTS), rows).astype(bf16)


def put_packets(packed, packet_refs):
    kinds, width = packet_refs[0].shape[2], packet_refs[0].shape[4]
    for hop in range(REACH):
        for member in range(GROUP):
            start = (hop * GROUP + member) * CAP
            for kind in range(kinds):
                part = packed[start : start + CAP, kind * width : (kind + 1) * width]
                packet_refs[hop][member, 0, kind] = part


def flat(refs):
    parts = [(ref, 0) for ref in refs[:REACH]]
    parts += [(ref, hop) for ref in refs[REACH:] for hop in range(REACH)]
    kinds = refs[0].shape[2]
    return [jnp.concatenate([ref[hop, 0, k] for ref, hop in parts], axis=0) for k in range(kinds)]


def add_up(total_ref, term):
    first = pl.program_id(0) == 0

    @pl.when(first)
    def _():
        total_ref[...] = term

    @pl.when(jnp.logical_not(first))
    def _():
        total_ref[...] += term


def join_grads(total_ref, inward_grad, outward_grad):
    width = outward_grad.shape[0]
    for third in range(3):
        part = inward_grad[:, third * width : (third + 1) * width]
        total_ref[third * width : (third + 1) * width, :] = part.astype(bf16)
    total_ref[3 * width : 4 * width, :] = outward_grad.astype(bf16)


def add_grads(total_ref, sum_refs, grads, other_ref=None):
    for sum_ref, grad in zip(sum_refs, grads):
        add_up(sum_ref, grad)

    @pl.when(pl.program_id(0) == pl.num_programs(0) - 1)
    def _():
        join_grads(total_ref, *(ref[...] for ref in sum_refs))
        if other_ref is not None:
            total_ref[other_ref.shape[0] :, :] = other_ref[...]


def sample_row(meta_ref, kind):
    samples = meta_ref.shape[0] // 2
    return meta_ref[pl.ds(kind * samples + pl.program_id(0), 1), :]


def attend_balls(rounded):
    rows = rounded[0].shape[0]
    parts = [attend(*(array[ball] for array in rounded)) for ball in ball_slices(rows)]
    attended, inverse = (jnp.concatenate(part, axis=0) for part in zip(*parts))
    return attended, inverse


def forward_kernel(nodes_ref, cot_ref, inward_ref, outward_ref, meta_ref, *refs):
    after_ref, attended_ref, inverse_ref, rounded_ref, scales_ref, *packet_refs = refs
    width = nodes_ref.shape[2]
    widened, _, normed = norm(nodes_ref[0])
    (_, query_scale, _, key_scale), rounded = project(normed, inward_ref[...])
    attended, inverse = attend_balls(rounded)
    attended = attended.astype(bf16)
    attended_ref[0] = attended
    inverse_ref[0] = inverse
    for place, array in enumerate(rounded):
        rounded_ref[0, :, place * width : (place + 1) * width] = array
    lane = lax.broadcasted_iota(jnp.int32, scales_ref.shape[1:], 1)
    scales_ref[0] = jnp.where(lane == 0, query_scale, key_scale)
    result = (widened + dot(attended, outward_ref[...])).astype(bf16)
    after_ref[0] = result
    both = jnp.concatenate([result, cot_ref[0]], axis=1)
    put_packets(pack(sample_row(meta_ref, 0), both), packet_refs)


def each_ball(rows, body):
    @pl.loop(0, rows // BALL)
    def _(ball):
        body(ball, pl.ds(pl.multiple_of(ball * BALL, BALL), BALL))


def weights_kernel(rounded_ref, weights_ref):
    width = rounded_ref.shape[2] // 3
    own, _ = head_masks(width)

    def body(ball, here):
        queries = rounded_ref[0, here, :width]
        key_rows = rounded_ref[0, here, width : 2 * width]
        for head in range(HEADS):
            start = pl.multiple_of((ball * HEADS + head) * BALL, BALL)
            weights = key_weights(masked(key_rows, own[head]), queries)
            weights_ref[0, pl.ds(start, BALL), :] = weights.astype(bf16)

    each_ball(rounded_ref.shape[1], body)


def near_kernel(meta_ref, *refs):
    *home_refs, near_ref, picks_ref = refs
    picks_ref[...] = spread_column(sample_row(meta_ref, 1))
    rows, width = home_refs[0].shape[1:]

    def body(ball, here):
        hits = one_hot_picks(picks_ref[here, :], 0, rows)
        for kind, home_ref in enumerate(home_refs):
            near = dot(hits, home_ref[0]).astype(bf16)
            near_ref[0, here, kind * width : (kind + 1) * width] = near

    each_ball(rows, body)


def add_far(meta_ref, near_ref, landed_refs):
    hits = one_hot_picks(spread_column(sample_row(meta_ref, 1)), near_ref.shape[1], SLOTS)
    rows = []
    for kind, landed in enumerate(flat(landed_refs)):
        width = landed.shape[1]
        near = near_ref[0, :, kind * width : (kind + 1) * width]
        rows.append((near.astype(f32) + dot(hits, landed)).astype(bf16))
    return rows


def second_kernel(meta_ref, near_ref, inward_ref, outward_ref, *refs):
    arrived_refs, refs = refs[:LANDED], refs[LANDED:]
    grad_ref, total_ref, *packet_refs = refs[: 2 + REACH]
    *sum_refs, rotated_ref, rotated_cot_ref = refs[2 + REACH :]

    @pl.when(pl.program_id(0) >= 0)
    def _():
        rotated_ref[...], rotated_cot_ref[...] = add_far(meta_ref, near_ref, arrived_refs)

    kept = norm(rotated_ref[...])
    units, rounded = project(kept[2], inward_ref[...])
    attended, inverse = attend_balls(rounded)
    grad_input, *grads = block_backward(
        kept + units,
        rounded,
        attended,
        inverse,
        rotated_cot_ref[...],
        inward_ref[...],
        outward_ref[...],
    )
    grad_ref[0] = grad_input
    add_grads(total_ref, sum_refs, grads)
    put_packets(pack(sample_row(meta_ref, 0), grad_input), packet_refs)


def first_kernel(
    meta_ref,
    nodes_ref,
    near_ref,
    attended_ref,
    inverse_ref,
    rounded_ref,
    scales_ref,
    weights_ref,
    inward_ref,
    outward_ref,
    *refs,
):
    returned_refs, refs = refs[:LANDED], refs[LANDED:]
    other_ref, grad_ref, total_ref, *sum_refs = refs
    (grad_after,) = add_far(meta_ref, near_ref, returned_refs)
    width = nodes_ref.shape[2]
    rounded = [rounded_ref[0, :, place * width : (place + 1) * width] for place in range(3)]
    query_unit = rounded[0].astype(f32) * (1.0 / score_factor(width))
    key_unit = rounded[1].astype(f32)
    units = (query_unit, scales_ref[0, :, 0:1], key_unit, scales_ref[0, :, 1:2])
    grad_input, *grads = block_backward(
        norm(nodes_ref[0]) + units,
        rounded,
        attended_ref[0],
        inverse_ref[0],
        grad_after,
        inward_ref[...],
        outward_ref[...],
        weights_ref,
    )
    grad_ref[0] = grad_input
    add_grads(total_ref, sum_refs, grads, other_ref)


def split_kernel(whole_ref, *refs):
    width = refs[1].shape[0]
    for place, (inward_ref, outward_ref) in enumerate((refs[:2], refs[2:])):
        start = place * 4 * width
        for third in range(3):
            part = whole_ref[start + third * width : start + (third + 1) * width, :]
            inward_ref[:, third * width : (third + 1) * width] = part.astype(f32)
        outward_ref[...] = whole_ref[start + 3 * width : start + 4 * width, :].astype(f32)


def full_spec(shape):
    return pl.BlockSpec(shape, lambda i: (0,) * len(shape))


def call(kernel, name, micros, in_specs, operands, outs, out_specs=None, steps=1, **options):
    specs = [
        full_spec(operand.shape) if spec is None else spec
        for spec, operand in zip(in_specs or [None] * len(operands), operands)
    ]
    return pl.pallas_call(
        kernel,
        name=name,
        grid=(steps,),
        in_specs=specs,
        out_specs=out_specs or [full_spec(out.shape) for out in outs],
        out_shape=outs,
        compiler_params=pltpu.CompilerParams(vmem_limit_bytes=VMEM_LIMIT),
        cost_estimate=pl.CostEstimate(
            flops=int(micros * 1.15e9), bytes_accessed=2**20, transcendentals=0
        ),
        **options,
    )(*operands)


def rotate(value, axis, steps):
    count = lax.axis_size(axis)
    pairs = [(source, (source + steps) % count) for source in range(count)]
    return lax.ppermute(value, axis, pairs)


def hop_stage(packets):
    return [p if hop == 0 else rotate(p, "pts", hop) for hop, p in zip(HOPS, packets)]


def restack(moved):
    return [
        jnp.concatenate([packet[member : member + 1] for packet in moved], axis=0)
        for member in range(1, GROUP)
    ]


def member_stage(moved, stacked):
    return moved + [rotate(s, "grp", 1 + place) for place, s in enumerate(stacked)]


def exchange(packets):
    moved = hop_stage(packets)
    return member_stage(moved, restack(moved))


def reduce_all(terms, factor):
    count = lax.axis_size(AXES)
    pieces = terms.reshape(count, -1, terms.shape[1])
    mine = lax.all_to_all(pieces, AXES, 0, 0, tiled=True)
    total = (jnp.sum(mine.astype(f32), axis=0) * factor).astype(bf16)
    spread = jnp.broadcast_to(total[None], pieces.shape)
    return lax.all_to_all(spread, AXES, 0, 0, tiled=True).reshape(terms.shape)


def per_device(
    nodes,
    cotangent,
    first_inward,
    first_outward,
    second_inward,
    second_outward,
    rotated_source,
    rotated_index,
):
    samples, rows, width = nodes.shape
    shards = lax.axis_size(AXES)
    own = lax.axis_index(AXES).astype(jnp.int32).reshape(1)
    shape = jax.ShapeDtypeStruct
    smem = pl.BlockSpec(memory_space=pltpu.SMEM)
    rows_shape = shape(nodes.shape, bf16)
    meta_shape = shape((2 * samples, rows), jnp.int32)
    joined_shape = shape((4 * width, width), bf16)
    both_shape = shape((8 * width, width), bf16)
    sums = [pltpu.VMEM((width, 3 * width), f32), pltpu.VMEM((width, width), f32)]
    first_weights = (first_inward, first_outward)
    second_weights = (second_inward, second_outward)

    def by_sample(*dims):
        return pl.BlockSpec((1, *dims), lambda s: (s, *(0 for _ in dims)))

    def packets(kinds):
        return [shape((GROUP, samples, kinds, CAP, width), bf16)] * REACH

    def packets_by_sample(kinds):
        return [pl.BlockSpec((GROUP, 1, kinds, CAP, width), lambda s: (0, s, 0, 0, 0))] * REACH

    def landed_by_sample(kinds):
        one = pl.BlockSpec((1, 1, kinds, CAP, width), lambda s: (0, s, 0, 0, 0))
        hops = pl.BlockSpec((REACH, 1, kinds, CAP, width), lambda s: (0, s, 0, 0, 0))
        return [one] * REACH + [hops] * (GROUP - 1)

    rows_spec = by_sample(rows, width)
    (send_meta,) = call(
        functools.partial(send_kernel, shards=shards),
        "send_places",
        2,
        [smem, None],
        (own, rotated_index),
        [meta_shape],
    )
    after_first, attended, inverse, rounded, scales, *out_packets = call(
        forward_kernel,
        "forward",
        9,
        [rows_spec, rows_spec, None, None, None],
        (nodes, cotangent, *first_weights, send_meta),
        [
            rows_shape,
            rows_shape,
            shape(nodes.shape, f32),
            shape((samples, rows, 3 * width), bf16),
            shape((samples, rows, 128), f32),
        ]
        + packets(2),
        [rows_spec] * 3
        + [by_sample(rows, 3 * width), by_sample(rows, 128)]
        + packets_by_sample(2),
        samples,
    )
    arrived = exchange(out_packets)
    (receive_meta,) = call(
        functools.partial(receive_kernel, shards=shards),
        "receive_places",
        2,
        [smem, None],
        (own, rotated_source),
        [meta_shape],
    )
    (near,) = call(
        near_kernel,
        "near_out",
        3,
        [None, rows_spec, rows_spec],
        (receive_meta, after_first, cotangent),
        [shape((samples, rows, 2 * width), bf16)],
        [by_sample(rows, 2 * width)],
        samples,
        scratch_shapes=[pltpu.VMEM((rows, 128), f32)],
    )
    weights_spec = by_sample(rows * HEADS, BALL)
    (weights,) = call(
        weights_kernel,
        "weights",
        6,
        [by_sample(rows, 3 * width)],
        (rounded,),
        [shape((samples, rows * HEADS, BALL), bf16)],
        [weights_spec],
        samples,
    )
    rotated_grad, second_joined, *back_packets = call(
        second_kernel,
        "second",
        26,
        [None, by_sample(rows, 2 * width), None, None] + landed_by_sample(2),
        (receive_meta, near, *second_weights, *arrived),
        [rows_shape, joined_shape] + packets(1),
        [rows_spec, full_spec(joined_shape.shape)] + packets_by_sample(1),
        samples,
        scratch_shapes=sums + [pltpu.VMEM((rows, width), bf16)] * 2,
    )
    returned = exchange(back_packets)
    (grad_near,) = call(
        near_kernel,
        "near_back",
        2,
        [None, rows_spec],
        (send_meta, rotated_grad),
        [rows_shape],
        [rows_spec],
        samples,
        scratch_shapes=[pltpu.VMEM((rows, 128), f32)],
    )
    input_grad, joined = call(
        first_kernel,
        "first",
        16,
        [None]
        + [rows_spec] * 4
        + [by_sample(rows, 3 * width), by_sample(rows, 128), weights_spec, None, None]
        + landed_by_sample(1)
        + [None],
        (
            send_meta,
            nodes,
            grad_near,
            attended,
            inverse,
            rounded,
            scales,
            weights,
            *first_weights,
            *returned,
            second_joined,
        ),
        [rows_shape, both_shape],
        [rows_spec, full_spec(both_shape.shape)],
        samples,
        scratch_shapes=sums,
    )
    factor = 1.0 / math.sqrt(samples * rows * shards)
    grad_shapes = [shape((width, 3 * width), f32), shape((width, width), f32)]
    grads = call(split_kernel, "split", 2, None, (reduce_all(joined, factor),), grad_shapes * 2)
    return (input_grad, *grads)


def solution(mesh):
    in_specs = (
        P(None, AXES, None),
        P(None, AXES, None),
        P(),
        P(),
        P(),
        P(),
        P(None, AXES),
        P(None, AXES),
    )
    out_specs = (P(None, AXES, None), P(), P(), P(), P())
    return jax.shard_map(
        per_device, mesh=mesh, in_specs=in_specs, out_specs=out_specs, check_vma=False
    )
```

```python
import functools
import math

import jax
import jax.numpy as jnp
from jax import lax
from jax.experimental import pallas as pl
from jax.experimental.pallas import tpu as pltpu
from jax.sharding import PartitionSpec as P

HEADS = 8
BALL = 256
SPAN = 8
CAP = 32
EPSILON = 1e-06
AXES = ("pts", "grp")
GROUP = 4
HOPS = tuple(range(-(SPAN // GROUP), SPAN // GROUP + 1))
REACH = len(HOPS)
SLOTS = REACH * GROUP * CAP
LANDED = REACH + GROUP - 1
VMEM_LIMIT = 28 * 1024 * 1024

f32 = jnp.float32
bf16 = jnp.bfloat16


def dot(left, right, left_dim=1, right_dim=0):
    return lax.dot_general(
        left, right, (((left_dim,), (right_dim,)), ((), ())), preferred_element_type=f32
    )


def spread_column(row):
    return jnp.transpose(jnp.broadcast_to(row.astype(f32), (128, row.shape[1])))


def one_hot_rows(slot_row, slots):
    ids = lax.broadcasted_iota(jnp.int32, (slots, slot_row.shape[1]), 0)
    return jnp.where(ids == slot_row, 1.0, 0.0).astype(bf16)


def one_hot_picks(pick_column, start, width):
    lanes = lax.broadcasted_iota(jnp.int32, pick_column.shape, 1).astype(f32)
    pieces = [
        jnp.where(pick_column == lanes + float(start + 128 * piece), 1.0, 0.0).astype(bf16)
        for piece in range(width // 128)
    ]
    return jnp.concatenate(pieces, axis=1)


def same_before(column, row, row_ids, lane_ids):
    counts = []
    for piece in range(row.shape[1] // 128):
        lanes = slice(128 * piece, 128 * piece + 128)
        same = (column == row[:, lanes]) & (row_ids < lane_ids + float(128 * piece))
        counts.append(jnp.sum(jnp.where(same, 1.0, 0.0), axis=0, keepdims=True))
    return jnp.concatenate(counts, axis=1).astype(jnp.int32)


def count_between(column, floor_row, row):
    counts = []
    for piece in range(row.shape[1] // 128):
        lanes = slice(128 * piece, 128 * piece + 128)
        inside = (column >= floor_row[:, lanes]) & (column < row[:, lanes])
        counts.append(jnp.sum(jnp.where(inside, 1.0, 0.0), axis=0, keepdims=True))
    return jnp.concatenate(counts, axis=1).astype(jnp.int32)


def slots_of(shard, own, rank, shards):
    member = (shard - own) & (GROUP - 1)
    hop = ((shard // GROUP) - (own // GROUP) + REACH // 2) & (shards // GROUP - 1)
    leave = (hop * GROUP + member) * CAP + rank
    land = (((-member) & (GROUP - 1)) * REACH + (REACH - 1 - hop)) * CAP + rank
    return leave, land


def send_kernel(own_ref, index_ref, meta_ref, *, shards):
    samples, rows = index_ref.shape
    own = own_ref[0]
    row_ids = lax.broadcasted_iota(jnp.int32, (rows, 128), 0).astype(f32)
    lane_ids = lax.broadcasted_iota(jnp.int32, (rows, 128), 1).astype(f32)
    for sample in range(samples):
        index = index_ref[sample : sample + 1, :]
        shard = index // rows
        rank = same_before(spread_column(shard), shard.astype(f32), row_ids, lane_ids)
        leave, land = slots_of(shard, own, rank, shards)
        meta_ref[sample : sample + 1, :] = jnp.where(shard == own, -1, leave)
        meta_ref[samples + sample : samples + sample + 1, :] = jnp.where(
            shard == own, index - own * rows, rows + land
        )


def receive_kernel(own_ref, source_ref, meta_ref, *, shards):
    samples, rows = source_ref.shape
    own = own_ref[0]
    for sample in range(samples):
        source = source_ref[sample : sample + 1, :]
        shard = source // rows
        floor_row = (shard * rows).astype(f32)
        rank = count_between(spread_column(source), floor_row, source.astype(f32))
        leave, land = slots_of(shard, own, rank, shards)
        meta_ref[sample : sample + 1, :] = jnp.where(shard == own, -1, leave)
        meta_ref[samples + sample : samples + sample + 1, :] = jnp.where(
            shard == own, source - own * rows, rows + land
        )


LOG2E = 1.4426950408889634
JOINED = 4


def masked(array, mask):
    return jnp.where(mask, array, jnp.zeros_like(array))


def head_masks(width):
    heads = lax.broadcasted_iota(jnp.int32, (BALL, width), 1) // (width // HEADS)
    own = [heads == head for head in range(HEADS)]
    return own, own[1:] + own[:1]


def norm(rows):
    widened = rows.astype(f32)
    row_scale = lax.rsqrt(jnp.mean(widened * widened, axis=-1, keepdims=True) + EPSILON)
    return widened, row_scale, (widened * row_scale).astype(bf16)


def score_factor(width):
    return LOG2E * (width // HEADS) ** (-0.5)


def project(normed, inward):
    width = normed.shape[1]
    mixture = dot(normed, inward)
    query_raw = mixture[:, :width]
    key_raw = mixture[:, width : 2 * width]
    query_scale = lax.rsqrt(jnp.mean(query_raw * query_raw, axis=-1, keepdims=True) + EPSILON)
    key_scale = lax.rsqrt(jnp.mean(key_raw * key_raw, axis=-1, keepdims=True) + EPSILON)
    query_unit = query_raw * query_scale
    key_unit = key_raw * key_scale
    rounded = (
        (query_unit * score_factor(width)).astype(bf16),
        key_unit.astype(bf16),
        mixture[:, 2 * width :].astype(bf16),
    )
    return (query_unit, query_scale, key_unit, key_scale), rounded


def key_weights(own_keys, queries):
    return jnp.exp2(dot(own_keys, queries, 1, 1))


def attend(queries, key_rows, values):
    width = queries.shape[1]
    half = width // 2
    own, _ = head_masks(width)
    results = []
    for start in range(0, HEADS, HEADS // 2):
        weights = []
        rights = []
        for head in range(start, start + HEADS // 2):
            scores = dot(masked(queries, own[head]), key_rows, 1, 1)
            weights.append(jnp.exp2(scores).astype(bf16))
            opposite = own[(head + HEADS // 2) % HEADS]
            ones = jnp.where(opposite, jnp.ones_like(values), jnp.zeros_like(values))
            rights.append(jnp.where(own[head], values, ones))
        results.append(dot(jnp.concatenate(weights, axis=1), jnp.concatenate(rights, axis=0)))
    low, high = results
    sums = jnp.concatenate([low[:, :half], high[:, half:]], axis=1)
    inverse = 1.0 / jnp.concatenate([low[:, half:], high[:, :half]], axis=1)
    return sums * inverse, inverse


def attend_backward(
    queries, key_rows, values, attended, inverse, grad_attended, kept_weights=None
):
    width = queries.shape[1]
    depth = width // HEADS
    own, after = head_masks(width)
    scaled = (grad_attended * inverse).astype(bf16)
    product = scaled.astype(f32) * attended
    high = product.astype(bf16)
    low = (product - high.astype(f32)).astype(bf16)
    groups = lax.broadcasted_iota(jnp.int32, (width, width), 0) // depth
    same_head = groups == lax.broadcasted_iota(jnp.int32, (width, width), 1) // depth
    group_ones = jnp.where(same_head, 1.0, 0.0).astype(bf16)
    column_sum = pltpu.roll(dot(high, group_ones) + dot(low, group_ones), depth, 1)
    column_high = column_sum.astype(bf16)
    column_low = (column_sum - column_high.astype(f32)).astype(bf16)
    lane = lax.broadcasted_iota(jnp.int32, (BALL, width), 1) % depth
    carried = jnp.where(lane == 0, column_high, masked(column_low, lane == 1))
    grad_queries = jnp.zeros((BALL, width), f32)
    grad_keys = jnp.zeros((BALL, width), f32)
    grad_values = jnp.zeros((BALL, width), f32)
    for start in range(0, HEADS, JOINED):
        weight_parts, score_parts, scaled_parts, query_parts, key_parts = [], [], [], [], []
        for head in range(start, start + JOINED):
            own_keys = masked(key_rows, own[head])
            left = jnp.where(own[head], scaled, masked(carried, after[head]))
            right = jnp.where(after[head], -jnp.ones_like(values), values)
            if kept_weights is None:
                weights = key_weights(own_keys, queries)
            else:
                weights = kept_weights[head * BALL : (head + 1) * BALL, :].astype(f32)
            score_parts.append((weights * dot(right, left, 1, 1)).astype(bf16))
            weight_parts.append(weights.astype(bf16))
            scaled_parts.append(masked(scaled, own[head]))
            query_parts.append(masked(queries, own[head]))
            key_parts.append(own_keys)
        grad_values += dot(
            jnp.concatenate(weight_parts, axis=1), jnp.concatenate(scaled_parts, axis=0)
        )
        grad_keys += dot(
            jnp.concatenate(score_parts, axis=1), jnp.concatenate(query_parts, axis=0)
        )
        grad_queries += dot(
            jnp.concatenate(score_parts, axis=0), jnp.concatenate(key_parts, axis=0), 0, 0
        )
    return grad_queries, grad_keys * (1.0 / LOG2E), grad_values


def ball_slices(rows):
    return [slice(start, start + BALL) for start in range(0, rows, BALL)]


def block_backward(
    kept, rounded, attended, inverse, grad_rows, inward, outward, weights_ref=None
):
    widened, row_scale, normed, query_unit, query_scale, key_unit, key_scale = kept
    width = widened.shape[1]
    grad_attended = dot(grad_rows, outward, 1, 1)
    parts = []
    for place, ball in enumerate(ball_slices(widened.shape[0])):
        kept_weights = None
        if weights_ref is not None:
            kept_weights = weights_ref[0, place * HEADS * BALL : (place + 1) * HEADS * BALL, :]
        parts.append(
            attend_backward(
                *(array[ball] for array in rounded),
                attended[ball].astype(f32),
                inverse[ball],
                grad_attended[ball],
                kept_weights,
            )
        )
    grad_queries, grad_keys, grad_values = (jnp.concatenate(p, axis=0) for p in zip(*parts))
    grad_queries = grad_queries * (width // HEADS) ** (-0.5)
    grad_qraw = query_scale * (
        grad_queries - query_unit * jnp.mean(grad_queries * query_unit, axis=-1, keepdims=True)
    )
    grad_kraw = key_scale * (
        grad_keys - key_unit * jnp.mean(grad_keys * key_unit, axis=-1, keepdims=True)
    )
    grad_mixture = jnp.concatenate([grad_qraw, grad_kraw, grad_values], axis=1).astype(bf16)
    grad_outward = dot(attended.astype(bf16), grad_rows, 0, 0)
    grad_inward = dot(normed, grad_mixture, 0, 0)
    grad_normed = dot(grad_mixture, inward, 1, 1)
    unit_rows = widened * row_scale
    grad_input = grad_rows.astype(f32) + row_scale * (
        grad_normed - unit_rows * jnp.mean(grad_normed * unit_rows, axis=-1, keepdims=True)
    )
    return grad_input.astype(bf16), grad_inward, grad_outward


def pack(slot_row, rows):
    return dot(one_hot_rows(slot_row, SLOTS), rows).astype(bf16)


def put_packets(packed, packet_refs):
    kinds, width = packet_refs[0].shape[2], packet_refs[0].shape[4]
    for hop in range(REACH):
        for member in range(GROUP):
            start = (hop * GROUP + member) * CAP
            for kind in range(kinds):
                part = packed[start : start + CAP, kind * width : (kind + 1) * width]
                packet_refs[hop][member, 0, kind] = part


def flat(refs):
    parts = [(ref, 0) for ref in refs[:REACH]]
    parts += [(ref, hop) for ref in refs[REACH:] for hop in range(REACH)]
    kinds = refs[0].shape[2]
    return [jnp.concatenate([ref[hop, 0, k] for ref, hop in parts], axis=0) for k in range(kinds)]


def add_up(total_ref, term):
    first = pl.program_id(0) == 0

    @pl.when(first)
    def _():
        total_ref[...] = term

    @pl.when(jnp.logical_not(first))
    def _():
        total_ref[...] += term


def join_grads(total_ref, inward_grad, outward_grad):
    width = outward_grad.shape[0]
    for third in range(3):
        part = inward_grad[:, third * width : (third + 1) * width]
        total_ref[third * width : (third + 1) * width, :] = part.astype(bf16)
    total_ref[3 * width : 4 * width, :] = outward_grad.astype(bf16)


def add_grads(total_ref, sum_refs, grads, other_ref=None):
    for sum_ref, grad in zip(sum_refs, grads):
        add_up(sum_ref, grad)

    @pl.when(pl.program_id(0) == pl.num_programs(0) - 1)
    def _():
        join_grads(total_ref, *(ref[...] for ref in sum_refs))
        if other_ref is not None:
            total_ref[other_ref.shape[0] :, :] = other_ref[...]


def sample_row(meta_ref, kind):
    samples = meta_ref.shape[0] // 2
    return meta_ref[pl.ds(kind * samples + pl.program_id(0), 1), :]


def attend_balls(rounded):
    rows = rounded[0].shape[0]
    parts = [attend(*(array[ball] for array in rounded)) for ball in ball_slices(rows)]
    attended, inverse = (jnp.concatenate(part, axis=0) for part in zip(*parts))
    return attended, inverse


def forward_kernel(nodes_ref, cot_ref, inward_ref, outward_ref, meta_ref, *refs):
    after_ref, attended_ref, inverse_ref, rounded_ref, scales_ref, *packet_refs = refs
    width = nodes_ref.shape[2]
    widened, _, normed = norm(nodes_ref[0])
    (_, query_scale, _, key_scale), rounded = project(normed, inward_ref[...])
    attended, inverse = attend_balls(rounded)
    attended = attended.astype(bf16)
    attended_ref[0] = attended
    inverse_ref[0] = inverse
    for place, array in enumerate(rounded):
        rounded_ref[0, :, place * width : (place + 1) * width] = array
    lane = lax.broadcasted_iota(jnp.int32, scales_ref.shape[1:], 1)
    scales_ref[0] = jnp.where(lane == 0, query_scale, key_scale)
    result = (widened + dot(attended, outward_ref[...])).astype(bf16)
    after_ref[0] = result
    both = jnp.concatenate([result, cot_ref[0]], axis=1)
    put_packets(pack(sample_row(meta_ref, 0), both), packet_refs)


def each_ball(rows, body):
    @pl.loop(0, rows // BALL)
    def _(ball):
        body(ball, pl.ds(pl.multiple_of(ball * BALL, BALL), BALL))


def weights_kernel(rounded_ref, weights_ref):
    width = rounded_ref.shape[2] // 3
    own, _ = head_masks(width)

    def body(ball, here):
        queries = rounded_ref[0, here, :width]
        key_rows = rounded_ref[0, here, width : 2 * width]
        for head in range(HEADS):
            start = pl.multiple_of((ball * HEADS + head) * BALL, BALL)
            weights = key_weights(masked(key_rows, own[head]), queries)
            weights_ref[0, pl.ds(start, BALL), :] = weights.astype(bf16)

    each_ball(rounded_ref.shape[1], body)


def near_kernel(meta_ref, *refs):
    *home_refs, near_ref, picks_ref = refs
    picks_ref[...] = spread_column(sample_row(meta_ref, 1))
    rows, width = home_refs[0].shape[1:]

    def body(ball, here):
        hits = one_hot_picks(picks_ref[here, :], 0, rows)
        for kind, home_ref in enumerate(home_refs):
            near = dot(hits, home_ref[0]).astype(bf16)
            near_ref[0, here, kind * width : (kind + 1) * width] = near

    each_ball(rows, body)


def add_far(meta_ref, near_ref, landed_refs):
    hits = one_hot_picks(spread_column(sample_row(meta_ref, 1)), near_ref.shape[1], SLOTS)
    rows = []
    for kind, landed in enumerate(flat(landed_refs)):
        width = landed.shape[1]
        near = near_ref[0, :, kind * width : (kind + 1) * width]
        rows.append((near.astype(f32) + dot(hits, landed)).astype(bf16))
    return rows


def second_kernel(meta_ref, near_ref, inward_ref, outward_ref, *refs):
    arrived_refs, refs = refs[:LANDED], refs[LANDED:]
    grad_ref, total_ref, *packet_refs = refs[: 2 + REACH]
    *sum_refs, rotated_ref, rotated_cot_ref = refs[2 + REACH :]

    @pl.when(pl.program_id(0) >= 0)
    def _():
        rotated_ref[...], rotated_cot_ref[...] = add_far(meta_ref, near_ref, arrived_refs)

    kept = norm(rotated_ref[...])
    units, rounded = project(kept[2], inward_ref[...])
    attended, inverse = attend_balls(rounded)
    grad_input, *grads = block_backward(
        kept + units,
        rounded,
        attended,
        inverse,
        rotated_cot_ref[...],
        inward_ref[...],
        outward_ref[...],
    )
    grad_ref[0] = grad_input
    add_grads(total_ref, sum_refs, grads)
    put_packets(pack(sample_row(meta_ref, 0), grad_input), packet_refs)


def first_kernel(
    meta_ref,
    nodes_ref,
    near_ref,
    attended_ref,
    inverse_ref,
    rounded_ref,
    scales_ref,
    weights_ref,
    inward_ref,
    outward_ref,
    *refs,
):
    returned_refs, refs = refs[:LANDED], refs[LANDED:]
    other_ref, grad_ref, total_ref, *sum_refs = refs
    (grad_after,) = add_far(meta_ref, near_ref, returned_refs)
    width = nodes_ref.shape[2]
    rounded = [rounded_ref[0, :, place * width : (place + 1) * width] for place in range(3)]
    query_unit = rounded[0].astype(f32) * (1.0 / score_factor(width))
    key_unit = rounded[1].astype(f32)
    units = (query_unit, scales_ref[0, :, 0:1], key_unit, scales_ref[0, :, 1:2])
    grad_input, *grads = block_backward(
        norm(nodes_ref[0]) + units,
        rounded,
        attended_ref[0],
        inverse_ref[0],
        grad_after,
        inward_ref[...],
        outward_ref[...],
        weights_ref,
    )
    grad_ref[0] = grad_input
    add_grads(total_ref, sum_refs, grads, other_ref)


def split_kernel(whole_ref, *refs):
    width = refs[1].shape[0]
    for place, (inward_ref, outward_ref) in enumerate((refs[:2], refs[2:])):
        start = place * 4 * width
        for third in range(3):
            part = whole_ref[start + third * width : start + (third + 1) * width, :]
            inward_ref[:, third * width : (third + 1) * width] = part.astype(f32)
        outward_ref[...] = whole_ref[start + 3 * width : start + 4 * width, :].astype(f32)


def full_spec(shape):
    return pl.BlockSpec(shape, lambda i: (0,) * len(shape))


def call(kernel, name, micros, in_specs, operands, outs, out_specs=None, steps=1, **options):
    specs = [
        full_spec(operand.shape) if spec is None else spec
        for spec, operand in zip(in_specs or [None] * len(operands), operands)
    ]
    return pl.pallas_call(
        kernel,
        name=name,
        grid=(steps,),
        in_specs=specs,
        out_specs=out_specs or [full_spec(out.shape) for out in outs],
        out_shape=outs,
        compiler_params=pltpu.CompilerParams(vmem_limit_bytes=VMEM_LIMIT),
        cost_estimate=pl.CostEstimate(
            flops=int(micros * 1.15e9), bytes_accessed=2**20, transcendentals=0
        ),
        **options,
    )(*operands)


def rotate(value, axis, steps):
    count = lax.axis_size(axis)
    pairs = [(source, (source + steps) % count) for source in range(count)]
    return lax.ppermute(value, axis, pairs)


def hop_stage(packets):
    return [p if hop == 0 else rotate(p, "pts", hop) for hop, p in zip(HOPS, packets)]


def restack(moved):
    return [
        jnp.concatenate([packet[member : member + 1] for packet in moved], axis=0)
        for member in range(1, GROUP)
    ]


def member_stage(moved, stacked):
    return moved + [rotate(s, "grp", 1 + place) for place, s in enumerate(stacked)]


def exchange(packets):
    moved = hop_stage(packets)
    return member_stage(moved, restack(moved))


def reduce_all(terms, factor):
    count = lax.axis_size(AXES)
    pieces = terms.reshape(count, -1, terms.shape[1])
    mine = lax.all_to_all(pieces, AXES, 0, 0, tiled=True)
    total = (jnp.sum(mine.astype(f32), axis=0) * factor).astype(bf16)
    spread = jnp.broadcast_to(total[None], pieces.shape)
    return lax.all_to_all(spread, AXES, 0, 0, tiled=True).reshape(terms.shape)


def per_device(
    nodes,
    cotangent,
    first_inward,
    first_outward,
    second_inward,
    second_outward,
    rotated_source,
    rotated_index,
):
    samples, rows, width = nodes.shape
    shards = lax.axis_size(AXES)
    own = lax.axis_index(AXES).astype(jnp.int32).reshape(1)
    shape = jax.ShapeDtypeStruct
    smem = pl.BlockSpec(memory_space=pltpu.SMEM)
    rows_shape = shape(nodes.shape, bf16)
    meta_shape = shape((2 * samples, rows), jnp.int32)
    joined_shape = shape((4 * width, width), bf16)
    both_shape = shape((8 * width, width), bf16)
    sums = [pltpu.VMEM((width, 3 * width), f32), pltpu.VMEM((width, width), f32)]
    first_weights = (first_inward, first_outward)
    second_weights = (second_inward, second_outward)

    def by_sample(*dims):
        return pl.BlockSpec((1, *dims), lambda s: (s, *(0 for _ in dims)))

    def packets(kinds):
        return [shape((GROUP, samples, kinds, CAP, width), bf16)] * REACH

    def packets_by_sample(kinds):
        return [pl.BlockSpec((GROUP, 1, kinds, CAP, width), lambda s: (0, s, 0, 0, 0))] * REACH

    def landed_by_sample(kinds):
        one = pl.BlockSpec((1, 1, kinds, CAP, width), lambda s: (0, s, 0, 0, 0))
        hops = pl.BlockSpec((REACH, 1, kinds, CAP, width), lambda s: (0, s, 0, 0, 0))
        return [one] * REACH + [hops] * (GROUP - 1)

    rows_spec = by_sample(rows, width)
    (send_meta,) = call(
        functools.partial(send_kernel, shards=shards),
        "send_places",
        2,
        [smem, None],
        (own, rotated_index),
        [meta_shape],
    )
    after_first, attended, inverse, rounded, scales, *out_packets = call(
        forward_kernel,
        "forward",
        9,
        [rows_spec, rows_spec, None, None, None],
        (nodes, cotangent, *first_weights, send_meta),
        [
            rows_shape,
            rows_shape,
            shape(nodes.shape, f32),
            shape((samples, rows, 3 * width), bf16),
            shape((samples, rows, 128), f32),
        ]
        + packets(2),
        [rows_spec] * 3
        + [by_sample(rows, 3 * width), by_sample(rows, 128)]
        + packets_by_sample(2),
        samples,
    )
    arrived = exchange(out_packets)
    (receive_meta,) = call(
        functools.partial(receive_kernel, shards=shards),
        "receive_places",
        2,
        [smem, None],
        (own, rotated_source),
        [meta_shape],
    )
    (near,) = call(
        near_kernel,
        "near_out",
        3,
        [None, rows_spec, rows_spec],
        (receive_meta, after_first, cotangent),
        [shape((samples, rows, 2 * width), bf16)],
        [by_sample(rows, 2 * width)],
        samples,
        scratch_shapes=[pltpu.VMEM((rows, 128), f32)],
    )
    weights_spec = by_sample(rows * HEADS, BALL)
    (weights,) = call(
        weights_kernel,
        "weights",
        6,
        [by_sample(rows, 3 * width)],
        (rounded,),
        [shape((samples, rows * HEADS, BALL), bf16)],
        [weights_spec],
        samples,
    )
    near, weights = lax.optimization_barrier((near, weights))
    rotated_grad, second_joined, *back_packets = call(
        second_kernel,
        "second",
        26,
        [None, by_sample(rows, 2 * width), None, None] + landed_by_sample(2),
        (receive_meta, near, *second_weights, *arrived),
        [rows_shape, joined_shape] + packets(1),
        [rows_spec, full_spec(joined_shape.shape)] + packets_by_sample(1),
        samples,
        scratch_shapes=sums + [pltpu.VMEM((rows, width), bf16)] * 2,
    )
    returned = exchange(back_packets)
    (grad_near,) = call(
        near_kernel,
        "near_back",
        2,
        [None, rows_spec],
        (send_meta, rotated_grad),
        [rows_shape],
        [rows_spec],
        samples,
        scratch_shapes=[pltpu.VMEM((rows, 128), f32)],
    )
    input_grad, joined = call(
        first_kernel,
        "first",
        16,
        [None]
        + [rows_spec] * 4
        + [by_sample(rows, 3 * width), by_sample(rows, 128), weights_spec, None, None]
        + landed_by_sample(1)
        + [None],
        (
            send_meta,
            nodes,
            grad_near,
            attended,
            inverse,
            rounded,
            scales,
            weights,
            *first_weights,
            *returned,
            second_joined,
        ),
        [rows_shape, both_shape],
        [rows_spec, full_spec(both_shape.shape)],
        samples,
        scratch_shapes=sums,
    )
    factor = 1.0 / math.sqrt(samples * rows * shards)
    grad_shapes = [shape((width, 3 * width), f32), shape((width, width), f32)]
    grads = call(split_kernel, "split", 2, None, (reduce_all(joined, factor),), grad_shapes * 2)
    return (input_grad, *grads)


def solution(mesh):
    in_specs = (
        P(None, AXES, None),
        P(None, AXES, None),
        P(),
        P(),
        P(),
        P(),
        P(None, AXES),
        P(None, AXES),
    )
    out_specs = (P(None, AXES, None), P(), P(), P(), P())
    return jax.shard_map(
        per_device, mesh=mesh, in_specs=in_specs, out_specs=out_specs, check_vma=False
    )
```

```python
import functools
import math

import jax
import jax.numpy as jnp
from jax import lax
from jax.experimental import pallas as pl
from jax.experimental.pallas import tpu as pltpu
from jax.sharding import PartitionSpec as P

HEADS = 8
BALL = 256
SPAN = 8
CAP = 32
EPSILON = 1e-06
AXES = ("pts", "grp")
GROUP = 4
HOPS = tuple(range(-(SPAN // GROUP), SPAN // GROUP + 1))
REACH = len(HOPS)
SLOTS = REACH * GROUP * CAP
LANDED = REACH + GROUP - 1
VMEM_LIMIT = 28 * 1024 * 1024

f32 = jnp.float32
bf16 = jnp.bfloat16


def dot(left, right, left_dim=1, right_dim=0):
    return lax.dot_general(
        left, right, (((left_dim,), (right_dim,)), ((), ())), preferred_element_type=f32
    )


def spread_column(row):
    return jnp.transpose(jnp.broadcast_to(row.astype(f32), (128, row.shape[1])))


def one_hot_rows(slot_row, slots):
    ids = lax.broadcasted_iota(jnp.int32, (slots, slot_row.shape[1]), 0)
    return jnp.where(ids == slot_row, 1.0, 0.0).astype(bf16)


def one_hot_picks(pick_column, start, width):
    lanes = lax.broadcasted_iota(jnp.int32, pick_column.shape, 1).astype(f32)
    pieces = [
        jnp.where(pick_column == lanes + float(start + 128 * piece), 1.0, 0.0).astype(bf16)
        for piece in range(width // 128)
    ]
    return jnp.concatenate(pieces, axis=1)


def same_before(column, row, row_ids, lane_ids):
    counts = []
    for piece in range(row.shape[1] // 128):
        lanes = slice(128 * piece, 128 * piece + 128)
        same = (column == row[:, lanes]) & (row_ids < lane_ids + float(128 * piece))
        counts.append(jnp.sum(jnp.where(same, 1.0, 0.0), axis=0, keepdims=True))
    return jnp.concatenate(counts, axis=1).astype(jnp.int32)


def count_between(column, floor_row, row):
    counts = []
    for piece in range(row.shape[1] // 128):
        lanes = slice(128 * piece, 128 * piece + 128)
        inside = (column >= floor_row[:, lanes]) & (column < row[:, lanes])
        counts.append(jnp.sum(jnp.where(inside, 1.0, 0.0), axis=0, keepdims=True))
    return jnp.concatenate(counts, axis=1).astype(jnp.int32)


def slots_of(shard, own, rank, shards):
    member = (shard - own) & (GROUP - 1)
    hop = ((shard // GROUP) - (own // GROUP) + REACH // 2) & (shards // GROUP - 1)
    leave = (hop * GROUP + member) * CAP + rank
    land = (((-member) & (GROUP - 1)) * REACH + (REACH - 1 - hop)) * CAP + rank
    return leave, land


def send_kernel(own_ref, index_ref, meta_ref, *, shards):
    samples, rows = index_ref.shape
    own = own_ref[0]
    row_ids = lax.broadcasted_iota(jnp.int32, (rows, 128), 0).astype(f32)
    lane_ids = lax.broadcasted_iota(jnp.int32, (rows, 128), 1).astype(f32)
    for sample in range(samples):
        index = index_ref[sample : sample + 1, :]
        shard = index // rows
        rank = same_before(spread_column(shard), shard.astype(f32), row_ids, lane_ids)
        leave, land = slots_of(shard, own, rank, shards)
        meta_ref[sample : sample + 1, :] = jnp.where(shard == own, -1, leave)
        meta_ref[samples + sample : samples + sample + 1, :] = jnp.where(
            shard == own, index - own * rows, rows + land
        )


def receive_kernel(own_ref, source_ref, meta_ref, *, shards):
    samples, rows = source_ref.shape
    own = own_ref[0]
    for sample in range(samples):
        source = source_ref[sample : sample + 1, :]
        shard = source // rows
        floor_row = (shard * rows).astype(f32)
        rank = count_between(spread_column(source), floor_row, source.astype(f32))
        leave, land = slots_of(shard, own, rank, shards)
        meta_ref[sample : sample + 1, :] = jnp.where(shard == own, -1, leave)
        meta_ref[samples + sample : samples + sample + 1, :] = jnp.where(
            shard == own, source - own * rows, rows + land
        )


LOG2E = 1.4426950408889634
JOINED = 4


def masked(array, mask):
    return jnp.where(mask, array, jnp.zeros_like(array))


def head_masks(width):
    heads = lax.broadcasted_iota(jnp.int32, (BALL, width), 1) // (width // HEADS)
    own = [heads == head for head in range(HEADS)]
    return own, own[1:] + own[:1]


def norm(rows):
    widened = rows.astype(f32)
    row_scale = lax.rsqrt(jnp.mean(widened * widened, axis=-1, keepdims=True) + EPSILON)
    return widened, row_scale, (widened * row_scale).astype(bf16)


def score_factor(width):
    return LOG2E * (width // HEADS) ** (-0.5)


def project(normed, inward):
    width = normed.shape[1]
    mixture = dot(normed, inward)
    query_raw = mixture[:, :width]
    key_raw = mixture[:, width : 2 * width]
    query_scale = lax.rsqrt(jnp.mean(query_raw * query_raw, axis=-1, keepdims=True) + EPSILON)
    key_scale = lax.rsqrt(jnp.mean(key_raw * key_raw, axis=-1, keepdims=True) + EPSILON)
    query_unit = query_raw * query_scale
    key_unit = key_raw * key_scale
    rounded = (
        (query_unit * score_factor(width)).astype(bf16),
        key_unit.astype(bf16),
        mixture[:, 2 * width :].astype(bf16),
    )
    return (query_unit, query_scale, key_unit, key_scale), rounded


def key_weights(own_keys, queries):
    return jnp.exp2(dot(own_keys, queries, 1, 1))


def attend(queries, key_rows, values):
    width = queries.shape[1]
    half = width // 2
    own, _ = head_masks(width)
    results = []
    for start in range(0, HEADS, HEADS // 2):
        weights = []
        rights = []
        for head in range(start, start + HEADS // 2):
            scores = dot(masked(queries, own[head]), key_rows, 1, 1)
            weights.append(jnp.exp2(scores).astype(bf16))
            opposite = own[(head + HEADS // 2) % HEADS]
            ones = jnp.where(opposite, jnp.ones_like(values), jnp.zeros_like(values))
            rights.append(jnp.where(own[head], values, ones))
        results.append(dot(jnp.concatenate(weights, axis=1), jnp.concatenate(rights, axis=0)))
    low, high = results
    sums = jnp.concatenate([low[:, :half], high[:, half:]], axis=1)
    inverse = 1.0 / jnp.concatenate([low[:, half:], high[:, :half]], axis=1)
    return sums * inverse, inverse


def attend_backward(
    queries, key_rows, values, attended, inverse, grad_attended, kept_weights=None
):
    width = queries.shape[1]
    depth = width // HEADS
    own, after = head_masks(width)
    scaled = (grad_attended * inverse).astype(bf16)
    product = scaled.astype(f32) * attended
    high = product.astype(bf16)
    low = (product - high.astype(f32)).astype(bf16)
    groups = lax.broadcasted_iota(jnp.int32, (width, width), 0) // depth
    same_head = groups == lax.broadcasted_iota(jnp.int32, (width, width), 1) // depth
    group_ones = jnp.where(same_head, 1.0, 0.0).astype(bf16)
    column_sum = pltpu.roll(dot(high, group_ones) + dot(low, group_ones), depth, 1)
    column_high = column_sum.astype(bf16)
    column_low = (column_sum - column_high.astype(f32)).astype(bf16)
    lane = lax.broadcasted_iota(jnp.int32, (BALL, width), 1) % depth
    carried = jnp.where(lane == 0, column_high, masked(column_low, lane == 1))
    grad_queries = jnp.zeros((BALL, width), f32)
    grad_keys = jnp.zeros((BALL, width), f32)
    grad_values = jnp.zeros((BALL, width), f32)
    for start in range(0, HEADS, JOINED):
        weight_parts, score_parts, scaled_parts, query_parts, key_parts = [], [], [], [], []
        for head in range(start, start + JOINED):
            own_keys = masked(key_rows, own[head])
            left = jnp.where(own[head], scaled, masked(carried, after[head]))
            right = jnp.where(after[head], -jnp.ones_like(values), values)
            if kept_weights is None:
                weights = key_weights(own_keys, queries)
            else:
                weights = kept_weights[head * BALL : (head + 1) * BALL, :].astype(f32)
            score_parts.append((weights * dot(right, left, 1, 1)).astype(bf16))
            weight_parts.append(weights.astype(bf16))
            scaled_parts.append(masked(scaled, own[head]))
            query_parts.append(masked(queries, own[head]))
            key_parts.append(own_keys)
        grad_values += dot(
            jnp.concatenate(weight_parts, axis=1), jnp.concatenate(scaled_parts, axis=0)
        )
        grad_keys += dot(
            jnp.concatenate(score_parts, axis=1), jnp.concatenate(query_parts, axis=0)
        )
        grad_queries += dot(
            jnp.concatenate(score_parts, axis=0), jnp.concatenate(key_parts, axis=0), 0, 0
        )
    return grad_queries, grad_keys * (1.0 / LOG2E), grad_values


def ball_slices(rows):
    return [slice(start, start + BALL) for start in range(0, rows, BALL)]


def block_backward(
    kept, rounded, attended, inverse, grad_rows, inward, outward, weights_ref=None
):
    widened, row_scale, normed, query_unit, query_scale, key_unit, key_scale = kept
    width = widened.shape[1]
    grad_attended = dot(grad_rows, outward, 1, 1)
    parts = []
    for place, ball in enumerate(ball_slices(widened.shape[0])):
        kept_weights = None
        if weights_ref is not None:
            kept_weights = weights_ref[0, place * HEADS * BALL : (place + 1) * HEADS * BALL, :]
        parts.append(
            attend_backward(
                *(array[ball] for array in rounded),
                attended[ball].astype(f32),
                inverse[ball],
                grad_attended[ball],
                kept_weights,
            )
        )
    grad_queries, grad_keys, grad_values = (jnp.concatenate(p, axis=0) for p in zip(*parts))
    grad_queries = grad_queries * (width // HEADS) ** (-0.5)
    grad_qraw = query_scale * (
        grad_queries - query_unit * jnp.mean(grad_queries * query_unit, axis=-1, keepdims=True)
    )
    grad_kraw = key_scale * (
        grad_keys - key_unit * jnp.mean(grad_keys * key_unit, axis=-1, keepdims=True)
    )
    grad_mixture = jnp.concatenate([grad_qraw, grad_kraw, grad_values], axis=1).astype(bf16)
    grad_outward = dot(attended.astype(bf16), grad_rows, 0, 0)
    grad_inward = dot(normed, grad_mixture, 0, 0)
    grad_normed = dot(grad_mixture, inward, 1, 1)
    unit_rows = widened * row_scale
    grad_input = grad_rows.astype(f32) + row_scale * (
        grad_normed - unit_rows * jnp.mean(grad_normed * unit_rows, axis=-1, keepdims=True)
    )
    return grad_input.astype(bf16), grad_inward, grad_outward


def pack(slot_row, rows):
    return dot(one_hot_rows(slot_row, SLOTS), rows).astype(bf16)


def put_packets(packed, packet_refs):
    kinds, width = packet_refs[0].shape[2], packet_refs[0].shape[4]
    for hop in range(REACH):
        for member in range(GROUP):
            start = (hop * GROUP + member) * CAP
            for kind in range(kinds):
                part = packed[start : start + CAP, kind * width : (kind + 1) * width]
                packet_refs[hop][member, 0, kind] = part


def flat(refs):
    parts = [(ref, 0) for ref in refs[:REACH]]
    parts += [(ref, hop) for ref in refs[REACH:] for hop in range(REACH)]
    kinds = refs[0].shape[2]
    return [jnp.concatenate([ref[hop, 0, k] for ref, hop in parts], axis=0) for k in range(kinds)]


def add_up(total_ref, term):
    first = pl.program_id(0) == 0

    @pl.when(first)
    def _():
        total_ref[...] = term

    @pl.when(jnp.logical_not(first))
    def _():
        total_ref[...] += term


def join_grads(total_ref, inward_grad, outward_grad):
    width = outward_grad.shape[0]
    for third in range(3):
        part = inward_grad[:, third * width : (third + 1) * width]
        total_ref[third * width : (third + 1) * width, :] = part.astype(bf16)
    total_ref[3 * width : 4 * width, :] = outward_grad.astype(bf16)


def add_grads(total_ref, sum_refs, grads, other_ref=None):
    for sum_ref, grad in zip(sum_refs, grads):
        add_up(sum_ref, grad)

    @pl.when(pl.program_id(0) == pl.num_programs(0) - 1)
    def _():
        join_grads(total_ref, *(ref[...] for ref in sum_refs))
        if other_ref is not None:
            total_ref[other_ref.shape[0] :, :] = other_ref[...]


def sample_row(meta_ref, kind):
    samples = meta_ref.shape[0] // 2
    return meta_ref[pl.ds(kind * samples + pl.program_id(0), 1), :]


def attend_balls(rounded):
    rows = rounded[0].shape[0]
    parts = [attend(*(array[ball] for array in rounded)) for ball in ball_slices(rows)]
    attended, inverse = (jnp.concatenate(part, axis=0) for part in zip(*parts))
    return attended, inverse


def forward_kernel(nodes_ref, cot_ref, inward_ref, outward_ref, meta_ref, *refs):
    after_ref, attended_ref, inverse_ref, rounded_ref, scales_ref, *packet_refs = refs
    width = nodes_ref.shape[2]
    widened, _, normed = norm(nodes_ref[0])
    (_, query_scale, _, key_scale), rounded = project(normed, inward_ref[...])
    attended, inverse = attend_balls(rounded)
    attended = attended.astype(bf16)
    attended_ref[0] = attended
    inverse_ref[0] = inverse
    for place, array in enumerate(rounded):
        rounded_ref[0, :, place * width : (place + 1) * width] = array
    lane = lax.broadcasted_iota(jnp.int32, scales_ref.shape[1:], 1)
    scales_ref[0] = jnp.where(lane == 0, query_scale, key_scale)
    result = (widened + dot(attended, outward_ref[...])).astype(bf16)
    after_ref[0] = result
    both = jnp.concatenate([result, cot_ref[0]], axis=1)
    put_packets(pack(sample_row(meta_ref, 0), both), packet_refs)


def each_ball(rows, body):
    @pl.loop(0, rows // BALL)
    def _(ball):
        body(ball, pl.ds(pl.multiple_of(ball * BALL, BALL), BALL))


def weights_kernel(rounded_ref, weights_ref):
    width = rounded_ref.shape[2] // 3
    own, _ = head_masks(width)

    def body(ball, here):
        queries = rounded_ref[0, here, :width]
        key_rows = rounded_ref[0, here, width : 2 * width]
        for head in range(HEADS):
            start = pl.multiple_of((ball * HEADS + head) * BALL, BALL)
            weights = key_weights(masked(key_rows, own[head]), queries)
            weights_ref[0, pl.ds(start, BALL), :] = weights.astype(bf16)

    each_ball(rounded_ref.shape[1], body)


def near_kernel(meta_ref, *refs):
    *home_refs, near_ref, picks_ref = refs
    picks_ref[...] = spread_column(sample_row(meta_ref, 1))
    rows, width = home_refs[0].shape[1:]

    def body(ball, here):
        hits = one_hot_picks(picks_ref[here, :], 0, rows)
        for kind, home_ref in enumerate(home_refs):
            near = dot(hits, home_ref[0]).astype(bf16)
            near_ref[0, here, kind * width : (kind + 1) * width] = near

    each_ball(rows, body)


def add_far(meta_ref, near_ref, landed_refs):
    hits = one_hot_picks(spread_column(sample_row(meta_ref, 1)), near_ref.shape[1], SLOTS)
    rows = []
    for kind, landed in enumerate(flat(landed_refs)):
        width = landed.shape[1]
        near = near_ref[0, :, kind * width : (kind + 1) * width]
        rows.append((near.astype(f32) + dot(hits, landed)).astype(bf16))
    return rows


def second_kernel(meta_ref, near_ref, inward_ref, outward_ref, *refs):
    arrived_refs, refs = refs[:LANDED], refs[LANDED:]
    grad_ref, total_ref, *packet_refs = refs[: 2 + REACH]
    *sum_refs, rotated_ref, rotated_cot_ref = refs[2 + REACH :]

    @pl.when(pl.program_id(0) >= 0)
    def _():
        rotated_ref[...], rotated_cot_ref[...] = add_far(meta_ref, near_ref, arrived_refs)

    kept = norm(rotated_ref[...])
    units, rounded = project(kept[2], inward_ref[...])
    attended, inverse = attend_balls(rounded)
    grad_input, *grads = block_backward(
        kept + units,
        rounded,
        attended,
        inverse,
        rotated_cot_ref[...],
        inward_ref[...],
        outward_ref[...],
    )
    grad_ref[0] = grad_input
    add_grads(total_ref, sum_refs, grads)
    put_packets(pack(sample_row(meta_ref, 0), grad_input), packet_refs)


def first_kernel(
    meta_ref,
    nodes_ref,
    near_ref,
    attended_ref,
    inverse_ref,
    rounded_ref,
    scales_ref,
    weights_ref,
    inward_ref,
    outward_ref,
    *refs,
):
    returned_refs, refs = refs[:LANDED], refs[LANDED:]
    other_ref, grad_ref, total_ref, *sum_refs = refs
    (grad_after,) = add_far(meta_ref, near_ref, returned_refs)
    width = nodes_ref.shape[2]
    rounded = [rounded_ref[0, :, place * width : (place + 1) * width] for place in range(3)]
    query_unit = rounded[0].astype(f32) * (1.0 / score_factor(width))
    key_unit = rounded[1].astype(f32)
    units = (query_unit, scales_ref[0, :, 0:1], key_unit, scales_ref[0, :, 1:2])
    grad_input, *grads = block_backward(
        norm(nodes_ref[0]) + units,
        rounded,
        attended_ref[0],
        inverse_ref[0],
        grad_after,
        inward_ref[...],
        outward_ref[...],
        weights_ref,
    )
    grad_ref[0] = grad_input
    add_grads(total_ref, sum_refs, grads, other_ref)


def split_kernel(whole_ref, *refs):
    width = refs[1].shape[0]
    for place, (inward_ref, outward_ref) in enumerate((refs[:2], refs[2:])):
        start = place * 4 * width
        for third in range(3):
            part = whole_ref[start + third * width : start + (third + 1) * width, :]
            inward_ref[:, third * width : (third + 1) * width] = part.astype(f32)
        outward_ref[...] = whole_ref[start + 3 * width : start + 4 * width, :].astype(f32)


def full_spec(shape):
    return pl.BlockSpec(shape, lambda i: (0,) * len(shape))


def call(kernel, name, micros, in_specs, operands, outs, out_specs=None, steps=1, **options):
    specs = [
        full_spec(operand.shape) if spec is None else spec
        for spec, operand in zip(in_specs or [None] * len(operands), operands)
    ]
    return pl.pallas_call(
        kernel,
        name=name,
        grid=(steps,),
        in_specs=specs,
        out_specs=out_specs or [full_spec(out.shape) for out in outs],
        out_shape=outs,
        compiler_params=pltpu.CompilerParams(vmem_limit_bytes=VMEM_LIMIT),
        cost_estimate=pl.CostEstimate(
            flops=int(micros * 1.15e9), bytes_accessed=2**20, transcendentals=0
        ),
        **options,
    )(*operands)


def rotate(value, axis, steps):
    count = lax.axis_size(axis)
    pairs = [(source, (source + steps) % count) for source in range(count)]
    return lax.ppermute(value, axis, pairs)


def hop_stage(packets):
    moved = dict(zip(HOPS, packets))
    for hop in sorted((hop for hop in HOPS if hop != 0), key=lambda hop: (-abs(hop), hop)):
        moved[hop] = rotate(moved[hop], "pts", hop)
    return [moved[hop] for hop in HOPS]


def restack(moved):
    return [
        jnp.concatenate([packet[member : member + 1] for packet in moved], axis=0)
        for member in range(1, GROUP)
    ]


def member_stage(moved, stacked):
    return moved + [rotate(s, "grp", 1 + place) for place, s in enumerate(stacked)]


def exchange(packets):
    moved = hop_stage(packets)
    return member_stage(moved, restack(moved))


def reduce_all(terms, factor):
    count = lax.axis_size(AXES)
    pieces = terms.reshape(count, -1, terms.shape[1])
    mine = lax.all_to_all(pieces, AXES, 0, 0, tiled=True)
    total = (jnp.sum(mine.astype(f32), axis=0) * factor).astype(bf16)
    spread = jnp.broadcast_to(total[None], pieces.shape)
    return lax.all_to_all(spread, AXES, 0, 0, tiled=True).reshape(terms.shape)


def per_device(
    nodes,
    cotangent,
    first_inward,
    first_outward,
    second_inward,
    second_outward,
    rotated_source,
    rotated_index,
):
    samples, rows, width = nodes.shape
    shards = lax.axis_size(AXES)
    own = lax.axis_index(AXES).astype(jnp.int32).reshape(1)
    shape = jax.ShapeDtypeStruct
    smem = pl.BlockSpec(memory_space=pltpu.SMEM)
    rows_shape = shape(nodes.shape, bf16)
    meta_shape = shape((2 * samples, rows), jnp.int32)
    joined_shape = shape((4 * width, width), bf16)
    both_shape = shape((8 * width, width), bf16)
    sums = [pltpu.VMEM((width, 3 * width), f32), pltpu.VMEM((width, width), f32)]
    first_weights = (first_inward, first_outward)
    second_weights = (second_inward, second_outward)

    def by_sample(*dims):
        return pl.BlockSpec((1, *dims), lambda s: (s, *(0 for _ in dims)))

    def packets(kinds):
        return [shape((GROUP, samples, kinds, CAP, width), bf16)] * REACH

    def packets_by_sample(kinds):
        return [pl.BlockSpec((GROUP, 1, kinds, CAP, width), lambda s: (0, s, 0, 0, 0))] * REACH

    def landed_by_sample(kinds):
        one = pl.BlockSpec((1, 1, kinds, CAP, width), lambda s: (0, s, 0, 0, 0))
        hops = pl.BlockSpec((REACH, 1, kinds, CAP, width), lambda s: (0, s, 0, 0, 0))
        return [one] * REACH + [hops] * (GROUP - 1)

    rows_spec = by_sample(rows, width)
    (send_meta,) = call(
        functools.partial(send_kernel, shards=shards),
        "send_places",
        2,
        [smem, None],
        (own, rotated_index),
        [meta_shape],
    )
    after_first, attended, inverse, rounded, scales, *out_packets = call(
        forward_kernel,
        "forward",
        9,
        [rows_spec, rows_spec, None, None, None],
        (nodes, cotangent, *first_weights, send_meta),
        [
            rows_shape,
            rows_shape,
            shape(nodes.shape, f32),
            shape((samples, rows, 3 * width), bf16),
            shape((samples, rows, 128), f32),
        ]
        + packets(2),
        [rows_spec] * 3
        + [by_sample(rows, 3 * width), by_sample(rows, 128)]
        + packets_by_sample(2),
        samples,
    )
    arrived = exchange(out_packets)
    (receive_meta,) = call(
        functools.partial(receive_kernel, shards=shards),
        "receive_places",
        2,
        [smem, None],
        (own, rotated_source),
        [meta_shape],
    )
    (near,) = call(
        near_kernel,
        "near_out",
        3,
        [None, rows_spec, rows_spec],
        (receive_meta, after_first, cotangent),
        [shape((samples, rows, 2 * width), bf16)],
        [by_sample(rows, 2 * width)],
        samples,
        scratch_shapes=[pltpu.VMEM((rows, 128), f32)],
    )
    weights_spec = by_sample(rows * HEADS, BALL)
    (weights,) = call(
        weights_kernel,
        "weights",
        6,
        [by_sample(rows, 3 * width)],
        (rounded,),
        [shape((samples, rows * HEADS, BALL), bf16)],
        [weights_spec],
        samples,
    )
    near, weights = lax.optimization_barrier((near, weights))
    rotated_grad, second_joined, *back_packets = call(
        second_kernel,
        "second",
        26,
        [None, by_sample(rows, 2 * width), None, None] + landed_by_sample(2),
        (receive_meta, near, *second_weights, *arrived),
        [rows_shape, joined_shape] + packets(1),
        [rows_spec, full_spec(joined_shape.shape)] + packets_by_sample(1),
        samples,
        scratch_shapes=sums + [pltpu.VMEM((rows, width), bf16)] * 2,
    )
    returned = exchange(back_packets)
    (grad_near,) = call(
        near_kernel,
        "near_back",
        2,
        [None, rows_spec],
        (send_meta, rotated_grad),
        [rows_shape],
        [rows_spec],
        samples,
        scratch_shapes=[pltpu.VMEM((rows, 128), f32)],
    )
    input_grad, joined = call(
        first_kernel,
        "first",
        16,
        [None]
        + [rows_spec] * 4
        + [by_sample(rows, 3 * width), by_sample(rows, 128), weights_spec, None, None]
        + landed_by_sample(1)
        + [None],
        (
            send_meta,
            nodes,
            grad_near,
            attended,
            inverse,
            rounded,
            scales,
            weights,
            *first_weights,
            *returned,
            second_joined,
        ),
        [rows_shape, both_shape],
        [rows_spec, full_spec(both_shape.shape)],
        samples,
        scratch_shapes=sums,
    )
    factor = 1.0 / math.sqrt(samples * rows * shards)
    grad_shapes = [shape((width, 3 * width), f32), shape((width, width), f32)]
    grads = call(split_kernel, "split", 2, None, (reduce_all(joined, factor),), grad_shapes * 2)
    return (input_grad, *grads)


def solution(mesh):
    in_specs = (
        P(None, AXES, None),
        P(None, AXES, None),
        P(),
        P(),
        P(),
        P(),
        P(None, AXES),
        P(None, AXES),
    )
    out_specs = (P(None, AXES, None), P(), P(), P(), P())
    return jax.shard_map(
        per_device, mesh=mesh, in_specs=in_specs, out_specs=out_specs, check_vma=False
    )
```
